256 devices in a mesh: dp: 2 (over core), seq: 32 (over y, z), tensor: 4 (over x).
Axes of the slice: x: 4, y: 4, z: 8, core: 2. Of those that a mesh axis runs over, the one named last changes fastest.
Arguments:
- q_raw: bfloat16 [2, 8192, 3072], P('dp', 'seq', 'tensor'), may hold values from -240 to 240
- k_raw: bfloat16 [2, 8192, 3072], P('dp', 'seq', 'tensor'), may hold values from -240 to 240
- v_raw: bfloat16 [2, 8192, 3072], P('dp', 'seq', 'tensor'), may hold values from -6 to 6
- out_grad: bfloat16 [2, 8192, 3072], P('dp', 'seq', 'tensor'), may hold values from -54 to 54
- gain_q: float32 [128], replicated, may hold values from 0.5 to 6
- gain_k: float32 [128], replicated, may hold values from 0.5 to 6
- keep_list: int32 [2, 4096], P('dp'), may hold values from 0 to 8191, as said below
Outputs:
- q_grad: bfloat16 [2, 8192, 3072], P('dp', 'seq', 'tensor')
- k_grad: bfloat16 [2, 8192, 3072], P('dp', 'seq', 'tensor')
- v_grad: bfloat16 [2, 8192, 3072], P('dp', 'seq', 'tensor')
- gain_q_grad: float32 [128], replicated
- gain_k_grad: float32 [128], replicated
The draws below stay inside these ranges and needn't reach their ends.
Inputs may be any that keep to these rules, and one draw needn't show every extreme that they name: `keep_list`: for each clip the list names 4096 different tokens of that clip. For every i and j, positions j * 128 to (j + 1) * 128 - 1 hold at most 8 of the tokens i * 256 to (i + 1) * 256 - 1, and for every j some i gives exactly 8.
All inputs are finite; a program needn't handle non-finite values.
Results may differ from the reference program's by a relative error of at most 0.008.
The reference program's roundings to bfloat16 on the way count: a program that leaves them out, or rounds other values in their place, can miss the bound.
Values may be sent and summed in bfloat16 or wider, within the bound.
A program may use at most 128 MiB of HBM per device.

```python
import math
import jax
import jax.numpy as jnp
from jax import lax

HD = 128
HEADS = 24
BLOCK = 256
KEEP_DEV = 128
TOKENS = 8192
KEPT = 4096
CLIPS = 2


def query_field(key, row_high, col_high):
    key_gauss = jax.random.fold_in(key, 0)
    key_row = jax.random.fold_in(key, 2)
    key_col = jax.random.fold_in(key, 3)
    full_shape = (CLIPS, TOKENS, HEADS, HD)
    gauss = jnp.clip(jax.random.normal(key_gauss, full_shape, jnp.float32), -6.0, 6.0)
    base = gauss
    row_scale = jnp.exp(jax.random.uniform(key_row, (CLIPS, TOKENS, HEADS, 1), jnp.float32, 0.0, math.log(row_high)))
    col_scale = jnp.exp(jax.random.uniform(key_col, (1, 1, HEADS, HD), jnp.float32, 0.0, math.log(col_high)))
    return (base * row_scale * col_scale).reshape(CLIPS, TOKENS, HEADS * HD)


def draw_q_raw(key, part):
    field = query_field(key, 10.0, 4.0)
    return field.astype(jnp.bfloat16)


def draw_k_raw(key, part):
    own_key = jax.random.fold_in(key, 7)
    field = query_field(own_key, 10.0, 4.0)
    return field.astype(jnp.bfloat16)


def draw_out_grad(key, part):
    key = jax.random.fold_in(key, 13)
    full_shape = (CLIPS, TOKENS, HEADS, HD)
    head_factor = 1.0 + 2.0 * jnp.arange(HEADS, dtype=jnp.float32) / max(HEADS - 1, 1)
    clip_factor = 1.0 + 2.0 * jnp.arange(CLIPS, dtype=jnp.float32) / max(CLIPS - 1, 1)
    factor = clip_factor[:, None, None, None] * head_factor[None, None, :, None]
    base = jnp.clip(jax.random.normal(key, full_shape, jnp.float32), -6.0, 6.0)
    return (base * factor).reshape(CLIPS, TOKENS, HEADS * HD).astype(jnp.bfloat16)


def draw_gain_q(key, part):
    key = jax.random.fold_in(key, 17)
    return jnp.exp(jax.random.uniform(key, (HD,), jnp.float32, math.log(0.5), math.log(2.0)))


def draw_gain_k(key, part):
    key = jax.random.fold_in(key, 19)
    return jnp.exp(jax.random.uniform(key, (HD,), jnp.float32, math.log(0.5), math.log(2.0)))


def draw_keep_list(key, part):
    key = jax.random.fold_in(key, 23)
    groups = KEPT // KEEP_DEV
    half_cap = KEEP_DEV // groups

    def one_clip(clip_key):
        key_order, key_shift, key_token, key_shuffle = jax.random.split(clip_key, 4)
        orders = jax.vmap(lambda sub_key: jax.random.permutation(sub_key, groups))(jax.random.split(key_order, groups))
        shifts = jax.random.randint(key_shift, (groups, groups // 2), 0, half_cap + 1)
        shifts = shifts.at[:, 0].set(half_cap)
        gainers = orders[:, 0::2]
        losers = orders[:, 1::2]
        lines = jnp.arange(groups)[:, None]
        counts = jnp.full((groups, groups), half_cap, jnp.int32)
        counts = counts.at[lines, gainers].add(shifts).at[lines, losers].add(-shifts)
        before = jnp.cumsum(counts, axis=0) - counts
        col_end = jnp.cumsum(counts, axis=1)
        col_start = col_end - counts
        entries = jnp.arange(KEEP_DEV)
        sender = jnp.sum((col_end[:, None, :] <= entries[None, :, None]).astype(jnp.int32), axis=-1)
        slot_index = entries[None, :] - jnp.take_along_axis(col_start, sender, axis=1)
        offset = jnp.take_along_axis(before, sender, axis=1) + slot_index
        token_order = jax.vmap(lambda sub_key: jax.random.permutation(sub_key, BLOCK))(jax.random.split(key_token, groups))
        tokens = sender * BLOCK + token_order[sender, offset]
        shuffle = jax.vmap(lambda sub_key: jax.random.permutation(sub_key, KEEP_DEV))(jax.random.split(key_shuffle, groups))
        tokens = jnp.take_along_axis(tokens, shuffle, axis=1)
        return tokens.reshape(-1).astype(jnp.int32)
    return jax.vmap(one_clip)(jax.random.split(key, CLIPS))


def shard_levels(key, extent, pieces, low, high):
    factor_of, own = 1.0, jax.random.fold_in(key, 6)
    for dim, blocks in pieces:
        draws = jnp.exp(jax.random.uniform(jax.random.fold_in(own, dim), (blocks,), jnp.float32, low / len(pieces), high / len(pieces)))
        factor_of = factor_of * jnp.repeat(draws, extent[dim] // blocks).reshape([-1 if axis == dim else 1 for axis in range(len(extent))])
    return factor_of


def gaussian(stream_key, extent, spread, most, pieces=(), kind=jnp.bfloat16):
    loudness = shard_levels(stream_key, extent, pieces, -0.22, 0.18) if pieces else 1.0
    values = jax.random.normal(stream_key, extent, jnp.float32) * spread * loudness
    return jnp.minimum(jnp.maximum(values, -most), most).astype(kind)


def setup_inputs(seed: int = 0) -> dict:
    streams_of = jax.random.split(jax.random.key(seed), 8)
    return {
        "q_raw": draw_q_raw(jax.random.fold_in(streams_of[7], 71), 0),
        "k_raw": draw_k_raw(jax.random.fold_in(streams_of[7], 71), 0),
        "v_raw": gaussian(streams_of[2], (CLIPS, TOKENS, HEADS * HD), 1.0, 6.0, ((0, 2), (1, 32), (2, 4))),
        "out_grad": draw_out_grad(jax.random.fold_in(streams_of[7], 71), 0),
        "gain_q": draw_gain_q(jax.random.fold_in(streams_of[7], 71), 0),
        "gain_k": draw_gain_k(jax.random.fold_in(streams_of[7], 71), 0),
        "keep_list": draw_keep_list(jax.random.fold_in(streams_of[7], 71), 0),
    }


EPSILON = 1e-06

def normalize(kept_rows, gain_vec, head_count):
    raw_rows = kept_rows.astype(jnp.float32).reshape(kept_rows.shape[0], head_count, -1)
    inverse = lax.rsqrt(lax.optimization_barrier(jnp.mean(raw_rows * raw_rows, axis=-1)) + EPSILON)
    normed = (raw_rows * inverse[..., None] * gain_vec).astype(jnp.bfloat16)
    return (raw_rows, inverse, normed)

def norm_grads(raw_rows, inverse, gain_vec, upstream):
    scaled = upstream * gain_vec
    inner = lax.optimization_barrier(jnp.mean(scaled * raw_rows, axis=-1))
    row_grads = inverse[..., None] * scaled - raw_rows * (inverse * inverse * inverse * inner)[..., None]
    gain_term = lax.optimization_barrier(jnp.sum(upstream * raw_rows * inverse[..., None], axis=(0, 1)))
    return (row_grads, gain_term)

def one_head(inputs):
    queries, key_rows, value_rows, grad_rows = inputs
    scaling = 1.0 / math.sqrt(HD)
    scores = jnp.dot(queries, key_rows.T, preferred_element_type=jnp.float32) * scaling
    highest = lax.optimization_barrier(jnp.max(scores, axis=1))
    log_norm = highest + jnp.log(lax.optimization_barrier(jnp.sum(jnp.exp(scores - highest[:, None]), axis=1)))
    probs = jnp.exp(scores - log_norm[:, None])
    grad_dots = jnp.dot(grad_rows, value_rows.T, preferred_element_type=jnp.float32)
    delta_rows = lax.optimization_barrier(jnp.sum(probs * grad_dots, axis=1))
    dscore = (probs * (grad_dots - delta_rows[:, None])).astype(jnp.bfloat16)
    probs_low = probs.astype(jnp.bfloat16)
    query_grad = jnp.dot(dscore, key_rows, preferred_element_type=jnp.float32) * scaling
    key_grad = jnp.dot(dscore.T, queries, preferred_element_type=jnp.float32) * scaling
    value_grad = jnp.dot(probs_low.T, grad_rows, preferred_element_type=jnp.float32)
    return (query_grad, key_grad, value_grad)

def heads_first(array):
    return jnp.transpose(array, (1, 0, 2))

def reference(q_raw, k_raw, v_raw, out_grad, gain_q, gain_k, keep_list):
    grads_q, grads_k, grads_v = ([], [], [])
    total_q = jnp.zeros((HD,), jnp.float32)
    total_k = jnp.zeros((HD,), jnp.float32)
    for clip_index in range(CLIPS):
        kept_index = keep_list[clip_index].astype(jnp.int32)
        raw_q, inv_q, norm_q = normalize(q_raw[clip_index][kept_index], gain_q, HEADS)
        raw_k, inv_k, norm_k = normalize(k_raw[clip_index][kept_index], gain_k, HEADS)
        kept_v = v_raw[clip_index][kept_index].reshape(KEPT, HEADS, HD)
        kept_grad = out_grad[clip_index][kept_index].reshape(KEPT, HEADS, HD)
        query_grad, key_grad, value_grad = lax.map(one_head, (heads_first(norm_q), heads_first(norm_k), heads_first(kept_v), heads_first(kept_grad)))
        rows_q, term_q = norm_grads(raw_q, inv_q, gain_q, heads_first(query_grad))
        rows_k, term_k = norm_grads(raw_k, inv_k, gain_k, heads_first(key_grad))
        total_q = total_q + term_q
        total_k = total_k + term_k
        empty = jnp.zeros((TOKENS, HEADS * HD), jnp.bfloat16)
        grads_q.append(empty.at[kept_index].set(rows_q.reshape(KEPT, HEADS * HD).astype(jnp.bfloat16)))
        grads_k.append(empty.at[kept_index].set(rows_k.reshape(KEPT, HEADS * HD).astype(jnp.bfloat16)))
        grads_v.append(empty.at[kept_index].set(heads_first(value_grad).reshape(KEPT, HEADS * HD).astype(jnp.bfloat16)))
    return (jnp.stack(grads_q), jnp.stack(grads_k), jnp.stack(grads_v), total_q, total_k)
```

```python
import math

import jax
import jax.numpy as jnp
from jax import lax
from jax.experimental import pallas as pl
from jax.experimental.pallas import tpu as pltpu
from jax.sharding import PartitionSpec as P

MESH = pl.DeviceIdType.MESH
HD = 128
EPSILON = 1e-06
SEQ = 32
SPAN = 256
SHARE = 128
SLOTS = 8
HEAD_PART = 6
UNITS = 6
ROWS = UNITS * SHARE
CHUNK = UNITS * SLOTS
FLAT = SEQ * CHUNK
MEMBERS = 16
KEPT = SEQ * SHARE
TILE = 256
TILES = ROWS // TILE
SCALING = 1.0 / math.sqrt(HD)
LOG2E = 1.4426950408889634
VMEM_LIMIT = 56 * 1024 * 1024

NT = (((1,), (1,)), ((), ()))

PATHS = (
    (0, 0, 0, 768, 0, (1, 2), None, None),
    (0, 1, 0, 768, 0, (1,), 1, 2),
    (1, None, 0, 768, 0, (0, 2), None, None),
    (2, 0, 0, 768, 0, (1,), 1, 0),
    (2, 1, 0, 256, 0, (1,), 1, 0),
    (2, 1, 256, 512, 1, (3, 4, 5), None, None),
    (3, None, 0, 768, 1, (2, 4), 2, 5),
    (4, None, 0, 768, 1, (5, 3), 5, 2),
    (5, 0, 0, 512, 1, (2, 3, 4), None, None),
    (5, 0, 512, 256, 2, (6,), 6, 7),
    (5, 1, 0, 768, 2, (6,), 6, 7),
    (6, None, 0, 768, 2, (5, 7), None, None),
    (7, 0, 0, 768, 2, (6, 5), None, None),
    (7, 1, 0, 768, 2, (6,), 6, 5),
)


def place(group, member):
    chip, core = member // 2, member % 2
    dz, dy = chip // 2, ((chip + 1) // 2) % 2
    y = 2 * (group // 2) + dy
    z = 4 * (group % 2) + dz
    return core, y * 8 + z


def my_place(dp, s):
    y, z = s // 8, s % 8
    dy, dz = y % 2, z % 4
    chip = 2 * dz + (dy + dz) % 2
    group = 2 * (y // 2) + z // 4
    return group, chip


def among(value, options):
    hit = value == options[0]
    for option in options[1:]:
        hit = hit | (value == option)
    return hit


def one_hot(hit):
    return jnp.where(hit, 1.0, 0.0).astype(jnp.bfloat16)


def inverse_norm(x):
    return lax.rsqrt(jnp.mean(x * x, axis=-1, keepdims=True) + EPSILON)


def norm_grads(raw, gain, upstream):
    raw = raw.astype(jnp.float32)
    inverse = inverse_norm(raw)
    scaled = upstream * gain
    inner = jnp.mean(scaled * raw, axis=-1, keepdims=True)
    grads = inverse * scaled - raw * (inverse * inverse * inverse * inner)
    terms = upstream * raw * inverse
    return grads, jnp.sum(terms.reshape(-1, 8, HD), axis=0)


def lane_fold(x, fold):
    parts = [x[:, i * 128 : (i + 1) * 128] for i in range(x.shape[1] // 128)]
    total = parts[0]
    for part in parts[1:]:
        total = fold(total, part)
    return total


def core_kernel(
    slot_ref,
    row_ref,
    enc_ref,
    k_ref,
    v_ref,
    q_ref,
    g_ref,
    gain_q_ref,
    gain_k_ref,
    home_ref,
    back_ref,
    total_ref,
    slots,
    arrived,
    other,
    codes,
    pick,
    full,
    raw,
    scores_ref,
    dots_ref,
    q_grad,
    q_slots,
    kv_slots,
    stats,
    terms,
    parts,
    partial,
    cross,
    enc_sem,
    route_send,
    route_recv,
    pair_send,
    pair_recv,
    path_send,
    path_recv,
    pass_send,
    hand_send,
    hand_recv,
    stat_send,
    stat_recv,
    home_send,
    home_recv,
    part_sem,
    cross_send,
    cross_recv,
):
    dp, s, x = lax.axis_index("dp"), lax.axis_index("seq"), lax.axis_index("tensor")
    group, chip = my_place(dp, s)
    clip = group // 2
    me = 2 * chip + dp
    seat = (group % 2) * MEMBERS + me
    sibling = (1 - dp, s, x)
    corner = dp * 4 + x
    same = clip == dp

    def remote(src, dst, send_sem, recv_sem, device):
        return pltpu.make_async_remote_copy(
            src_ref=src, dst_ref=dst, send_sem=send_sem, recv_sem=recv_sem, device_id=device, device_id_type=MESH
        )


    barrier = pltpu.get_barrier_semaphore()

    def greet(i, _):
        @pl.when((i // SEQ != dp) | (i % SEQ != s))
        def _():
            pl.semaphore_signal(barrier, inc=1, device_id=(i // SEQ, i % SEQ, x), device_id_type=MESH)

        return 0

    lax.fori_loop(0, 2 * SEQ, greet, 0)

    def greet_corner(i, _):
        @pl.when(i % 4 != x)
        def _():
            pl.semaphore_signal(barrier, inc=1, device_id=(i // 4, s, i % 4), device_id_type=MESH)

        return 0

    lax.fori_loop(0, 8, greet_corner, 0)


    step = 512
    iota = lax.broadcasted_iota(jnp.int32, (SPAN, step), 0)
    take = jnp.zeros((SPAN, SPAN), jnp.float32)
    back = jnp.zeros((SPAN, SPAN), jnp.float32)
    for c in range(KEPT // step):
        cols = slice(c * step, (c + 1) * step)
        a = one_hot(iota == slot_ref[:, cols])
        b = one_hot(iota == row_ref[:, cols])
        take += lax.dot_general(a, b, NT, preferred_element_type=jnp.float32)
        back += lax.dot_general(b, a, NT, preferred_element_type=jnp.float32)
    take = take.astype(jnp.bfloat16)
    back_ref[...] = back.astype(jnp.bfloat16)

    def to_slots(i, ref):
        rows = jnp.dot(take, ref[...], preferred_element_type=jnp.float32).astype(jnp.bfloat16)
        for h in range(HEAD_PART):
            slots[i, h * SPAN : (h + 1) * SPAN, :] = rows[:, h * HD : (h + 1) * HD]

    def target(i):
        core, seq = place(2 * dp + i // MEMBERS, i % MEMBERS)
        return core, seq, (core == dp) & (seq == s)

    def chunk(ref, a, i):
        return ref.at[a, pl.ds(pl.multiple_of(i * CHUNK, 16), CHUNK), :]

    def route(a):
        def start(n, _):
            i = (n + s) % SEQ
            core, seq, own = target(i)

            @pl.when(jnp.logical_not(own))
            def _():
                remote(
                    chunk(slots, a, i), chunk(arrived, a, s), route_send.at[a], route_recv.at[a], (core, seq, x)
                ).start()

            @pl.when(own)
            def _():
                pltpu.make_async_copy(chunk(slots, a, i), chunk(arrived, a, s), route_recv.at[a]).start()

            return 0

        lax.fori_loop(0, SEQ, start, 0)

    to_slots(0, k_ref)
    pl.semaphore_wait(barrier, 2 * SEQ - 1 + 6)
    exchange = remote(enc_ref, other, enc_sem.at[0], enc_sem.at[1], sibling)
    exchange.start()
    route(0)
    for a, ref in ((1, v_ref), (2, q_ref), (3, g_ref)):
        to_slots(a, ref)
        route(a)


    exchange.wait()
    codes[...] = jnp.where(same, enc_ref[...], other[...])

    def unit_codes(u):
        return codes[pl.ds((UNITS * me + u) % SEQ, 1), :]

    wide_iota = lax.broadcasted_iota(jnp.int32, (SHARE, 128), 1).astype(jnp.float32)
    index = []
    for u in range(UNITS):
        code = unit_codes(u)
        code = (code >> 3) * CHUNK + u * SLOTS + (code & 7)
        index.append(code)
        wide = jnp.broadcast_to(code.astype(jnp.float32), (SHARE, 128)).T
        for c in range(FLAT // 128):
            pick[u * SHARE : (u + 1) * SHARE, c * 128 : (c + 1) * 128] = one_hot(wide == wide_iota + c * 128.0)
    index = jnp.concatenate(index, axis=1)

    own_rows = pl.ds(pl.multiple_of(me * ROWS, 256), ROWS)

    def to_dense(a):
        remote(slots.at[a], arrived.at[a], route_send.at[a], route_recv.at[a], sibling).wait_recv()
        rows = jnp.dot(pick[...], arrived[a], preferred_element_type=jnp.float32)
        if a % 2 == 0:
            raw[a // 2] = rows.astype(jnp.bfloat16)
            gain = (gain_k_ref, gain_q_ref)[a // 2][...]
            rows = rows * inverse_norm(rows) * gain
        full[a, own_rows, :] = rows.astype(jnp.bfloat16)


    def member_needs(member, head):
        return ((UNITS * member) // SEQ <= head) & (head <= (UNITS * member + UNITS - 1) // SEQ)

    def device(c):
        core, seq = place(group, 2 * c + dp)
        return (core, seq, x)

    def segment(phase, member, first, count):
        return full.at[2 * phase : 2 * phase + 2, pl.ds(pl.multiple_of(member * ROWS + first, 256), count), :]

    def lane(core):
        return True if core is None else dp == core

    def other_lane(core):
        return True if core is None else dp != core

    def reached(path):
        chips = list(path[5])
        if path[7] is not None:
            chips.append(path[7])
        return chips

    def pair(phase, member):
        rows = segment(phase, member, 0, ROWS)
        return remote(rows, rows, pair_send.at[phase], pair_recv.at[phase], sibling)

    def path_copy(phase, n, member, to, send_sem):
        _, _, first, count, *_ = PATHS[n]
        rows = segment(phase, member, first, count)
        return remote(rows, rows, send_sem, path_recv.at[phase, n], device(to))

    def hand_copy(phase, n, member):
        _, _, first, count, *_ = PATHS[n]
        rows = segment(phase, member, first, count)
        return remote(rows, rows, hand_send.at[phase, n], hand_recv.at[phase, n], sibling)

    def gather_start(phase):
        for n, (c, core, _, _, _, direct, _, _) in enumerate(PATHS):

            @pl.when((chip == c) & lane(core))
            def _():
                for i, to in enumerate(direct):
                    path_copy(phase, n, me, to, path_send.at[phase, n, i]).start()

        pair(phase, me).start()

    def gather_pass(phase):
        for n, path in enumerate(PATHS):
            c, core, _, _, head, _, via, to = path
            member = 2 * c + dp

            @pl.when(among(chip, reached(path)) & lane(core))
            def _():
                path_copy(phase, n, member, c, path_send.at[phase, n, 0]).wait_recv()
                if via is not None:

                    @pl.when(chip == via)
                    def _():
                        path_copy(phase, n, member, to, pass_send.at[phase, n]).start()

                @pl.when(member_needs(2 * chip + 1 - dp, head))
                def _():
                    hand_copy(phase, n, member).start()

    def gather_finish(phase):
        pair(phase, 2 * chip + 1 - dp).wait_recv()
        for n, path in enumerate(PATHS):
            c, core, _, _, head, *_ = path

            @pl.when(among(chip, reached(path)) & other_lane(core) & member_needs(me, head))
            def _():
                hand_copy(phase, n, 2 * c + 1 - dp).wait_recv()

    def gather_sent(phase):
        pair(phase, me).wait_send()
        for n, path in enumerate(PATHS):
            c, core, _, _, head, direct, via, to = path
            member = 2 * c + dp

            @pl.when((chip == c) & lane(core))
            def _():
                for i, chip_to in enumerate(direct):
                    path_copy(phase, n, me, chip_to, path_send.at[phase, n, i]).wait_send()

            @pl.when(among(chip, reached(path)) & lane(core))
            def _():
                if via is not None:

                    @pl.when(chip == via)
                    def _():
                        path_copy(phase, n, member, to, pass_send.at[phase, n]).wait_send()

                @pl.when(member_needs(2 * chip + 1 - dp, head))
                def _():
                    hand_copy(phase, n, member).wait_send()

    to_dense(0)
    to_dense(1)
    gather_start(0)
    to_dense(2)
    to_dense(3)
    gather_start(1)
    gather_pass(0)
    gather_finish(0)


    terms[...] = jnp.zeros_like(terms)
    chunks = [slice(i * step, (i + 1) * step) for i in range(KEPT // step)]

    def tile_head(t):
        return (UNITS * me + 2 * t) // SEQ

    def head_rows(a, t, cols):
        first = tile_head(t) * KEPT + cols.start
        return full[a, pl.ds(pl.multiple_of(first, step), step), :]

    def tile_rows(a, t):
        return full[a, pl.ds(pl.multiple_of(me * ROWS + t * TILE, TILE), TILE), :]

    def query_tile(t, _):
        query, grad = tile_rows(2, t), tile_rows(3, t)
        top = None
        for cols in chunks:
            scores = lax.dot_general(query, head_rows(0, t, cols), NT, preferred_element_type=jnp.float32)
            scores = scores * (SCALING * LOG2E)
            scores_ref[:, cols] = scores
            part = lane_fold(scores, jnp.maximum)
            top = part if top is None else jnp.maximum(top, part)
        top = jnp.max(top, axis=-1, keepdims=True)
        total = jnp.zeros((TILE, 128), jnp.float32)
        weighted = jnp.zeros((TILE, 128), jnp.float32)
        for cols in chunks:
            weights = jnp.exp2(scores_ref[:, cols] - top)
            dots = lax.dot_general(grad, head_rows(1, t, cols), NT, preferred_element_type=jnp.float32)
            scores_ref[:, cols] = weights
            dots_ref[:, cols] = dots
            total += lane_fold(weights, jnp.add)
            weighted += lane_fold(weights * dots, jnp.add)
        total = jnp.sum(total, axis=-1, keepdims=True)
        share = 1.0 / total
        delta = jnp.sum(weighted, axis=-1, keepdims=True) * share
        result = jnp.zeros((TILE, HD), jnp.float32)
        for cols in chunks:
            dscore = (scores_ref[:, cols] * share) * (dots_ref[:, cols] - delta)
            result += jnp.dot(dscore.astype(jnp.bfloat16), head_rows(0, t, cols), preferred_element_type=jnp.float32)
        rows = pl.ds(pl.multiple_of(t * TILE, TILE), TILE)
        grads, term = norm_grads(raw[1, rows, :], gain_q_ref[...], result * SCALING)
        q_grad[rows, :] = grads.astype(jnp.bfloat16)
        terms[0:8, :] += term
        for i, value in enumerate((top + jnp.log2(total), delta)):
            wide = jnp.broadcast_to(value, (TILE, 128)).T
            for j in range(TILE // SHARE):
                stats[me, i, pl.ds(2 * t + j, 1), :] = wide[0:1, j * SHARE : (j + 1) * SHARE]

        @pl.when(t == 1)
        def _():
            gather_pass(1)

        return 0

    lax.fori_loop(0, TILES, query_tile, 0)


    def shares(member):
        return (
            ((UNITS * member) // SEQ <= (UNITS * me + UNITS - 1) // SEQ)
            & ((UNITS * me) // SEQ <= (UNITS * member + UNITS - 1) // SEQ)
            & (member != me)
        )

    def stat_copy(member, dst):
        core, seq = place(group, member)
        return remote(stats.at[me], stats.at[dst], stat_send.at[member], stat_recv.at[dst], (core, seq, x))

    def stat_start(i, _):
        @pl.when(shares(i))
        def _():
            stat_copy(i, me).start()

        return 0

    def stat_finish(i, _):
        @pl.when(shares(i))
        def _():
            stat_copy(i, i).wait_recv()
            stat_copy(i, me).wait_send()

        return 0

    lax.fori_loop(0, MEMBERS, stat_start, 0)


    def to_self(i):
        return same & (i == s)

    flat_iota = lax.broadcasted_iota(jnp.int32, (step, ROWS), 0)
    for c in range(FLAT // step):
        spread = one_hot(flat_iota + c * step == index)
        rows = jnp.dot(spread, q_grad[...], preferred_element_type=jnp.float32)
        q_slots[c * step : (c + 1) * step, :] = rows.astype(jnp.bfloat16)

    def q_home(i):
        return (
            q_slots.at[pl.ds(pl.multiple_of(i * CHUNK, 16), CHUNK), :],
            home_ref.at[0, pl.ds(pl.multiple_of(seat * CHUNK, 16), CHUNK), :],
        )

    def q_home_start(n, _):
        i = (n + s) % SEQ
        src, dst = q_home(i)

        @pl.when(jnp.logical_not(to_self(i)))
        def _():
            remote(src, dst, home_send.at[0], home_recv.at[0], (clip, i, x)).start()

        @pl.when(to_self(i))
        def _():
            pltpu.make_async_copy(src, dst, home_recv.at[0]).start()

        return 0

    lax.fori_loop(0, SEQ, q_home_start, 0)


    gather_finish(1)
    lax.fori_loop(0, MEMBERS, stat_finish, 0)
    tile_iota = lax.broadcasted_iota(jnp.int32, (2 * SLOTS * SEQ, TILE), 0)

    def stat_row(i, t, cols):
        first = tile_head(t) * SEQ + cols.start // SHARE
        pieces = []
        for j in range(step // SHARE):
            unit = first + j
            pieces.append(stats[unit // UNITS, i, pl.ds(unit % UNITS, 1), :])
        return jnp.concatenate(pieces, axis=1)

    def kv_home(t, i):
        return (
            kv_slots.at[t, :, pl.ds(pl.multiple_of(i * 2 * SLOTS, 16), 2 * SLOTS), :],
            home_ref.at[1:3, pl.ds(pl.multiple_of(seat * CHUNK + t * 2 * SLOTS, 16), 2 * SLOTS), :],
        )

    def key_tile(t, _):
        key, value = tile_rows(0, t), tile_rows(1, t)
        key_grad = jnp.zeros((TILE, HD), jnp.float32)
        value_grad = jnp.zeros((TILE, HD), jnp.float32)
        for cols in chunks:
            query, grad = head_rows(2, t, cols), head_rows(3, t, cols)
            scores = lax.dot_general(key, query, NT, preferred_element_type=jnp.float32)
            weights = jnp.exp2(scores * (SCALING * LOG2E) - stat_row(0, t, cols))
            dots = lax.dot_general(value, grad, NT, preferred_element_type=jnp.float32)
            dscore = weights * (dots - stat_row(1, t, cols))
            key_grad += jnp.dot(dscore.astype(jnp.bfloat16), query, preferred_element_type=jnp.float32)
            value_grad += jnp.dot(weights.astype(jnp.bfloat16), grad, preferred_element_type=jnp.float32)
        rows = pl.ds(pl.multiple_of(t * TILE, TILE), TILE)
        grads, term = norm_grads(raw[0, rows, :], gain_k_ref[...], key_grad * SCALING)
        terms[8:16, :] += term
        tile_codes = []
        for j in range(2):
            code = unit_codes(2 * t + j)
            tile_codes.append((code >> 3) * (2 * SLOTS) + j * SLOTS + (code & 7))
        spread = one_hot(tile_iota == jnp.concatenate(tile_codes, axis=1))
        for i, result in enumerate((grads, value_grad)):
            result = jnp.dot(spread, result.astype(jnp.bfloat16), preferred_element_type=jnp.float32)
            kv_slots[t, i] = result.astype(jnp.bfloat16)

        def start(n, _):
            i = (n + s) % SEQ
            src, dst = kv_home(t, i)

            @pl.when(jnp.logical_not(to_self(i)))
            def _():
                remote(src, dst, home_send.at[1], home_recv.at[1], (clip, i, x)).start()

            @pl.when(to_self(i))
            def _():
                pltpu.make_async_copy(src, dst, home_recv.at[1]).start()

            return 0

        lax.fori_loop(0, SEQ, start, 0)
        return 0

    lax.fori_loop(0, TILES, key_tile, 0)


    def part_start(i, _):
        @pl.when(jnp.logical_not(to_self(i)))
        def _():
            remote(terms, parts.at[seat], part_sem.at[0], part_sem.at[1], (clip, i, x)).start()

        @pl.when(to_self(i))
        def _():
            pltpu.make_async_copy(terms, parts.at[seat], part_sem.at[1]).start()

        return 0

    lax.fori_loop(0, SEQ, part_start, 0)
    remote(parts, parts, part_sem.at[0], part_sem.at[1], sibling).wait_recv()
    partial[...] = jnp.sum(parts[...], axis=0)

    def cross_copy(i, dst):
        return remote(partial, cross.at[dst], cross_send.at[i], cross_recv.at[dst], (i // 4, s, i % 4))

    def cross_start(i, _):
        @pl.when(i != corner)
        def _():
            cross_copy(i, corner).start()

        return 0

    def cross_finish(i, _):
        @pl.when(i != corner)
        def _():
            cross_copy(i, i).wait_recv()
            cross_copy(i, corner).wait_send()

        return 0

    cross[pl.ds(corner, 1)] = partial[...][None]
    lax.fori_loop(0, 8, cross_start, 0)
    lax.fori_loop(0, 8, cross_finish, 0)
    total_ref[...] = jnp.sum(cross[...], axis=0)


    @pl.when(same)
    def _():
        most = SEQ - 1
        for a in range(4):
            rows = slots.at[a, 0 : most * CHUNK, :]
            remote(rows, rows, route_send.at[a], route_recv.at[a], sibling).wait_send()
        rows = q_slots.at[0 : most * CHUNK, :]
        remote(rows, rows, home_send.at[0], home_recv.at[0], sibling).wait_send()
        rows = kv_slots.at[:, :, 0 : most * 2 * SLOTS, :]
        remote(rows, rows, home_send.at[1], home_recv.at[1], sibling).wait_send()
        rows = parts.at[0:most]
        remote(rows, rows, part_sem.at[0], part_sem.at[1], sibling).wait_send()

    @pl.when(jnp.logical_not(same))
    def _():
        for a in range(4):
            remote(slots.at[a], slots.at[a], route_send.at[a], route_recv.at[a], sibling).wait_send()
        remote(q_slots, q_slots, home_send.at[0], home_recv.at[0], sibling).wait_send()
        remote(kv_slots, kv_slots, home_send.at[1], home_recv.at[1], sibling).wait_send()
        remote(parts, parts, part_sem.at[0], part_sem.at[1], sibling).wait_send()

    gather_sent(0)
    gather_sent(1)
    remote(q_slots, home_ref.at[0], home_send.at[0], home_recv.at[0], sibling).wait_recv()
    remote(home_ref.at[1:3], home_ref.at[1:3], home_send.at[1], home_recv.at[1], sibling).wait_recv()


def core(slot_row, token_row, enc, k, v, q, g, gain_q, gain_k):
    bf16, f32 = jnp.bfloat16, jnp.float32
    dma = pltpu.SemaphoreType.DMA
    paths = len(PATHS)
    in_vmem = pl.BlockSpec(memory_space=pltpu.VMEM)
    return pl.pallas_call(
        core_kernel,
        name="core",
        in_specs=[in_vmem] * 9,
        out_specs=[pl.BlockSpec(memory_space=pl.ANY), in_vmem, in_vmem],
        out_shape=(
            jax.ShapeDtypeStruct((3, FLAT, HD), bf16),
            jax.ShapeDtypeStruct((SPAN, SPAN), bf16),
            jax.ShapeDtypeStruct((16, HD), f32),
        ),
        scratch_shapes=[
            pltpu.VMEM((4, FLAT, HD), bf16),
            pltpu.VMEM((4, FLAT, HD), bf16),
            pltpu.VMEM((SEQ, SHARE), jnp.int32),
            pltpu.VMEM((SEQ, SHARE), jnp.int32),
            pltpu.VMEM((ROWS, FLAT), bf16),
            pltpu.VMEM((4, MEMBERS * ROWS, HD), bf16),
            pltpu.VMEM((2, ROWS, HD), bf16),
            pltpu.VMEM((TILE, KEPT), f32),
            pltpu.VMEM((TILE, KEPT), f32),
            pltpu.VMEM((ROWS, HD), bf16),
            pltpu.VMEM((FLAT, HD), bf16),
            pltpu.VMEM((TILES, 2, 2 * SLOTS * SEQ, HD), bf16),
            pltpu.VMEM((MEMBERS, 2, 8, SHARE), f32),
            pltpu.VMEM((16, HD), f32),
            pltpu.VMEM((SEQ, 16, HD), f32),
            pltpu.VMEM((16, HD), f32),
            pltpu.VMEM((8, 16, HD), f32),
            dma((2,)),
            dma((4,)),
            dma((4,)),
            dma((2,)),
            dma((2,)),
            dma((2, paths, 3)),
            dma((2, paths)),
            dma((2, paths)),
            dma((2, paths)),
            dma((2, paths)),
            dma((MEMBERS,)),
            dma((MEMBERS,)),
            dma((2,)),
            dma((2,)),
            dma((2,)),
            dma((8,)),
            dma((8,)),
        ],
        compiler_params=pltpu.CompilerParams(
            collective_id=0, has_side_effects=True, vmem_limit_bytes=VMEM_LIMIT
        ),
    )(slot_row, token_row, enc, k, v, q, g, gain_q, gain_k)


def rows_kernel(back_ref, slots_ref, total_ref, q_ref, k_ref, v_ref, gain_q_ref, gain_k_ref):
    for i, ref in enumerate((q_ref, k_ref, v_ref)):
        ref[0] = jnp.dot(back_ref[...], slots_ref[i], preferred_element_type=jnp.float32).astype(jnp.bfloat16)
    gain_q_ref[...] = jnp.sum(total_ref[0:8, :], axis=0, keepdims=True)
    gain_k_ref[...] = jnp.sum(total_ref[8:16, :], axis=0, keepdims=True)


def to_rows(back, slots, total):
    width = HEAD_PART * HD
    big = jax.ShapeDtypeStruct((1, SPAN, width), jnp.bfloat16)
    small = jax.ShapeDtypeStruct((1, HD), jnp.float32)
    return pl.pallas_call(
        rows_kernel,
        name="to_rows",
        grid=(HEAD_PART,),
        in_specs=[
            pl.BlockSpec((SPAN, SPAN), lambda h: (0, 0)),
            pl.BlockSpec((3, SPAN, HD), lambda h: (0, h, 0)),
            pl.BlockSpec((16, HD), lambda h: (0, 0)),
        ],
        out_specs=[pl.BlockSpec((1, SPAN, HD), lambda h: (0, 0, h))] * 3 + [pl.BlockSpec((1, HD), lambda h: (0, 0))] * 2,
        out_shape=(big, big, big, small, small),
        cost_estimate=pl.CostEstimate(flops=3 * 10**8, bytes_accessed=3 * 10**6, transcendentals=0),
    )(back, slots, total)


def on_device(q_raw, k_raw, v_raw, out_grad, gain_q, gain_k, keep_list):
    s = lax.axis_index("seq")
    listing = keep_list[0].reshape(SEQ, SHARE)
    source = listing // SPAN
    hits = source[None] == jnp.arange(SEQ, dtype=jnp.int32)[:, None, None]
    earlier = jnp.triu(jnp.ones((SHARE, SHARE), jnp.bfloat16), 1)
    counts = jnp.dot(hits.astype(jnp.bfloat16), earlier, preferred_element_type=jnp.float32)
    rank = jnp.sum(jnp.where(hits, counts, 0.0), axis=0).astype(jnp.int32)
    slot = jnp.arange(SEQ, dtype=jnp.int32)[:, None] * SLOTS + rank
    slot_row = jnp.where(source == s, slot, -1).reshape(1, KEPT)
    token_row = (listing - s * SPAN).reshape(1, KEPT)
    enc = source * SLOTS + rank
    home, back, total = core(
        slot_row,
        token_row,
        enc,
        k_raw[0],
        v_raw[0],
        q_raw[0],
        out_grad[0],
        gain_q.reshape(1, HD),
        gain_k.reshape(1, HD),
    )
    q_out, k_out, v_out, gain_q_grad, gain_k_grad = to_rows(back, home, total)
    return q_out, k_out, v_out, gain_q_grad.reshape(HD), gain_k_grad.reshape(HD)


def solution(mesh):
    big = P("dp", "seq", "tensor")
    return jax.shard_map(
        on_device,
        mesh=mesh,
        in_specs=(big, big, big, big, P(), P(), P("dp", None)),
        out_specs=(big, big, big, P(), P()),
        check_vma=False,
    )
```

```python
import math

import jax
import jax.numpy as jnp
from jax import lax
from jax.experimental import pallas as pl
from jax.experimental.pallas import tpu as pltpu
from jax.sharding import PartitionSpec as P

MESH = pl.DeviceIdType.MESH
HD = 128
EPSILON = 1e-06
SEQ = 32
SPAN = 256
SHARE = 128
SLOTS = 8
HEAD_PART = 6
UNITS = 6
ROWS = UNITS * SHARE
CHUNK = UNITS * SLOTS
FLAT = SEQ * CHUNK
MEMBERS = 16
KEPT = SEQ * SHARE
TILE = 256
TILES = ROWS // TILE
SCALING = 1.0 / math.sqrt(HD)
LOG2E = 1.4426950408889634
VMEM_LIMIT = 56 * 1024 * 1024

NT = (((1,), (1,)), ((), ()))

PATHS = (
    (0, None, 0, 768, 0, (1,), 1, 2),
    (1, None, 0, 768, 0, (2, 0), None, None),
    (2, 0, 0, 768, 0, (1,), 1, 0),
    (2, 1, 0, 256, 0, (1,), 1, 0),
    (2, 1, 256, 512, 1, (3, 5), 5, 4),
    (3, 0, 0, 768, 1, (2, 4), 2, 5),
    (3, 1, 0, 768, 1, (4, 2), 4, 5),
    (4, 0, 0, 768, 1, (5, 3), 5, 2),
    (4, 1, 0, 768, 1, (3, 5), 3, 2),
    (5, 0, 0, 512, 1, (4, 2), 2, 3),
    (5, 0, 512, 256, 2, (6,), 6, 7),
    (5, 1, 0, 768, 2, (6,), 6, 7),
    (6, None, 0, 768, 2, (5, 7), None, None),
    (7, None, 0, 768, 2, (6,), 6, 5),
)


def place(x, clip, third, member):
    chip, core = member >> 1, member & 1
    dz = chip >> 2
    turn = chip ^ (7 * dz)
    dx = turn >> 1
    dy = dx ^ (turn & 1)
    y = 2 * (x & 1) + dy
    z = 4 * clip + 2 * third + dz
    return core, y * 8 + z, (x & 2) + dx


def my_place(dp, s, x):
    y, z = s >> 3, s & 7
    dx, dy, dz = x & 1, y & 1, z & 1
    turn = 2 * dx + (dx ^ dy)
    return (x & 2) + (y >> 1), z >> 2, (z >> 1) & 1, turn ^ (7 * dz)


def among(value, options):
    hit = value == options[0]
    for option in options[1:]:
        hit = hit | (value == option)
    return hit


def one_hot(hit):
    return jnp.where(hit, 1.0, 0.0).astype(jnp.bfloat16)


def inverse_norm(x):
    return lax.rsqrt(jnp.mean(x * x, axis=-1, keepdims=True) + EPSILON)


def norm_grads(raw, gain, upstream):
    raw = raw.astype(jnp.float32)
    inverse = inverse_norm(raw)
    scaled = upstream * gain
    inner = jnp.mean(scaled * raw, axis=-1, keepdims=True)
    grads = inverse * scaled - raw * (inverse * inverse * inverse * inner)
    terms = upstream * raw * inverse
    return grads, jnp.sum(terms.reshape(-1, 8, HD), axis=0)


def lane_fold(x, fold):
    parts = [x[:, i * 128 : (i + 1) * 128] for i in range(x.shape[1] // 128)]
    total = parts[0]
    for part in parts[1:]:
        total = fold(total, part)
    return total


def core_kernel(
    list_ref,
    k_ref,
    q_ref,
    v_ref,
    g_ref,
    gain_q_ref,
    gain_k_ref,
    home_ref,
    back_ref,
    total_ref,
    slots,
    arrived,
    enc_ref,
    other,
    codes,
    pick,
    full,
    raw,
    scores_ref,
    dots_ref,
    sums,
    q_grad,
    q_slots,
    kv_slots,
    stats,
    flat_stats,
    terms,
    parts,
    partial,
    cross,
    enc_sem,
    route_send,
    route_recv,
    pair_send,
    pair_recv,
    path_send,
    path_recv,
    pass_send,
    hand_send,
    hand_recv,
    stat_send,
    stat_recv,
    home_send,
    home_recv,
    part_sem,
    cross_send,
    cross_recv,
):
    dp, s, x = lax.axis_index("dp"), lax.axis_index("seq"), lax.axis_index("tensor")
    head_x, clip, third, chip = my_place(dp, s, x)
    me = 2 * chip + dp
    seat = third * MEMBERS + me
    sibling = (1 - dp, s, x)
    corner = dp * 4 + x
    same = (clip == dp) & (head_x == x)

    own_source = jnp.where(same, s, -1)

    def to_self(i):
        return i == own_source

    own_target = jnp.where(same, seat, -1)

    def target(i):
        return place(x, dp, i >> 4, i & 15), i == own_target

    def source(i):
        return (clip, i, head_x)

    def device(c):
        return place(head_x, clip, third, 2 * c + dp)

    def remote(src, dst, send_sem, recv_sem, device):
        return pltpu.make_async_remote_copy(
            src_ref=src, dst_ref=dst, send_sem=send_sem, recv_sem=recv_sem, device_id=device, device_id_type=MESH
        )


    barrier = pltpu.get_barrier_semaphore()

    def greet_device(there):
        pl.semaphore_signal(barrier, inc=1, device_id=there, device_id_type=MESH)

    def greet(i, _):
        there, own = target(i)

        @pl.when(jnp.logical_not(own))
        def _():
            greet_device(there)

        @pl.when(jnp.logical_not(to_self(i)))
        def _():
            greet_device(source(i))

        return 0

    lax.fori_loop(0, SEQ, greet, 0)

    def greet_near(i, _):
        @pl.when(i != corner)
        def _():
            greet_device((i >> 2, s, i & 3))

        @pl.when(i != chip)
        def _():
            greet_device(device(i))

        return 0

    lax.fori_loop(0, 8, greet_near, 0)
    greet_device(sibling)


    listing = list_ref[...]
    from_block = listing >> 8
    hits = one_hot(jnp.concatenate([from_block == i for i in range(SEQ)], axis=0))
    earlier = lax.broadcasted_iota(jnp.int32, (SHARE, SHARE), 0) < lax.broadcasted_iota(jnp.int32, (SHARE, SHARE), 1)
    counts = jnp.dot(hits, one_hot(earlier), preferred_element_type=jnp.float32) * hits.astype(jnp.float32)
    rank = counts[0:SEQ]
    for i in range(1, SEQ):
        rank += counts[i * SEQ : (i + 1) * SEQ]
    rank = rank.astype(jnp.int32)
    enc_ref[...] = from_block * SLOTS + rank
    slot = lax.broadcasted_iota(jnp.int32, (SEQ, SHARE), 0) * SLOTS + rank
    slot = jnp.where(from_block == s, slot, -1)
    token = listing - s * SPAN

    def lanes(x, c):
        return jnp.concatenate([x[j : j + 1] for j in range(c * step // SHARE, (c + 1) * step // SHARE)], axis=1)

    step = 512
    iota = lax.broadcasted_iota(jnp.int32, (SPAN, step), 0)
    take = jnp.zeros((SPAN, SPAN), jnp.float32)
    back = jnp.zeros((SPAN, SPAN), jnp.float32)
    for c in range(KEPT // step):
        a = one_hot(iota == lanes(slot, c))
        b = one_hot(iota == lanes(token, c))
        take += lax.dot_general(a, b, NT, preferred_element_type=jnp.float32)
        back += lax.dot_general(b, a, NT, preferred_element_type=jnp.float32)
    take = take.astype(jnp.bfloat16)
    back_ref[...] = back.astype(jnp.bfloat16)

    def to_slots(i, ref):
        rows = jnp.dot(take, ref[...], preferred_element_type=jnp.float32).astype(jnp.bfloat16)
        for h in range(HEAD_PART):
            slots[i, h * SPAN : (h + 1) * SPAN, :] = rows[:, h * HD : (h + 1) * HD]

    def chunk(ref, a, i):
        return ref.at[a, pl.ds(pl.multiple_of(i * CHUNK, 16), CHUNK), :]

    def route(a):
        def start(n, _):
            i = (n + s) & (SEQ - 1)
            there, own = target(i)

            @pl.when(jnp.logical_not(own))
            def _():
                remote(chunk(slots, a, i), chunk(arrived, a, s), route_send.at[a], route_recv.at[a], there).start()

            return 0

        lax.fori_loop(0, SEQ, start, 0)

        @pl.when(same)
        def _():
            pltpu.make_async_copy(chunk(slots, a, seat), chunk(arrived, a, s), route_recv.at[a]).start()

    to_slots(0, k_ref)
    pl.semaphore_wait(barrier, 2 * SEQ + 15 - 2 * same.astype(jnp.int32))
    exchange = remote(enc_ref, other, enc_sem.at[0], enc_sem.at[1], sibling)
    exchange.start()
    route(0)
    to_slots(1, q_ref)
    route(1)
    to_slots(2, v_ref)
    route(2)
    to_slots(3, g_ref)


    exchange.wait()
    codes[...] = jnp.where(clip == dp, enc_ref[...], other[...])

    def unit_codes(u):
        return codes[pl.ds((UNITS * me + u) & (SEQ - 1), 1), :]

    wide_iota = lax.broadcasted_iota(jnp.int32, (SHARE, 128), 1).astype(jnp.float32)
    index = []
    for u in range(UNITS):
        code = unit_codes(u)
        code = (code >> 3) * CHUNK + u * SLOTS + (code & 7)
        index.append(code)
        wide = jnp.broadcast_to(code.astype(jnp.float32), (SHARE, 128)).T
        for c in range(FLAT // 128):
            pick[u * SHARE : (u + 1) * SHARE, c * 128 : (c + 1) * 128] = one_hot(wide == wide_iota + c * 128.0)
    index = jnp.concatenate(index, axis=1)

    own_rows = pl.ds(pl.multiple_of(me * ROWS, 256), ROWS)

    def to_dense(a):
        remote(slots.at[a], arrived.at[a], route_send.at[a], route_recv.at[a], sibling).wait_recv()
        rows = jnp.dot(pick[...], arrived[a], preferred_element_type=jnp.float32)
        if a < 2:
            raw[a] = rows.astype(jnp.bfloat16)
            gain = (gain_k_ref, gain_q_ref)[a][...]
            rows = rows * inverse_norm(rows) * gain
        full[a, own_rows, :] = rows.astype(jnp.bfloat16)


    def heads_of(member):
        return (UNITS * member) >> 5, (UNITS * member + UNITS - 1) >> 5

    my_heads, pair_heads = heads_of(me), heads_of(2 * chip + 1 - dp)

    def have(heads, head):
        return (heads[0] <= head) & (head <= heads[1])

    def segment(phase, member, first, count):
        return full.at[phase, pl.ds(pl.multiple_of(member * ROWS + first, 256), count), :]

    def lane(core):
        return True if core is None else dp == core

    def other_lane(core):
        return True if core is None else dp != core

    def reached(path):
        chips = list(path[5])
        if path[7] is not None:
            chips.append(path[7])
        return chips

    def pair(phase, member):
        rows = segment(phase, member, 0, ROWS)
        return remote(rows, rows, pair_send.at[phase], pair_recv.at[phase], sibling)

    def path_copy(phase, n, member, to, send_sem):
        _, _, first, count, *_ = PATHS[n]
        rows = segment(phase, member, first, count)
        return remote(rows, rows, send_sem, path_recv.at[phase, n], device(to))

    def hand_copy(phase, n, member):
        _, _, first, count, *_ = PATHS[n]
        rows = segment(phase, member, first, count)
        return remote(rows, rows, hand_send.at[phase, n], hand_recv.at[phase, n], sibling)

    def gather_start(phase):
        for n, (c, core, _, _, _, direct, _, _) in enumerate(PATHS):

            @pl.when((chip == c) & lane(core))
            def _():
                for i, to in enumerate(direct):
                    path_copy(phase, n, me, to, path_send.at[phase, n, i]).start()

        pair(phase, me).start()

    def gather_pass(phase):
        def take_in(n, chips, via, to):
            c, core, _, _, head, *_ = PATHS[n]
            member = 2 * c + dp

            @pl.when(among(chip, chips) & lane(core))
            def _():
                path_copy(phase, n, member, c, path_send.at[phase, n, 0]).wait_recv()
                if via is not None:

                    @pl.when(chip == via)
                    def _():
                        path_copy(phase, n, member, to, pass_send.at[phase, n]).start()

                @pl.when(have(pair_heads, head))
                def _():
                    hand_copy(phase, n, member).start()

        for n, path in enumerate(PATHS):
            take_in(n, path[5], path[6], path[7])
        for n, path in enumerate(PATHS):
            if path[7] is not None:
                take_in(n, (path[7],), None, None)

    def gather_finish(phase):
        pair(phase, 2 * chip + 1 - dp).wait_recv()
        for n, path in enumerate(PATHS):
            c, core, _, _, head, *_ = path

            @pl.when(among(chip, reached(path)) & other_lane(core) & have(my_heads, head))
            def _():
                hand_copy(phase, n, 2 * c + 1 - dp).wait_recv()

    def gather_sent(phase):
        pair(phase, me).wait_send()
        for n, path in enumerate(PATHS):
            c, core, _, _, head, direct, via, to = path
            member = 2 * c + dp

            @pl.when((chip == c) & lane(core))
            def _():
                for i, chip_to in enumerate(direct):
                    path_copy(phase, n, me, chip_to, path_send.at[phase, n, i]).wait_send()

            @pl.when(among(chip, reached(path)) & lane(core))
            def _():
                if via is not None:

                    @pl.when(chip == via)
                    def _():
                        path_copy(phase, n, member, to, pass_send.at[phase, n]).wait_send()

                @pl.when(have(pair_heads, head))
                def _():
                    hand_copy(phase, n, member).wait_send()

    to_dense(0)
    gather_start(0)
    route(3)
    to_dense(1)
    gather_pass(0)
    gather_finish(0)


    terms[...] = jnp.zeros_like(terms)
    chunks = [slice(i * step, (i + 1) * step) for i in range(KEPT // step)]

    def tile_head(t):
        return (UNITS * me + 2 * t) >> 5

    def head_rows(a, t, cols):
        first = tile_head(t) * KEPT + cols.start
        return full[a, pl.ds(pl.multiple_of(first, step), step), :]

    def tile_rows(a, t):
        return full[a, pl.ds(pl.multiple_of(me * ROWS + t * TILE, TILE), TILE), :]

    def local_rows(t):
        return pl.ds(pl.multiple_of(t * TILE, TILE), TILE)

    def store_stat(i, t, value):
        wide = jnp.broadcast_to(value, (TILE, 128)).T
        for j in range(TILE // SHARE):
            stats[me, i, pl.ds(2 * t + j, 1), :] = wide[0:1, j * SHARE : (j + 1) * SHARE]

    def score_tile(t, _):
        query = tile_rows(1, t)
        rows = local_rows(t)
        top = None
        for cols in chunks:
            scores = lax.dot_general(query, head_rows(0, t, cols), NT, preferred_element_type=jnp.float32)
            scores = scores * (SCALING * LOG2E)
            scores_ref[rows, cols] = scores
            part = lane_fold(scores, jnp.maximum)
            top = part if top is None else jnp.maximum(top, part)
        top = jnp.max(top, axis=-1, keepdims=True)
        total = jnp.zeros((TILE, 128), jnp.float32)
        for cols in chunks:
            weights = jnp.exp2(scores_ref[rows, cols] - top)
            scores_ref[rows, cols] = weights
            total += lane_fold(weights, jnp.add)
        total = jnp.sum(total, axis=-1, keepdims=True)
        sums[rows, :] = jnp.broadcast_to(total, (TILE, 128))
        store_stat(0, t, top + jnp.log2(total))

        @pl.when(t == 0)
        def _():
            to_dense(2)
            gather_start(2)
            gather_start(1)

        return 0

    lax.fori_loop(0, TILES, score_tile, 0)
    gather_pass(2)
    to_dense(3)
    gather_start(3)
    gather_finish(2)

    def query_tile(t, _):
        grad = tile_rows(3, t)
        rows = local_rows(t)
        weighted = jnp.zeros((TILE, 128), jnp.float32)
        for cols in chunks:
            dots = lax.dot_general(grad, head_rows(2, t, cols), NT, preferred_element_type=jnp.float32)
            dots_ref[:, cols] = dots
            weighted += lane_fold(scores_ref[rows, cols] * dots, jnp.add)
        share = 1.0 / sums[rows, 0:1]
        delta = jnp.sum(weighted, axis=-1, keepdims=True) * share
        result = jnp.zeros((TILE, HD), jnp.float32)
        for cols in chunks:
            dscore = (scores_ref[rows, cols] * share) * (dots_ref[:, cols] - delta)
            result += jnp.dot(dscore.astype(jnp.bfloat16), head_rows(0, t, cols), preferred_element_type=jnp.float32)
        grads, term = norm_grads(raw[1, rows, :], gain_q_ref[...], result * SCALING)
        q_grad[rows, :] = grads.astype(jnp.bfloat16)
        terms[0:8, :] += term
        store_stat(1, t, delta)

        @pl.when(t == 0)
        def _():
            gather_pass(1)

        @pl.when(t == 1)
        def _():
            gather_pass(3)

        return 0

    lax.fori_loop(0, TILES, query_tile, 0)


    def shares(member):
        first, last = heads_of(member)
        return (first <= my_heads[1]) & (my_heads[0] <= last) & (member != me)

    def stat_copy(member, dst):
        there = place(head_x, clip, third, member)
        return remote(stats.at[me], stats.at[dst], stat_send.at[member], stat_recv.at[dst], there)

    def stat_start(i, _):
        @pl.when(shares(i))
        def _():
            stat_copy(i, me).start()

        return 0

    def stat_finish(i, _):
        @pl.when(shares(i))
        def _():
            stat_copy(i, i).wait_recv()
            stat_copy(i, me).wait_send()

        return 0

    def stat_flat(i):
        @pl.when(shares(i) | (me == i))
        def _():
            flat_stats[:, i * UNITS : (i + 1) * UNITS, :] = stats[i, :, 0:UNITS, :]

    lax.fori_loop(0, MEMBERS, stat_start, 0)


    flat_iota = lax.broadcasted_iota(jnp.int32, (step, ROWS), 0)
    for c in range(FLAT // step):
        spread = one_hot(flat_iota + c * step == index)
        rows = jnp.dot(spread, q_grad[...], preferred_element_type=jnp.float32)
        q_slots[c * step : (c + 1) * step, :] = rows.astype(jnp.bfloat16)

    def q_home(i):
        return (
            q_slots.at[pl.ds(pl.multiple_of(i * CHUNK, 16), CHUNK), :],
            home_ref.at[0, pl.ds(pl.multiple_of(seat * CHUNK, 16), CHUNK), :],
        )

    def q_home_start(n, _):
        i = (n + s) & (SEQ - 1)
        src, dst = q_home(i)

        @pl.when(jnp.logical_not(to_self(i)))
        def _():
            remote(src, dst, home_send.at[0], home_recv.at[0], source(i)).start()

        return 0

    lax.fori_loop(0, SEQ, q_home_start, 0)

    @pl.when(same)
    def _():
        src, dst = q_home(s)
        pltpu.make_async_copy(src, dst, home_recv.at[0]).start()


    gather_finish(1)
    gather_finish(3)
    lax.fori_loop(0, MEMBERS, stat_finish, 0)
    for i in range(MEMBERS):
        stat_flat(i)
    tile_iota = lax.broadcasted_iota(jnp.int32, (2 * SLOTS * SEQ, TILE), 0)

    def stat_row(i, t, cols):
        first = tile_head(t) * SEQ + cols.start // SHARE
        return jnp.concatenate([flat_stats[i, pl.ds(first + j, 1), :] for j in range(step // SHARE)], axis=1)

    def kv_home(t, i):
        return (
            kv_slots.at[t, :, pl.ds(pl.multiple_of(i * 2 * SLOTS, 16), 2 * SLOTS), :],
            home_ref.at[1:3, pl.ds(pl.multiple_of(seat * CHUNK + t * 2 * SLOTS, 16), 2 * SLOTS), :],
        )

    def key_tile(t, _):
        key, value = tile_rows(0, t), tile_rows(2, t)
        key_grad = jnp.zeros((TILE, HD), jnp.float32)
        value_grad = jnp.zeros((TILE, HD), jnp.float32)
        for cols in chunks:
            query, grad = head_rows(1, t, cols), head_rows(3, t, cols)
            scores = lax.dot_general(key, query, NT, preferred_element_type=jnp.float32)
            weights = jnp.exp2(scores * (SCALING * LOG2E) - stat_row(0, t, cols))
            dots = lax.dot_general(value, grad, NT, preferred_element_type=jnp.float32)
            dscore = weights * (dots - stat_row(1, t, cols))
            key_grad += jnp.dot(dscore.astype(jnp.bfloat16), query, preferred_element_type=jnp.float32)
            value_grad += jnp.dot(weights.astype(jnp.bfloat16), grad, preferred_element_type=jnp.float32)
        grads, term = norm_grads(raw[0, local_rows(t), :], gain_k_ref[...], key_grad * SCALING)
        terms[8:16, :] += term
        tile_codes = []
        for j in range(2):
            code = unit_codes(2 * t + j)
            tile_codes.append((code >> 3) * (2 * SLOTS) + j * SLOTS + (code & 7))
        spread = one_hot(tile_iota == jnp.concatenate(tile_codes, axis=1))
        for i, result in enumerate((grads, value_grad)):
            result = jnp.dot(spread, result.astype(jnp.bfloat16), preferred_element_type=jnp.float32)
            kv_slots[t, i] = result.astype(jnp.bfloat16)

        def start(n, _):
            i = (n + s) & (SEQ - 1)
            src, dst = kv_home(t, i)

            @pl.when(jnp.logical_not(to_self(i)))
            def _():
                remote(src, dst, home_send.at[1], home_recv.at[1], source(i)).start()

            return 0

        lax.fori_loop(0, SEQ, start, 0)

        @pl.when(same)
        def _():
            src, dst = kv_home(t, s)
            pltpu.make_async_copy(src, dst, home_recv.at[1]).start()

        return 0

    lax.fori_loop(0, TILES, key_tile, 0)


    def part_start(i, _):
        @pl.when(jnp.logical_not(to_self(i)))
        def _():
            remote(terms, parts.at[seat], part_sem.at[0], part_sem.at[1], source(i)).start()

        return 0

    lax.fori_loop(0, SEQ, part_start, 0)

    @pl.when(same)
    def _():
        pltpu.make_async_copy(terms, parts.at[seat], part_sem.at[1]).start()

    remote(parts, parts, part_sem.at[0], part_sem.at[1], sibling).wait_recv()
    partial[...] = jnp.sum(parts[...], axis=0)

    def cross_copy(i, dst):
        return remote(partial, cross.at[dst], cross_send.at[i], cross_recv.at[dst], (i >> 2, s, i & 3))

    def cross_start(i, _):
        @pl.when(i != corner)
        def _():
            cross_copy(i, corner).start()

        return 0

    def cross_finish(i, _):
        @pl.when(i != corner)
        def _():
            cross_copy(i, i).wait_recv()
            cross_copy(i, corner).wait_send()

        return 0

    cross[pl.ds(corner, 1)] = partial[...][None]
    lax.fori_loop(0, 8, cross_start, 0)
    lax.fori_loop(0, 8, cross_finish, 0)
    total_ref[...] = jnp.sum(cross[...], axis=0)


    @pl.when(same)
    def _():
        most = SEQ - 1
        for a in range(4):
            rows = slots.at[a, 0 : most * CHUNK, :]
            remote(rows, rows, route_send.at[a], route_recv.at[a], sibling).wait_send()
        rows = q_slots.at[0 : most * CHUNK, :]
        remote(rows, rows, home_send.at[0], home_recv.at[0], sibling).wait_send()
        rows = kv_slots.at[:, :, 0 : most * 2 * SLOTS, :]
        remote(rows, rows, home_send.at[1], home_recv.at[1], sibling).wait_send()
        rows = parts.at[0:most]
        remote(rows, rows, part_sem.at[0], part_sem.at[1], sibling).wait_send()

    @pl.when(jnp.logical_not(same))
    def _():
        for a in range(4):
            remote(slots.at[a], slots.at[a], route_send.at[a], route_recv.at[a], sibling).wait_send()
        remote(q_slots, q_slots, home_send.at[0], home_recv.at[0], sibling).wait_send()
        remote(kv_slots, kv_slots, home_send.at[1], home_recv.at[1], sibling).wait_send()
        remote(parts, parts, part_sem.at[0], part_sem.at[1], sibling).wait_send()

    for a in range(4):
        gather_sent(a)
    remote(q_slots, home_ref.at[0], home_send.at[0], home_recv.at[0], sibling).wait_recv()
    remote(home_ref.at[1:3], home_ref.at[1:3], home_send.at[1], home_recv.at[1], sibling).wait_recv()


def core(listing, k, q, v, g, gain_q, gain_k):
    bf16, f32 = jnp.bfloat16, jnp.float32
    dma = pltpu.SemaphoreType.DMA
    paths = len(PATHS)
    in_vmem = pl.BlockSpec(memory_space=pltpu.VMEM)
    return pl.pallas_call(
        core_kernel,
        name="core",
        in_specs=[in_vmem] * 7,
        out_specs=[pl.BlockSpec(memory_space=pl.ANY), in_vmem, in_vmem],
        out_shape=(
            jax.ShapeDtypeStruct((3, FLAT, HD), bf16),
            jax.ShapeDtypeStruct((SPAN, SPAN), bf16),
            jax.ShapeDtypeStruct((16, HD), f32),
        ),
        scratch_shapes=[
            pltpu.VMEM((4, FLAT, HD), bf16),
            pltpu.VMEM((4, FLAT, HD), bf16),
            pltpu.VMEM((SEQ, SHARE), jnp.int32),
            pltpu.VMEM((SEQ, SHARE), jnp.int32),
            pltpu.VMEM((SEQ, SHARE), jnp.int32),
            pltpu.VMEM((ROWS, FLAT), bf16),
            pltpu.VMEM((4, MEMBERS * ROWS, HD), bf16),
            pltpu.VMEM((2, ROWS, HD), bf16),
            pltpu.VMEM((ROWS, KEPT), f32),
            pltpu.VMEM((TILE, KEPT), f32),
            pltpu.VMEM((ROWS, 128), f32),
            pltpu.VMEM((ROWS, HD), bf16),
            pltpu.VMEM((FLAT, HD), bf16),
            pltpu.VMEM((TILES, 2, 2 * SLOTS * SEQ, HD), bf16),
            pltpu.VMEM((MEMBERS, 2, 8, SHARE), f32),
            pltpu.VMEM((2, MEMBERS * UNITS, SHARE), f32),
            pltpu.VMEM((16, HD), f32),
            pltpu.VMEM((SEQ, 16, HD), f32),
            pltpu.VMEM((16, HD), f32),
            pltpu.VMEM((8, 16, HD), f32),
            dma((2,)),
            dma((4,)),
            dma((4,)),
            dma((4,)),
            dma((4,)),
            dma((4, paths, 2)),
            dma((4, paths)),
            dma((4, paths)),
            dma((4, paths)),
            dma((4, paths)),
            dma((MEMBERS,)),
            dma((MEMBERS,)),
            dma((2,)),
            dma((2,)),
            dma((2,)),
            dma((8,)),
            dma((8,)),
        ],
        compiler_params=pltpu.CompilerParams(
            collective_id=0, has_side_effects=True, vmem_limit_bytes=VMEM_LIMIT
        ),
    )(listing, k, q, v, g, gain_q, gain_k)


def rows_kernel(back_ref, slots_ref, total_ref, q_ref, k_ref, v_ref, gain_q_ref, gain_k_ref):
    for i, ref in enumerate((q_ref, k_ref, v_ref)):
        for h in range(slots_ref.shape[1] // SPAN):
            rows = slots_ref[i, h * SPAN : (h + 1) * SPAN, :]
            rows = jnp.dot(back_ref[...], rows, preferred_element_type=jnp.float32)
            ref[0, :, h * HD : (h + 1) * HD] = rows.astype(jnp.bfloat16)
    gain_q_ref[...] = jnp.sum(total_ref[0:8, :], axis=0, keepdims=True)
    gain_k_ref[...] = jnp.sum(total_ref[8:16, :], axis=0, keepdims=True)


def to_rows(back, slots, total):
    width = HEAD_PART * HD
    parts = 2
    big = jax.ShapeDtypeStruct((1, SPAN, width), jnp.bfloat16)
    small = jax.ShapeDtypeStruct((1, HD), jnp.float32)
    return pl.pallas_call(
        rows_kernel,
        name="to_rows",
        grid=(parts,),
        in_specs=[
            pl.BlockSpec((SPAN, SPAN), lambda h: (0, 0)),
            pl.BlockSpec((3, FLAT // parts, HD), lambda h: (0, h, 0)),
            pl.BlockSpec((16, HD), lambda h: (0, 0)),
        ],
        out_specs=[pl.BlockSpec((1, SPAN, width // parts), lambda h: (0, 0, h))] * 3
        + [pl.BlockSpec((1, HD), lambda h: (0, 0))] * 2,
        out_shape=(big, big, big, small, small),
        compiler_params=pltpu.CompilerParams(vmem_limit_bytes=VMEM_LIMIT),
        cost_estimate=pl.CostEstimate(flops=3 * 10**8, bytes_accessed=3 * 10**6, transcendentals=0),
    )(back, slots, total)


def on_device(q_raw, k_raw, v_raw, out_grad, gain_q, gain_k, keep_list):
    home, back, total = core(
        keep_list.reshape(SEQ, SHARE),
        k_raw[0],
        q_raw[0],
        v_raw[0],
        out_grad[0],
        gain_q.reshape(1, HD),
        gain_k.reshape(1, HD),
    )
    q_out, k_out, v_out, gain_q_grad, gain_k_grad = to_rows(back, home, total)
    return q_out, k_out, v_out, gain_q_grad.reshape(HD), gain_k_grad.reshape(HD)


def solution(mesh):
    big = P("dp", "seq", "tensor")
    return jax.shard_map(
        on_device,
        mesh=mesh,
        in_specs=(big, big, big, big, P(), P(), P("dp", None)),
        out_specs=(big, big, big, P(), P()),
        check_vma=False,
    )
```

```python
import math

import jax
import jax.numpy as jnp
from jax import lax
from jax.experimental import pallas as pl
from jax.experimental.pallas import tpu as pltpu
from jax.sharding import PartitionSpec as P

MESH = pl.DeviceIdType.MESH
HD = 128
EPSILON = 1e-06
SEQ = 32
SPAN = 256
SHARE = 128
SLOTS = 8
HEAD_PART = 6
UNITS = 8
ROWS = UNITS * SHARE
CHUNK = UNITS * SLOTS
MEMBERS = 4
TARGETS = HEAD_PART * MEMBERS
OUT = TARGETS * CHUNK
FLAT = SEQ * CHUNK
KEPT = SEQ * SHARE
TILE = 256
TILES = ROWS // TILE
SCALING = 1.0 / math.sqrt(HD)
LOG2E = 1.4426950408889634
VMEM_LIMIT = 56 * 1024 * 1024

NT = (((1,), (1,)), ((), ()))

def place(x, clip, i):
    head, quarter = i >> 2, i & 3
    third = (head * 11) >> 5
    pair = head - 3 * third
    y = 2 * (x & 1) + (pair & 1)
    z = 4 * clip + 2 * third + (pair >> 1)
    return quarter & 1, y * 8 + z, (x & 2) + (quarter >> 1)


def my_place(dp, s, x):
    y, z = s >> 3, s & 7
    third, pair = (z >> 1) & 1, (y & 1) + 2 * (z & 1)
    return (x & 2) + (y >> 1), z >> 2, (3 * third + pair) * 4 + 2 * (x & 1) + dp, pair < 3


def one_hot(hit):
    return jnp.where(hit, 1.0, 0.0).astype(jnp.bfloat16)


def inverse_norm(x):
    return lax.rsqrt(jnp.mean(x * x, axis=-1, keepdims=True) + EPSILON)


def norm_grads(raw, gain, upstream):
    raw = raw.astype(jnp.float32)
    inverse = inverse_norm(raw)
    scaled = upstream * gain
    inner = jnp.mean(scaled * raw, axis=-1, keepdims=True)
    grads = inverse * scaled - raw * (inverse * inverse * inverse * inner)
    terms = upstream * raw * inverse
    return grads, jnp.sum(terms.reshape(-1, 8, HD), axis=0)


def lane_fold(x, fold):
    parts = [x[:, i * 128 : (i + 1) * 128] for i in range(x.shape[1] // 128)]
    total = parts[0]
    for part in parts[1:]:
        total = fold(total, part)
    return total


def core_kernel(
    list_ref,
    k_ref,
    q_ref,
    v_ref,
    g_ref,
    gain_q_ref,
    gain_k_ref,
    home_ref,
    back_ref,
    total_ref,
    slots,
    arrived,
    enc_ref,
    other,
    codes,
    pick,
    full,
    raw,
    scores_ref,
    dots_ref,
    sums,
    q_slots,
    kv_slots,
    stats,
    terms,
    part_bytes,
    parts,
    partial,
    cross,
    enc_sem,
    route_send,
    route_recv,
    near_send,
    near_recv,
    stat_send,
    stat_recv,
    home_send,
    home_recv,
    part_sem,
    cross_send,
    cross_recv,
):
    dp, s, x = lax.axis_index("dp"), lax.axis_index("seq"), lax.axis_index("tensor")
    head_x, clip, seat, active = my_place(dp, s, x)
    me = seat & 3
    sibling = (1 - dp, s, x)
    corner = dp * 4 + x
    same = active & (clip == dp) & (head_x == x)
    own_source = jnp.where(same, s, -1)
    own_target = jnp.where(same, seat, -1)

    def to_self(i):
        return i == own_source

    def target(i):
        return place(x, dp, i), i == own_target

    def source(i):
        return (clip, i, head_x)

    def member(i):
        return (i & 1, s, (x & 2) + (i >> 1))

    def remote(src, dst, send_sem, recv_sem, device):
        return pltpu.make_async_remote_copy(
            src_ref=src, dst_ref=dst, send_sem=send_sem, recv_sem=recv_sem, device_id=device, device_id_type=MESH
        )


    barrier = pltpu.get_barrier_semaphore()

    def greet_device(there):
        pl.semaphore_signal(barrier, inc=1, device_id=there, device_id_type=MESH)

    def greet_target(i, _):
        there, own = target(i)

        @pl.when(jnp.logical_not(own))
        def _():
            greet_device(there)

        return 0

    def greet_source(i, _):
        @pl.when(jnp.logical_not(to_self(i)))
        def _():
            greet_device(source(i))

        return 0

    def greet_corner(i, _):
        @pl.when(i != corner)
        def _():
            greet_device((i >> 2, s, i & 3))

        return 0

    @pl.when(active)
    def _():
        lax.fori_loop(0, SEQ, greet_source, 0)
        for step in (1, 2, 3):
            greet_device(member(me ^ step))

    lax.fori_loop(0, TARGETS, greet_target, 0)
    lax.fori_loop(0, 8, greet_corner, 0)


    listing = list_ref[...]
    from_block = listing >> 8
    hits = one_hot(jnp.concatenate([from_block == i for i in range(SEQ)], axis=0))
    earlier = lax.broadcasted_iota(jnp.int32, (SHARE, SHARE), 0) < lax.broadcasted_iota(jnp.int32, (SHARE, SHARE), 1)
    counts = jnp.dot(hits, one_hot(earlier), preferred_element_type=jnp.float32) * hits.astype(jnp.float32)
    rank = counts[0:SEQ]
    for i in range(1, SEQ):
        rank += counts[i * SEQ : (i + 1) * SEQ]
    rank = rank.astype(jnp.int32)
    enc_ref[...] = from_block * SLOTS + rank
    slot = lax.broadcasted_iota(jnp.int32, (SEQ, SHARE), 0) * SLOTS + rank
    slot = jnp.where(from_block == s, slot, -1)
    token = listing - s * SPAN

    def lanes(x, c):
        return jnp.concatenate([x[j : j + 1] for j in range(c * step // SHARE, (c + 1) * step // SHARE)], axis=1)

    step = 512
    iota = lax.broadcasted_iota(jnp.int32, (SPAN, step), 0)
    take = jnp.zeros((SPAN, SPAN), jnp.float32)
    back = jnp.zeros((SPAN, SPAN), jnp.float32)
    for c in range(KEPT // step):
        a = one_hot(iota == lanes(slot, c))
        b = one_hot(iota == lanes(token, c))
        take += lax.dot_general(a, b, NT, preferred_element_type=jnp.float32)
        back += lax.dot_general(b, a, NT, preferred_element_type=jnp.float32)
    take = take.astype(jnp.bfloat16)
    back_ref[...] = back.astype(jnp.bfloat16)

    def to_slots(i, ref):
        rows = jnp.dot(take, ref[...], preferred_element_type=jnp.float32).astype(jnp.bfloat16)
        for h in range(HEAD_PART):
            slots[i, h * SPAN : (h + 1) * SPAN, :] = rows[:, h * HD : (h + 1) * HD]

    def chunk(ref, a, i):
        return ref.at[a, pl.ds(pl.multiple_of(i * CHUNK, 16), CHUNK), :]

    turn = (3 * s) >> 2

    def route(a):
        def start(n, _):
            i = n + turn
            i = jnp.where(i < TARGETS, i, i - TARGETS)
            there, own = target(i)

            @pl.when(jnp.logical_not(own))
            def _():
                remote(chunk(slots, a, i), chunk(arrived, a, s), route_send.at[a], route_recv.at[a], there).start()

            return 0

        lax.fori_loop(0, TARGETS, start, 0)

        @pl.when(same)
        def _():
            pltpu.make_async_copy(chunk(slots, a, seat), chunk(arrived, a, s), route_recv.at[a]).start()

    to_slots(0, k_ref)
    arrivals = jnp.where(active, SEQ + 3, 0) - jnp.where(same, 2, 0)
    pl.semaphore_wait(barrier, TARGETS + 7 + arrivals)
    exchange = remote(enc_ref, other, enc_sem.at[0], enc_sem.at[1], sibling)

    @pl.when(active)
    def _():
        exchange.start()

    route(0)
    to_slots(1, q_ref)
    route(1)
    to_slots(2, v_ref)
    to_slots(3, g_ref)


    def unit_codes(u):
        return codes[pl.ds(UNITS * me + u, 1), :]

    def build_pick():
        exchange.wait()
        codes[...] = jnp.where(clip == dp, enc_ref[...], other[...])
        wide_iota = lax.broadcasted_iota(jnp.int32, (SHARE, 128), 1).astype(jnp.float32)
        for u in range(UNITS):
            code = unit_codes(u)
            code = (code >> 3) * CHUNK + u * SLOTS + (code & 7)
            wide = jnp.broadcast_to(code.astype(jnp.float32), (SHARE, 128)).T
            for c in range(FLAT // 128):
                pick[u * SHARE : (u + 1) * SHARE, c * 128 : (c + 1) * 128] = one_hot(wide == wide_iota + c * 128.0)

    own_rows = pl.ds(pl.multiple_of(me * ROWS, 256), ROWS)

    def to_dense(a):
        remote(arrived.at[a], arrived.at[a], route_send.at[a], route_recv.at[a], sibling).wait_recv()
        rows = jnp.dot(pick[...], arrived[a], preferred_element_type=jnp.float32)
        if a < 2:
            raw[a] = rows.astype(jnp.bfloat16)
            gain = (gain_k_ref, gain_q_ref)[a][...]
            rows = rows * inverse_norm(rows) * gain
        full[a, own_rows, :] = rows.astype(jnp.bfloat16)


    def rows_of(a, i):
        return full.at[a, pl.ds(pl.multiple_of(i * ROWS, ROWS), ROWS), :]

    def near(a, way, rows, there):
        return remote(rows_of(a, rows), rows_of(a, rows), near_send.at[a, way], near_recv.at[a, way], member(there))

    def gather_start(a):
        near(a, 0, me, me ^ 2).start()
        near(a, 1, me, me ^ 1).start()

    def gather_pass(a):
        near(a, 0, me ^ 2, me).wait_recv()
        near(a, 2, me ^ 2, me ^ 1).start()

    def gather_finish(a):
        near(a, 1, me ^ 1, me).wait_recv()
        near(a, 2, me ^ 3, me).wait_recv()

    def gather_sent(a):
        near(a, 0, me, me ^ 2).wait_send()
        near(a, 1, me, me ^ 1).wait_send()
        near(a, 2, me ^ 2, me ^ 1).wait_send()


    chunks = [slice(i * step, (i + 1) * step) for i in range(KEPT // step)]

    def head_rows(a, cols):
        return full[a, cols, :]

    def tile_rows(a, t):
        return full[a, pl.ds(pl.multiple_of(me * ROWS + t * TILE, TILE), TILE), :]

    def local_rows(t):
        return pl.ds(pl.multiple_of(t * TILE, TILE), TILE)

    def store_stat(i, t, value):
        wide = jnp.broadcast_to(value, (TILE, 128)).T
        for j in range(TILE // SHARE):
            stats[me, i, pl.ds(2 * t + j, 1), :] = wide[0:1, j * SHARE : (j + 1) * SHARE]

    def score_tile(t, _):
        query = tile_rows(1, t)
        rows = local_rows(t)
        top = None
        for cols in chunks:
            scores = lax.dot_general(query, head_rows(0, cols), NT, preferred_element_type=jnp.float32)
            scores = scores * (SCALING * LOG2E)
            scores_ref[rows, cols] = scores
            part = lane_fold(scores, jnp.maximum)
            top = part if top is None else jnp.maximum(top, part)
        top = jnp.max(top, axis=-1, keepdims=True)
        total = jnp.zeros((TILE, 128), jnp.float32)
        for cols in chunks:
            weights = jnp.exp2(scores_ref[rows, cols] - top)
            scores_ref[rows, cols] = weights
            total += lane_fold(weights, jnp.add)
        total = jnp.sum(total, axis=-1, keepdims=True)
        sums[rows, :] = jnp.broadcast_to(total, (TILE, 128))
        store_stat(0, t, top + jnp.log2(total))

        @pl.when(t == 1)
        def _():
            to_dense(2)
            gather_start(2)
            gather_start(1)

        return 0

    def spread_tile(t, rows):
        tile_iota = lax.broadcasted_iota(jnp.int32, (2 * SLOTS * SEQ, TILE), 0)
        tile_codes = []
        for j in range(2):
            code = unit_codes(2 * t + j)
            tile_codes.append((code >> 3) * (2 * SLOTS) + j * SLOTS + (code & 7))
        spread = one_hot(tile_iota == jnp.concatenate(tile_codes, axis=1))
        rows = jnp.dot(spread, rows.astype(jnp.bfloat16), preferred_element_type=jnp.float32)
        return rows.astype(jnp.bfloat16).reshape(SEQ, 2 * SLOTS, HD)

    def query_tile(t, _):
        grad = tile_rows(3, t)
        rows = local_rows(t)
        weighted = jnp.zeros((TILE, 128), jnp.float32)
        for cols in chunks:
            dots = lax.dot_general(grad, head_rows(2, cols), NT, preferred_element_type=jnp.float32)
            dots_ref[:, cols] = dots
            weighted += lane_fold(scores_ref[rows, cols] * dots, jnp.add)
        share = 1.0 / sums[rows, 0:1]
        delta = jnp.sum(weighted, axis=-1, keepdims=True) * share
        result = jnp.zeros((TILE, HD), jnp.float32)
        for cols in chunks:
            dscore = (scores_ref[rows, cols] * share) * (dots_ref[:, cols] - delta)
            result += jnp.dot(dscore.astype(jnp.bfloat16), head_rows(0, cols), preferred_element_type=jnp.float32)
        grads, term = norm_grads(raw[1, rows, :], gain_q_ref[...], result * SCALING)
        terms[0:8, :] += term
        store_stat(1, t, delta)

        q_slots[:, pl.ds(pl.multiple_of(t * 2 * SLOTS, 16), 2 * SLOTS), :] = spread_tile(t, grads)

        @pl.when(t == 0)
        def _():
            gather_pass(1)

        @pl.when(t == 1)
        def _():
            gather_pass(3)

        return 0


    def stat_copy(rows, there):
        return remote(stats.at[rows], stats.at[rows], stat_send.at[there], stat_recv.at[rows], member(there))

    def stat_start():
        for step in (1, 2, 3):
            stat_copy(me, me ^ step).start()

    def stat_finish():
        for step in (1, 2, 3):
            stat_copy(me ^ step, me ^ step).wait_recv()
            stat_copy(me, me ^ step).wait_send()


    def q_home(i):
        return q_slots.at[i], home_ref.at[0, pl.ds(pl.multiple_of(seat * CHUNK, CHUNK), CHUNK), :]

    def kv_home(half, i):
        count = CHUNK // 2
        return (
            kv_slots.at[:, i, pl.ds(pl.multiple_of(half * count, count), count), :],
            home_ref.at[1:3, pl.ds(pl.multiple_of(seat * CHUNK + half * count, count), count), :],
        )

    def send_home(copies, sem):
        def start(n, _):
            i = (n + s) & (SEQ - 1)
            src, dst = copies(i)

            @pl.when(jnp.logical_not(to_self(i)))
            def _():
                remote(src, dst, home_send.at[sem], home_recv.at[sem], source(i)).start()

            return 0

        lax.fori_loop(0, SEQ, start, 0)

        @pl.when(same)
        def _():
            src, dst = copies(s)
            pltpu.make_async_copy(src, dst, home_recv.at[sem]).start()


    def stat_row(i, cols):
        units = range(cols.start // SHARE, cols.stop // SHARE)
        return jnp.concatenate([stats[u // UNITS, i, u % UNITS : u % UNITS + 1, :] for u in units], axis=1)

    def key_tile(t, _):
        key, value = tile_rows(0, t), tile_rows(2, t)
        key_grad = jnp.zeros((TILE, HD), jnp.float32)
        value_grad = jnp.zeros((TILE, HD), jnp.float32)
        for cols in chunks:
            query, grad = head_rows(1, cols), head_rows(3, cols)
            scores = lax.dot_general(key, query, NT, preferred_element_type=jnp.float32)
            weights = jnp.exp2(scores * (SCALING * LOG2E) - stat_row(0, cols))
            dots = lax.dot_general(value, grad, NT, preferred_element_type=jnp.float32)
            dscore = weights * (dots - stat_row(1, cols))
            key_grad += jnp.dot(dscore.astype(jnp.bfloat16), query, preferred_element_type=jnp.float32)
            value_grad += jnp.dot(weights.astype(jnp.bfloat16), grad, preferred_element_type=jnp.float32)
        grads, term = norm_grads(raw[0, local_rows(t), :], gain_k_ref[...], key_grad * SCALING)
        terms[8:16, :] += term
        for i, result in enumerate((grads, value_grad)):
            kv_slots[i, :, pl.ds(pl.multiple_of(t * 2 * SLOTS, 16), 2 * SLOTS), :] = spread_tile(t, result)

        @pl.when((t & 1) == 1)
        def _():
            send_home(lambda i: kv_home(t >> 1, i), 1)

        return 0


    def part_start(i, _):
        @pl.when(jnp.logical_not(to_self(i)))
        def _():
            remote(terms, parts.at[seat], part_sem.at[0], part_sem.at[1], source(i)).start()

        return 0

    @pl.when(active)
    def _():
        build_pick()
        to_dense(0)
        gather_start(0)

    route(2)

    @pl.when(active)
    def _():
        to_dense(1)
        gather_pass(0)

    route(3)

    @pl.when(active)
    def _():
        terms[...] = jnp.zeros_like(terms)
        gather_finish(0)
        lax.fori_loop(0, TILES, score_tile, 0)
        gather_pass(2)
        to_dense(3)
        gather_start(3)
        gather_finish(2)
        lax.fori_loop(0, TILES, query_tile, 0)
        stat_start()
        send_home(q_home, 0)
        gather_finish(1)
        gather_finish(3)
        stat_finish()
        lax.fori_loop(0, TILES, key_tile, 0)
        lax.fori_loop(0, SEQ, part_start, 0)

        @pl.when(same)
        def _():
            pltpu.make_async_copy(terms, parts.at[seat], part_sem.at[1]).start()

    remote(parts, parts, part_sem.at[0], part_sem.at[1], sibling).wait_recv()
    partial[...] = jnp.sum(parts[...], axis=0)

    def cross_copy(i, dst):
        return remote(partial, cross.at[dst], cross_send.at[i], cross_recv.at[dst], (i >> 2, s, i & 3))

    def cross_start(i, _):
        @pl.when(i != corner)
        def _():
            cross_copy(i, corner).start()

        return 0

    def cross_finish(i, _):
        @pl.when(i != corner)
        def _():
            cross_copy(i, i).wait_recv()
            cross_copy(i, corner).wait_send()

        return 0

    cross[pl.ds(corner, 1)] = partial[...][None]
    lax.fori_loop(0, 8, cross_start, 0)
    lax.fori_loop(0, 8, cross_finish, 0)
    total_ref[...] = jnp.sum(cross[...], axis=0)


    def sent(targets, sources):
        for a in range(4):
            rows = slots.at[a, 0 : targets * CHUNK, :]
            remote(rows, rows, route_send.at[a], route_recv.at[a], sibling).wait_send()
        if sources:
            for a in range(4):
                gather_sent(a)
            rows = q_slots.at[0:sources]
            remote(rows, rows, home_send.at[0], home_recv.at[0], sibling).wait_send()
            rows = kv_slots.at[:, 0:sources]
            remote(rows, rows, home_send.at[1], home_recv.at[1], sibling).wait_send()
            rows = part_bytes.at[0:sources]
            remote(rows, rows, part_sem.at[0], part_sem.at[1], sibling).wait_send()

    @pl.when(same)
    def _():
        sent(TARGETS - 1, SEQ - 1)

    @pl.when(active & jnp.logical_not(same))
    def _():
        sent(TARGETS, SEQ)

    @pl.when(jnp.logical_not(active))
    def _():
        sent(TARGETS, 0)

    remote(home_ref.at[0], home_ref.at[0], home_send.at[0], home_recv.at[0], sibling).wait_recv()
    remote(home_ref.at[1:3], home_ref.at[1:3], home_send.at[1], home_recv.at[1], sibling).wait_recv()


def core(listing, k, q, v, g, gain_q, gain_k):
    bf16, f32 = jnp.bfloat16, jnp.float32
    dma = pltpu.SemaphoreType.DMA
    in_vmem = pl.BlockSpec(memory_space=pltpu.VMEM)
    return pl.pallas_call(
        core_kernel,
        name="core",
        in_specs=[in_vmem] * 7,
        out_specs=[pl.BlockSpec(memory_space=pl.ANY), in_vmem, in_vmem],
        out_shape=(
            jax.ShapeDtypeStruct((3, OUT, HD), bf16),
            jax.ShapeDtypeStruct((SPAN, SPAN), bf16),
            jax.ShapeDtypeStruct((16, HD), f32),
        ),
        scratch_shapes=[
            pltpu.VMEM((4, OUT, HD), bf16),
            pltpu.VMEM((4, FLAT, HD), bf16),
            pltpu.VMEM((SEQ, SHARE), jnp.int32),
            pltpu.VMEM((SEQ, SHARE), jnp.int32),
            pltpu.VMEM((SEQ, SHARE), jnp.int32),
            pltpu.VMEM((ROWS, FLAT), bf16),
            pltpu.VMEM((4, KEPT, HD), bf16),
            pltpu.VMEM((2, ROWS, HD), bf16),
            pltpu.VMEM((ROWS, KEPT), f32),
            pltpu.VMEM((TILE, KEPT), f32),
            pltpu.VMEM((ROWS, 128), f32),
            pltpu.VMEM((SEQ, CHUNK, HD), bf16),
            pltpu.VMEM((2, SEQ, CHUNK, HD), bf16),
            pltpu.VMEM((MEMBERS, 2, 8, SHARE), f32),
            pltpu.VMEM((16, HD), f32),
            pltpu.VMEM((SEQ, 16, HD), f32),
            pltpu.VMEM((TARGETS, 16, HD), f32),
            pltpu.VMEM((16, HD), f32),
            pltpu.VMEM((8, 16, HD), f32),
            dma((2,)),
            dma((4,)),
            dma((4,)),
            dma((4, 3)),
            dma((4, 3)),
            dma((MEMBERS,)),
            dma((MEMBERS,)),
            dma((2,)),
            dma((2,)),
            dma((2,)),
            dma((8,)),
            dma((8,)),
        ],
        compiler_params=pltpu.CompilerParams(
            collective_id=0, has_side_effects=True, vmem_limit_bytes=VMEM_LIMIT
        ),
    )(listing, k, q, v, g, gain_q, gain_k)


def rows_kernel(back_ref, slots_ref, total_ref, q_ref, k_ref, v_ref, gain_q_ref, gain_k_ref):
    for i, ref in enumerate((q_ref, k_ref, v_ref)):
        for h in range(slots_ref.shape[1] // SPAN):
            rows = slots_ref[i, h * SPAN : (h + 1) * SPAN, :]
            rows = jnp.dot(back_ref[...], rows, preferred_element_type=jnp.float32)
            ref[0, :, h * HD : (h + 1) * HD] = rows.astype(jnp.bfloat16)
    gain_q_ref[...] = jnp.sum(total_ref[0:8, :], axis=0, keepdims=True)
    gain_k_ref[...] = jnp.sum(total_ref[8:16, :], axis=0, keepdims=True)


def to_rows(back, slots, total):
    width = HEAD_PART * HD
    parts = 2
    big = jax.ShapeDtypeStruct((1, SPAN, width), jnp.bfloat16)
    small = jax.ShapeDtypeStruct((1, HD), jnp.float32)
    return pl.pallas_call(
        rows_kernel,
        name="to_rows",
        grid=(parts,),
        in_specs=[
            pl.BlockSpec((SPAN, SPAN), lambda h: (0, 0)),
            pl.BlockSpec((3, OUT // parts, HD), lambda h: (0, h, 0)),
            pl.BlockSpec((16, HD), lambda h: (0, 0)),
        ],
        out_specs=[pl.BlockSpec((1, SPAN, width // parts), lambda h: (0, 0, h))] * 3
        + [pl.BlockSpec((1, HD), lambda h: (0, 0))] * 2,
        out_shape=(big, big, big, small, small),
        compiler_params=pltpu.CompilerParams(vmem_limit_bytes=VMEM_LIMIT),
        cost_estimate=pl.CostEstimate(flops=3 * 10**8, bytes_accessed=3 * 10**6, transcendentals=0),
    )(back, slots, total)


def on_device(q_raw, k_raw, v_raw, out_grad, gain_q, gain_k, keep_list):
    home, back, total = core(
        keep_list.reshape(SEQ, SHARE),
        k_raw[0],
        q_raw[0],
        v_raw[0],
        out_grad[0],
        gain_q.reshape(1, HD),
        gain_k.reshape(1, HD),
    )
    q_out, k_out, v_out, gain_q_grad, gain_k_grad = to_rows(back, home, total)
    return q_out, k_out, v_out, gain_q_grad.reshape(HD), gain_k_grad.reshape(HD)


def solution(mesh):
    big = P("dp", "seq", "tensor")
    return jax.shard_map(
        on_device,
        mesh=mesh,
        in_specs=(big, big, big, big, P(), P(), P("dp", None)),
        out_specs=(big, big, big, P(), P()),
        check_vma=False,
    )
```

```python
import math

import jax
import jax.numpy as jnp
from jax import lax
from jax.experimental import pallas as pl
from jax.experimental.pallas import tpu as pltpu
from jax.sharding import PartitionSpec as P

MESH = pl.DeviceIdType.MESH
HD = 128
EPSILON = 1e-06
SEQ = 32
SPAN = 256
SHARE = 128
SLOTS = 8
HEAD_PART = 6
UNITS = 8
ROWS = UNITS * SHARE
CHUNK = UNITS * SLOTS
MEMBERS = 4
TARGETS = HEAD_PART * MEMBERS
OUT = TARGETS * CHUNK
FLAT = SEQ * CHUNK
KEPT = SEQ * SHARE
TILE = 256
TILES = ROWS // TILE
PIECE = 128
SCALING = 1.0 / math.sqrt(HD)
LOG2E = 1.4426950408889634
VMEM_LIMIT = 56 * 1024 * 1024

NT = (((1,), (1,)), ((), ()))

def place(x, clip, i):
    head, quarter = i >> 2, i & 3
    third = (head * 11) >> 5
    pair = head - 3 * third
    y = 2 * (x & 1) + (pair & 1)
    z = 4 * clip + 2 * third + (pair >> 1)
    return quarter & 1, y * 8 + z, (x & 2) + (quarter >> 1)


def my_place(dp, s, x):
    y, z = s >> 3, s & 7
    third, pair = (z >> 1) & 1, (y & 1) + 2 * (z & 1)
    return (x & 2) + (y >> 1), z >> 2, (3 * third + pair) * 4 + 2 * (x & 1) + dp, pair < 3


def one_hot(hit):
    return jnp.where(hit, 1.0, 0.0).astype(jnp.bfloat16)


def inverse_norm(x):
    return lax.rsqrt(jnp.mean(x * x, axis=-1, keepdims=True) + EPSILON)


def norm_grads(raw, gain, upstream):
    raw = raw.astype(jnp.float32)
    inverse = inverse_norm(raw)
    scaled = upstream * gain
    inner = jnp.mean(scaled * raw, axis=-1, keepdims=True)
    grads = inverse * scaled - raw * (inverse * inverse * inverse * inner)
    terms = upstream * raw * inverse
    return grads, jnp.sum(terms.reshape(-1, 8, HD), axis=0)


def lane_fold(x, fold):
    parts = [x[:, i * 128 : (i + 1) * 128] for i in range(x.shape[1] // 128)]
    total = parts[0]
    for part in parts[1:]:
        total = fold(total, part)
    return total


def core_kernel(
    list_ref,
    k_ref,
    q_ref,
    v_ref,
    g_ref,
    gain_q_ref,
    gain_k_ref,
    home_ref,
    back_ref,
    total_ref,
    slots,
    arrived,
    enc_ref,
    other,
    codes,
    pick,
    full,
    raw,
    scores_ref,
    dots_ref,
    sums,
    q_slots,
    kv_slots,
    stats,
    terms,
    part_bytes,
    parts,
    partial,
    cross,
    enc_sem,
    route_send,
    route_recv,
    near_send,
    near_recv,
    stat_send,
    stat_recv,
    home_send,
    home_recv,
    part_sem,
    cross_send,
    cross_recv,
):
    dp, s, x = lax.axis_index("dp"), lax.axis_index("seq"), lax.axis_index("tensor")
    head_x, clip, seat, active = my_place(dp, s, x)
    me = seat & 3
    sibling = (1 - dp, s, x)
    corner = dp * 4 + x
    same = active & (clip == dp) & (head_x == x)
    own_source = jnp.where(same, s, -1)
    own_target = jnp.where(same, seat, -1)

    def to_self(i):
        return i == own_source

    def target(i):
        return place(x, dp, i), i == own_target

    def source(i):
        return (clip, i, head_x)

    def member(i):
        return (i & 1, s, (x & 2) + (i >> 1))

    def remote(src, dst, send_sem, recv_sem, device):
        return pltpu.make_async_remote_copy(
            src_ref=src, dst_ref=dst, send_sem=send_sem, recv_sem=recv_sem, device_id=device, device_id_type=MESH
        )


    barrier = pltpu.get_barrier_semaphore()

    def greet_device(there):
        pl.semaphore_signal(barrier, inc=1, device_id=there, device_id_type=MESH)

    def greet_target(i, _):
        there, own = target(i)

        @pl.when(jnp.logical_not(own))
        def _():
            greet_device(there)

        return 0

    def greet_source(i, _):
        @pl.when(jnp.logical_not(to_self(i)))
        def _():
            greet_device(source(i))

        return 0

    def greet_corner(i, _):
        @pl.when(i != corner)
        def _():
            greet_device((i >> 2, s, i & 3))

        return 0

    @pl.when(active)
    def _():
        lax.fori_loop(0, SEQ, greet_source, 0)
        for step in (1, 2, 3):
            greet_device(member(me ^ step))

    lax.fori_loop(0, TARGETS, greet_target, 0)
    lax.fori_loop(0, 8, greet_corner, 0)


    listing = list_ref[...]
    from_block = listing >> 8
    hits = one_hot(jnp.concatenate([from_block == i for i in range(SEQ)], axis=0))
    earlier = lax.broadcasted_iota(jnp.int32, (SHARE, SHARE), 0) < lax.broadcasted_iota(jnp.int32, (SHARE, SHARE), 1)
    counts = jnp.dot(hits, one_hot(earlier), preferred_element_type=jnp.float32) * hits.astype(jnp.float32)
    rank = counts[0:SEQ]
    for i in range(1, SEQ):
        rank += counts[i * SEQ : (i + 1) * SEQ]
    rank = rank.astype(jnp.int32)
    enc_ref[...] = from_block * SLOTS + rank
    slot = lax.broadcasted_iota(jnp.int32, (SEQ, SHARE), 0) * SLOTS + rank
    slot = jnp.where(from_block == s, slot, -1)
    token = listing - s * SPAN

    def lanes(x, c):
        return jnp.concatenate([x[j : j + 1] for j in range(c * step // SHARE, (c + 1) * step // SHARE)], axis=1)

    step = 512
    iota = lax.broadcasted_iota(jnp.int32, (SPAN, step), 0)
    take = jnp.zeros((SPAN, SPAN), jnp.float32)
    back = jnp.zeros((SPAN, SPAN), jnp.float32)
    for c in range(KEPT // step):
        a = one_hot(iota == lanes(slot, c))
        b = one_hot(iota == lanes(token, c))
        take += lax.dot_general(a, b, NT, preferred_element_type=jnp.float32)
        back += lax.dot_general(b, a, NT, preferred_element_type=jnp.float32)
    take = take.astype(jnp.bfloat16)
    back_ref[...] = back.astype(jnp.bfloat16)

    def to_slots(i, ref):
        rows = jnp.dot(take, ref[...], preferred_element_type=jnp.float32).astype(jnp.bfloat16)
        for h in range(HEAD_PART):
            slots[i, h * SPAN : (h + 1) * SPAN, :] = rows[:, h * HD : (h + 1) * HD]

    def chunk(ref, a, i):
        return ref.at[a, pl.ds(pl.multiple_of(i * CHUNK, 16), CHUNK), :]

    turn = (3 * s) >> 2

    def route(a, first, last, beside=None):
        def start(n, _):
            if beside is not None:

                @pl.when(n < first + ROWS // PIECE)
                def _():
                    @pl.when(active)
                    def _():
                        piece(beside, n - first).start()

            i = n + turn
            i = jnp.where(i < TARGETS, i, i - TARGETS)
            there, own = target(i)

            @pl.when(jnp.logical_not(own))
            def _():
                remote(chunk(slots, a, i), chunk(arrived, a, s), route_send.at[a], route_recv.at[a], there).start()

            return 0

        lax.fori_loop(first, last, start, 0)

        if last == TARGETS:

            @pl.when(same)
            def _():
                pltpu.make_async_copy(chunk(slots, a, seat), chunk(arrived, a, s), route_recv.at[a]).start()

    def rows_of(a, i):
        return full.at[a, pl.ds(pl.multiple_of(i * ROWS, ROWS), ROWS), :]

    def piece(a, n):
        rows = full.at[a, pl.ds(pl.multiple_of(me * ROWS + n * PIECE, PIECE), PIECE), :]
        return remote(rows, rows, near_send.at[a, 0], near_recv.at[a, 0], member(me ^ 2))

    to_slots(0, k_ref)
    arrivals = jnp.where(active, SEQ + 3, 0) - jnp.where(same, 2, 0)
    pl.semaphore_wait(barrier, TARGETS + 7 + arrivals)
    exchange = remote(enc_ref, other, enc_sem.at[0], enc_sem.at[1], sibling)

    @pl.when(active)
    def _():
        exchange.start()

    route(0, 0, TARGETS)
    to_slots(1, q_ref)
    route(1, 0, TARGETS)
    to_slots(2, v_ref)
    to_slots(3, g_ref)


    def unit_codes(u):
        return codes[pl.ds(UNITS * me + u, 1), :]

    def build_pick():
        exchange.wait()
        codes[...] = jnp.where(clip == dp, enc_ref[...], other[...])
        wide_iota = lax.broadcasted_iota(jnp.int32, (SHARE, 128), 1).astype(jnp.float32)
        for u in range(UNITS):
            code = unit_codes(u)
            code = (code >> 3) * CHUNK + u * SLOTS + (code & 7)
            wide = jnp.broadcast_to(code.astype(jnp.float32), (SHARE, 128)).T
            for c in range(FLAT // 128):
                pick[u * SHARE : (u + 1) * SHARE, c * 128 : (c + 1) * 128] = one_hot(wide == wide_iota + c * 128.0)


    def near(a, way, rows, there):
        return remote(rows_of(a, rows), rows_of(a, rows), near_send.at[a, way], near_recv.at[a, way], member(there))

    def gather_rest():
        def start(n, _):
            piece(3, n).start()
            return 0

        lax.fori_loop(0, ROWS // PIECE, start, 0)

    def gather_pass(a):
        near(a, 0, me ^ 2, me).wait_recv()
        near(a, 2, me ^ 2, me ^ 1).start()

    def gather_finish(a):
        near(a, 1, me ^ 1, me).wait_recv()
        near(a, 2, me ^ 3, me).wait_recv()

    def gather_sent(a):
        near(a, 0, me, me ^ 2).wait_send()
        near(a, 1, me, me ^ 1).wait_send()
        near(a, 2, me ^ 2, me ^ 1).wait_send()

    own_rows = pl.ds(pl.multiple_of(me * ROWS, 256), ROWS)

    def to_dense(a):
        remote(arrived.at[a], arrived.at[a], route_send.at[a], route_recv.at[a], sibling).wait_recv()
        rows = jnp.dot(pick[...], arrived[a], preferred_element_type=jnp.float32)
        if a < 2:
            raw[a] = rows.astype(jnp.bfloat16)
            gain = (gain_k_ref, gain_q_ref)[a][...]
            rows = rows * inverse_norm(rows) * gain
        full[a, own_rows, :] = rows.astype(jnp.bfloat16)
        near(a, 1, me, me ^ 1).start()


    chunks = [slice(i * step, (i + 1) * step) for i in range(KEPT // step)]

    def head_rows(a, cols):
        return full[a, cols, :]

    def tile_rows(a, t):
        return full[a, pl.ds(pl.multiple_of(me * ROWS + t * TILE, TILE), TILE), :]

    def local_rows(t):
        return pl.ds(pl.multiple_of(t * TILE, TILE), TILE)

    def store_stat(i, t, value):
        wide = jnp.broadcast_to(value, (TILE, 128)).T
        for j in range(TILE // SHARE):
            stats[me, i, pl.ds(2 * t + j, 1), :] = wide[0:1, j * SHARE : (j + 1) * SHARE]

    def score_tile(t, _):
        query = tile_rows(1, t)
        rows = local_rows(t)
        top = None
        for cols in chunks:
            scores = lax.dot_general(query, head_rows(0, cols), NT, preferred_element_type=jnp.float32)
            scores = scores * (SCALING * LOG2E)
            scores_ref[rows, cols] = scores
            part = lane_fold(scores, jnp.maximum)
            top = part if top is None else jnp.maximum(top, part)
        top = jnp.max(top, axis=-1, keepdims=True)
        total = jnp.zeros((TILE, 128), jnp.float32)
        for cols in chunks:
            weights = jnp.exp2(scores_ref[rows, cols] - top)
            scores_ref[rows, cols] = weights
            total += lane_fold(weights, jnp.add)
        total = jnp.sum(total, axis=-1, keepdims=True)
        sums[rows, :] = jnp.broadcast_to(total, (TILE, 128))
        store_stat(0, t, top + jnp.log2(total))

        return 0

    def spread_tile(t, rows):
        tile_iota = lax.broadcasted_iota(jnp.int32, (2 * SLOTS * SEQ, TILE), 0)
        tile_codes = []
        for j in range(2):
            code = unit_codes(2 * t + j)
            tile_codes.append((code >> 3) * (2 * SLOTS) + j * SLOTS + (code & 7))
        spread = one_hot(tile_iota == jnp.concatenate(tile_codes, axis=1))
        rows = jnp.dot(spread, rows.astype(jnp.bfloat16), preferred_element_type=jnp.float32)
        return rows.astype(jnp.bfloat16).reshape(SEQ, 2 * SLOTS, HD)

    def query_tile(t, _):
        grad = tile_rows(3, t)
        rows = local_rows(t)
        weighted = jnp.zeros((TILE, 128), jnp.float32)
        for cols in chunks:
            dots = lax.dot_general(grad, head_rows(2, cols), NT, preferred_element_type=jnp.float32)
            dots_ref[:, cols] = dots
            weighted += lane_fold(scores_ref[rows, cols] * dots, jnp.add)
        share = 1.0 / sums[rows, 0:1]
        delta = jnp.sum(weighted, axis=-1, keepdims=True) * share
        result = jnp.zeros((TILE, HD), jnp.float32)
        for cols in chunks:
            dscore = (scores_ref[rows, cols] * share) * (dots_ref[:, cols] - delta)
            result += jnp.dot(dscore.astype(jnp.bfloat16), head_rows(0, cols), preferred_element_type=jnp.float32)
        grads, term = norm_grads(raw[1, rows, :], gain_q_ref[...], result * SCALING)
        terms[0:8, :] += term
        store_stat(1, t, delta)

        q_slots[:, pl.ds(pl.multiple_of(t * 2 * SLOTS, 16), 2 * SLOTS), :] = spread_tile(t, grads)

        @pl.when((t & 1) == 1)
        def _():
            send_home(lambda i: q_home(t >> 1, i), 0)

        return 0


    def stat_copy(rows, there):
        return remote(stats.at[rows], stats.at[rows], stat_send.at[there], stat_recv.at[rows], member(there))

    def stat_start():
        for step in (1, 2, 3):
            stat_copy(me, me ^ step).start()

    def stat_finish():
        for step in (1, 2, 3):
            stat_copy(me ^ step, me ^ step).wait_recv()
            stat_copy(me, me ^ step).wait_send()


    def q_home(half, i):
        count = CHUNK // 2
        return (
            q_slots.at[i, pl.ds(pl.multiple_of(half * count, count), count), :],
            home_ref.at[0, pl.ds(pl.multiple_of(seat * CHUNK + half * count, count), count), :],
        )

    def kv_home(half, i):
        count = CHUNK // 2
        return (
            kv_slots.at[:, i, pl.ds(pl.multiple_of(half * count, count), count), :],
            home_ref.at[1:3, pl.ds(pl.multiple_of(seat * CHUNK + half * count, count), count), :],
        )

    def send_home(copies, sem):
        def start(n, _):
            i = (n + s) & (SEQ - 1)
            src, dst = copies(i)

            @pl.when(jnp.logical_not(to_self(i)))
            def _():
                remote(src, dst, home_send.at[sem], home_recv.at[sem], source(i)).start()

            return 0

        lax.fori_loop(0, SEQ, start, 0)

        @pl.when(same)
        def _():
            src, dst = copies(s)
            pltpu.make_async_copy(src, dst, home_recv.at[sem]).start()


    def stat_row(i, cols):
        units = range(cols.start // SHARE, cols.stop // SHARE)
        return jnp.concatenate([stats[u // UNITS, i, u % UNITS : u % UNITS + 1, :] for u in units], axis=1)

    def key_tile(t, _):
        key, value = tile_rows(0, t), tile_rows(2, t)
        key_grad = jnp.zeros((TILE, HD), jnp.float32)
        value_grad = jnp.zeros((TILE, HD), jnp.float32)
        for cols in chunks:
            query, grad = head_rows(1, cols), head_rows(3, cols)
            scores = lax.dot_general(key, query, NT, preferred_element_type=jnp.float32)
            weights = jnp.exp2(scores * (SCALING * LOG2E) - stat_row(0, cols))
            dots = lax.dot_general(value, grad, NT, preferred_element_type=jnp.float32)
            dscore = weights * (dots - stat_row(1, cols))
            key_grad += jnp.dot(dscore.astype(jnp.bfloat16), query, preferred_element_type=jnp.float32)
            value_grad += jnp.dot(weights.astype(jnp.bfloat16), grad, preferred_element_type=jnp.float32)
        grads, term = norm_grads(raw[0, local_rows(t), :], gain_k_ref[...], key_grad * SCALING)
        terms[8:16, :] += term
        for i, result in enumerate((grads, value_grad)):
            kv_slots[i, :, pl.ds(pl.multiple_of(t * 2 * SLOTS, 16), 2 * SLOTS), :] = spread_tile(t, result)

        @pl.when((t & 1) == 1)
        def _():
            send_home(lambda i: kv_home(t >> 1, i), 1)

        return 0


    def part_start(i, _):
        @pl.when(jnp.logical_not(to_self(i)))
        def _():
            remote(terms, parts.at[seat], part_sem.at[0], part_sem.at[1], source(i)).start()

        return 0

    @pl.when(active)
    def _():
        build_pick()
        to_dense(0)

    route(2, 0, TARGETS, beside=0)

    @pl.when(active)
    def _():
        to_dense(1)

    route(3, 0, TARGETS // 2, beside=1)

    @pl.when(active)
    def _():
        terms[...] = jnp.zeros_like(terms)
        gather_pass(0)
        gather_finish(0)
        lax.fori_loop(0, TILES // 2, score_tile, 0)
        to_dense(2)

    route(3, TARGETS // 2, TARGETS, beside=2)

    @pl.when(active)
    def _():
        gather_pass(1)
        lax.fori_loop(TILES // 2, TILES, score_tile, 0)
        gather_pass(2)
        to_dense(3)
        gather_rest()
        gather_finish(2)
        lax.fori_loop(0, TILES, query_tile, 0)
        stat_start()
        gather_pass(3)
        gather_finish(1)
        gather_finish(3)
        stat_finish()
        lax.fori_loop(0, TILES, key_tile, 0)
        lax.fori_loop(0, SEQ, part_start, 0)

        @pl.when(same)
        def _():
            pltpu.make_async_copy(terms, parts.at[seat], part_sem.at[1]).start()

    remote(parts, parts, part_sem.at[0], part_sem.at[1], sibling).wait_recv()
    partial[...] = jnp.sum(parts[...], axis=0)

    def cross_copy(i, dst):
        return remote(partial, cross.at[dst], cross_send.at[i], cross_recv.at[dst], (i >> 2, s, i & 3))

    def cross_start(i, _):
        @pl.when(i != corner)
        def _():
            cross_copy(i, corner).start()

        return 0

    def cross_finish(i, _):
        @pl.when(i != corner)
        def _():
            cross_copy(i, i).wait_recv()
            cross_copy(i, corner).wait_send()

        return 0

    cross[pl.ds(corner, 1)] = partial[...][None]
    lax.fori_loop(0, 8, cross_start, 0)
    lax.fori_loop(0, 8, cross_finish, 0)
    total_ref[...] = jnp.sum(cross[...], axis=0)


    def sent(targets, sources):
        for a in range(4):
            rows = slots.at[a, 0 : targets * CHUNK, :]
            remote(rows, rows, route_send.at[a], route_recv.at[a], sibling).wait_send()
        if sources:
            for a in range(4):
                gather_sent(a)
            rows = q_slots.at[0:sources]
            remote(rows, rows, home_send.at[0], home_recv.at[0], sibling).wait_send()
            rows = kv_slots.at[:, 0:sources]
            remote(rows, rows, home_send.at[1], home_recv.at[1], sibling).wait_send()
            rows = part_bytes.at[0:sources]
            remote(rows, rows, part_sem.at[0], part_sem.at[1], sibling).wait_send()

    @pl.when(same)
    def _():
        sent(TARGETS - 1, SEQ - 1)

    @pl.when(active & jnp.logical_not(same))
    def _():
        sent(TARGETS, SEQ)

    @pl.when(jnp.logical_not(active))
    def _():
        sent(TARGETS, 0)

    remote(home_ref.at[0], home_ref.at[0], home_send.at[0], home_recv.at[0], sibling).wait_recv()
    remote(home_ref.at[1:3], home_ref.at[1:3], home_send.at[1], home_recv.at[1], sibling).wait_recv()


def core(listing, k, q, v, g, gain_q, gain_k):
    bf16, f32 = jnp.bfloat16, jnp.float32
    dma = pltpu.SemaphoreType.DMA
    in_vmem = pl.BlockSpec(memory_space=pltpu.VMEM)
    return pl.pallas_call(
        core_kernel,
        name="core",
        in_specs=[in_vmem] * 7,
        out_specs=[pl.BlockSpec(memory_space=pl.ANY), in_vmem, in_vmem],
        out_shape=(
            jax.ShapeDtypeStruct((3, OUT, HD), bf16),
            jax.ShapeDtypeStruct((SPAN, SPAN), bf16),
            jax.ShapeDtypeStruct((16, HD), f32),
        ),
        scratch_shapes=[
            pltpu.VMEM((4, OUT, HD), bf16),
            pltpu.VMEM((4, FLAT, HD), bf16),
            pltpu.VMEM((SEQ, SHARE), jnp.int32),
            pltpu.VMEM((SEQ, SHARE), jnp.int32),
            pltpu.VMEM((SEQ, SHARE), jnp.int32),
            pltpu.VMEM((ROWS, FLAT), bf16),
            pltpu.VMEM((4, KEPT, HD), bf16),
            pltpu.VMEM((2, ROWS, HD), bf16),
            pltpu.VMEM((ROWS, KEPT), f32),
            pltpu.VMEM((TILE, KEPT), f32),
            pltpu.VMEM((ROWS, 128), f32),
            pltpu.VMEM((SEQ, CHUNK, HD), bf16),
            pltpu.VMEM((2, SEQ, CHUNK, HD), bf16),
            pltpu.VMEM((MEMBERS, 2, 8, SHARE), f32),
            pltpu.VMEM((16, HD), f32),
            pltpu.VMEM((SEQ, 16, HD), f32),
            pltpu.VMEM((TARGETS, 16, HD), f32),
            pltpu.VMEM((16, HD), f32),
            pltpu.VMEM((8, 16, HD), f32),
            dma((2,)),
            dma((4,)),
            dma((4,)),
            dma((4, 3)),
            dma((4, 3)),
            dma((MEMBERS,)),
            dma((MEMBERS,)),
            dma((2,)),
            dma((2,)),
            dma((2,)),
            dma((8,)),
            dma((8,)),
        ],
        compiler_params=pltpu.CompilerParams(
            collective_id=0, has_side_effects=True, vmem_limit_bytes=VMEM_LIMIT
        ),
    )(listing, k, q, v, g, gain_q, gain_k)


def rows_kernel(back_ref, slots_ref, total_ref, q_ref, k_ref, v_ref, gain_q_ref, gain_k_ref):
    for i, ref in enumerate((q_ref, k_ref, v_ref)):
        for h in range(slots_ref.shape[1] // SPAN):
            rows = slots_ref[i, h * SPAN : (h + 1) * SPAN, :]
            rows = jnp.dot(back_ref[...], rows, preferred_element_type=jnp.float32)
            ref[0, :, h * HD : (h + 1) * HD] = rows.astype(jnp.bfloat16)
    gain_q_ref[...] = jnp.sum(total_ref[0:8, :], axis=0, keepdims=True)
    gain_k_ref[...] = jnp.sum(total_ref[8:16, :], axis=0, keepdims=True)


def to_rows(back, slots, total):
    width = HEAD_PART * HD
    parts = 2
    big = jax.ShapeDtypeStruct((1, SPAN, width), jnp.bfloat16)
    small = jax.ShapeDtypeStruct((1, HD), jnp.float32)
    return pl.pallas_call(
        rows_kernel,
        name="to_rows",
        grid=(parts,),
        in_specs=[
            pl.BlockSpec((SPAN, SPAN), lambda h: (0, 0)),
            pl.BlockSpec((3, OUT // parts, HD), lambda h: (0, h, 0)),
            pl.BlockSpec((16, HD), lambda h: (0, 0)),
        ],
        out_specs=[pl.BlockSpec((1, SPAN, width // parts), lambda h: (0, 0, h))] * 3
        + [pl.BlockSpec((1, HD), lambda h: (0, 0))] * 2,
        out_shape=(big, big, big, small, small),
        compiler_params=pltpu.CompilerParams(vmem_limit_bytes=VMEM_LIMIT),
        cost_estimate=pl.CostEstimate(flops=3 * 10**8, bytes_accessed=3 * 10**6, transcendentals=0),
    )(back, slots, total)


def on_device(q_raw, k_raw, v_raw, out_grad, gain_q, gain_k, keep_list):
    home, back, total = core(
        keep_list.reshape(SEQ, SHARE),
        k_raw[0],
        q_raw[0],
        v_raw[0],
        out_grad[0],
        gain_q.reshape(1, HD),
        gain_k.reshape(1, HD),
    )
    q_out, k_out, v_out, gain_q_grad, gain_k_grad = to_rows(back, home, total)
    return q_out, k_out, v_out, gain_q_grad.reshape(HD), gain_k_grad.reshape(HD)


def solution(mesh):
    big = P("dp", "seq", "tensor")
    return jax.shard_map(
        on_device,
        mesh=mesh,
        in_specs=(big, big, big, big, P(), P(), P("dp", None)),
        out_specs=(big, big, big, P(), P()),
        check_vma=False,
    )
```

```python
import math

import jax
import jax.numpy as jnp
from jax import lax
from jax.experimental import pallas as pl
from jax.experimental.pallas import tpu as pltpu
from jax.sharding import PartitionSpec as P

MESH = pl.DeviceIdType.MESH
HD = 128
EPSILON = 1e-06
SEQ = 32
SPAN = 256
SHARE = 128
SLOTS = 8
HEAD_PART = 6
UNITS = 8
ROWS = UNITS * SHARE
CHUNK = UNITS * SLOTS
MEMBERS = 4
TARGETS = HEAD_PART * MEMBERS
OUT = TARGETS * CHUNK
FLAT = SEQ * CHUNK
KEPT = SEQ * SHARE
TILE = 256
TILES = ROWS // TILE
PIECE = 128
SCALING = 1.0 / math.sqrt(HD)
LOG2E = 1.4426950408889634
VMEM_LIMIT = 56 * 1024 * 1024

NT = (((1,), (1,)), ((), ()))

def place(clip, i):
    head, quarter = i >> 2, i & 3
    third = (head * 11) >> 5
    pair = head - 3 * third
    odd = pair >> 1
    y = 2 * ((pair & 1) + odd * third) + (quarter >> 1)
    z = 4 * clip + 2 * third + odd
    return quarter & 1, y * 8 + z


def my_place(dp, s):
    y, z = s >> 3, s & 7
    third, odd, high = (z >> 1) & 1, z & 1, y >> 1
    pair = high + odd * (2 - high)
    active = (odd == 0) | (high == third)
    return z >> 2, (3 * third + pair) * 4 + 2 * (y & 1) + dp, active


def one_hot(hit):
    return jnp.where(hit, 1.0, 0.0).astype(jnp.bfloat16)


def inverse_norm(x):
    return lax.rsqrt(jnp.mean(x * x, axis=-1, keepdims=True) + EPSILON)


def norm_grads(raw, gain, upstream):
    raw = raw.astype(jnp.float32)
    inverse = inverse_norm(raw)
    scaled = upstream * gain
    inner = jnp.mean(scaled * raw, axis=-1, keepdims=True)
    grads = inverse * scaled - raw * (inverse * inverse * inverse * inner)
    terms = upstream * raw * inverse
    return grads, jnp.sum(terms.reshape(-1, 8, HD), axis=0)


def lane_fold(x, fold):
    parts = [x[:, i * 128 : (i + 1) * 128] for i in range(x.shape[1] // 128)]
    total = parts[0]
    for part in parts[1:]:
        total = fold(total, part)
    return total


def core_kernel(
    list_ref,
    k_ref,
    q_ref,
    v_ref,
    g_ref,
    gain_q_ref,
    gain_k_ref,
    home_ref,
    back_ref,
    total_ref,
    slots,
    arrived,
    enc_ref,
    other,
    codes,
    pick,
    full,
    raw,
    scores_ref,
    dots_ref,
    sums,
    q_slots,
    kv_slots,
    stats,
    terms,
    part_bytes,
    parts,
    partial,
    cross,
    enc_sem,
    route_send,
    route_recv,
    near_send,
    near_recv,
    stat_send,
    stat_recv,
    home_send,
    home_recv,
    part_sem,
    cross_send,
    cross_recv,
):
    dp, s, x = lax.axis_index("dp"), lax.axis_index("seq"), lax.axis_index("tensor")
    clip, seat, active = my_place(dp, s)
    me = seat & 3
    sibling = (1 - dp, s, x)
    corner = dp * 4 + x
    same = active & (clip == dp)
    own_source = jnp.where(same, s, -1)
    own_target = jnp.where(same, seat, -1)

    def to_self(i):
        return i == own_source

    def target(i):
        return place(dp, i) + (x,), i == own_target

    def source(i):
        return (clip, i, x)

    def member(i):
        return (i & 1, (s & 23) + 8 * (i >> 1), x)

    def remote(src, dst, send_sem, recv_sem, device):
        return pltpu.make_async_remote_copy(
            src_ref=src, dst_ref=dst, send_sem=send_sem, recv_sem=recv_sem, device_id=device, device_id_type=MESH
        )


    barrier = pltpu.get_barrier_semaphore()

    def greet_device(there):
        pl.semaphore_signal(barrier, inc=1, device_id=there, device_id_type=MESH)

    def greet_target(i, _):
        there, own = target(i)

        @pl.when(jnp.logical_not(own))
        def _():
            greet_device(there)

        return 0

    def greet_source(i, _):
        @pl.when(jnp.logical_not(to_self(i)))
        def _():
            greet_device(source(i))

        return 0

    def greet_corner(i, _):
        @pl.when(i != corner)
        def _():
            greet_device((i >> 2, s, i & 3))

        return 0

    @pl.when(active)
    def _():
        lax.fori_loop(0, SEQ, greet_source, 0)
        for step in (1, 2, 3):
            greet_device(member(me ^ step))

    lax.fori_loop(0, TARGETS, greet_target, 0)
    lax.fori_loop(0, 8, greet_corner, 0)


    listing = list_ref[...]
    from_block = listing >> 8
    hits = one_hot(jnp.concatenate([from_block == i for i in range(SEQ)], axis=0))
    earlier = lax.broadcasted_iota(jnp.int32, (SHARE, SHARE), 0) < lax.broadcasted_iota(jnp.int32, (SHARE, SHARE), 1)
    counts = jnp.dot(hits, one_hot(earlier), preferred_element_type=jnp.float32) * hits.astype(jnp.float32)
    rank = counts[0:SEQ]
    for i in range(1, SEQ):
        rank += counts[i * SEQ : (i + 1) * SEQ]
    rank = rank.astype(jnp.int32)
    enc_ref[...] = from_block * SLOTS + rank
    slot = lax.broadcasted_iota(jnp.int32, (SEQ, SHARE), 0) * SLOTS + rank
    slot = jnp.where(from_block == s, slot, -1)
    token = listing - s * SPAN

    def lanes(x, c):
        return jnp.concatenate([x[j : j + 1] for j in range(c * step // SHARE, (c + 1) * step // SHARE)], axis=1)

    step = 512
    iota = lax.broadcasted_iota(jnp.int32, (SPAN, step), 0)
    take = jnp.zeros((SPAN, SPAN), jnp.float32)
    back = jnp.zeros((SPAN, SPAN), jnp.float32)
    for c in range(KEPT // step):
        a = one_hot(iota == lanes(slot, c))
        b = one_hot(iota == lanes(token, c))
        take += lax.dot_general(a, b, NT, preferred_element_type=jnp.float32)
        back += lax.dot_general(b, a, NT, preferred_element_type=jnp.float32)
    take = take.astype(jnp.bfloat16)
    back_ref[...] = back.astype(jnp.bfloat16)

    def to_slots(i, ref):
        rows = jnp.dot(take, ref[...], preferred_element_type=jnp.float32).astype(jnp.bfloat16)
        for h in range(HEAD_PART):
            slots[i, h * SPAN : (h + 1) * SPAN, :] = rows[:, h * HD : (h + 1) * HD]

    def chunk(ref, a, i):
        return ref.at[a, pl.ds(pl.multiple_of(i * CHUNK, 16), CHUNK), :]

    turn = (3 * s) >> 2

    def route(a, first, last, beside=None):
        def start(n, _):
            if beside is not None:

                @pl.when(n < first + ROWS // PIECE)
                def _():
                    @pl.when(active)
                    def _():
                        piece(beside, n - first).start()

            i = n + turn
            i = jnp.where(i < TARGETS, i, i - TARGETS)
            there, own = target(i)

            @pl.when(jnp.logical_not(own))
            def _():
                remote(chunk(slots, a, i), chunk(arrived, a, s), route_send.at[a], route_recv.at[a], there).start()

            return 0

        lax.fori_loop(first, last, start, 0)

        if last == TARGETS:

            @pl.when(same)
            def _():
                pltpu.make_async_copy(chunk(slots, a, seat), chunk(arrived, a, s), route_recv.at[a]).start()

    def rows_of(a, i):
        return full.at[a, pl.ds(pl.multiple_of(i * ROWS, ROWS), ROWS), :]

    def piece(a, n):
        rows = full.at[a, pl.ds(pl.multiple_of(me * ROWS + n * PIECE, PIECE), PIECE), :]
        return remote(rows, rows, near_send.at[a, 0], near_recv.at[a, 0], member(me ^ 2))

    to_slots(0, k_ref)
    arrivals = jnp.where(active, SEQ + 3, 0) - jnp.where(same, 2, 0)
    pl.semaphore_wait(barrier, TARGETS + 7 + arrivals)
    exchange = remote(enc_ref, other, enc_sem.at[0], enc_sem.at[1], sibling)

    @pl.when(active)
    def _():
        exchange.start()

    route(0, 0, TARGETS)
    to_slots(1, q_ref)
    route(1, 0, TARGETS)
    to_slots(2, v_ref)
    to_slots(3, g_ref)


    def unit_codes(u):
        return codes[pl.ds(UNITS * me + u, 1), :]

    def build_pick():
        exchange.wait()
        codes[...] = jnp.where(clip == dp, enc_ref[...], other[...])
        wide_iota = lax.broadcasted_iota(jnp.int32, (SHARE, 128), 1).astype(jnp.float32)
        for u in range(UNITS):
            code = unit_codes(u)
            code = (code >> 3) * CHUNK + u * SLOTS + (code & 7)
            wide = jnp.broadcast_to(code.astype(jnp.float32), (SHARE, 128)).T
            for c in range(FLAT // 128):
                pick[u * SHARE : (u + 1) * SHARE, c * 128 : (c + 1) * 128] = one_hot(wide == wide_iota + c * 128.0)


    def near(a, way, rows, there):
        return remote(rows_of(a, rows), rows_of(a, rows), near_send.at[a, way], near_recv.at[a, way], member(there))

    def gather_rest():
        def start(n, _):
            piece(3, n).start()
            return 0

        lax.fori_loop(0, ROWS // PIECE, start, 0)

    def gather_pass(a):
        near(a, 0, me ^ 2, me).wait_recv()
        near(a, 2, me ^ 2, me ^ 1).start()

    def gather_finish(a):
        near(a, 1, me ^ 1, me).wait_recv()
        near(a, 2, me ^ 3, me).wait_recv()

    def gather_sent(a):
        near(a, 0, me, me ^ 2).wait_send()
        near(a, 1, me, me ^ 1).wait_send()
        near(a, 2, me ^ 2, me ^ 1).wait_send()

    own_rows = pl.ds(pl.multiple_of(me * ROWS, 256), ROWS)

    def to_dense(a):
        remote(arrived.at[a], arrived.at[a], route_send.at[a], route_recv.at[a], sibling).wait_recv()
        rows = jnp.dot(pick[...], arrived[a], preferred_element_type=jnp.float32)
        if a < 2:
            raw[a] = rows.astype(jnp.bfloat16)
            gain = (gain_k_ref, gain_q_ref)[a][...]
            rows = rows * inverse_norm(rows) * gain
        full[a, own_rows, :] = rows.astype(jnp.bfloat16)
        near(a, 1, me, me ^ 1).start()


    chunks = [slice(i * step, (i + 1) * step) for i in range(KEPT // step)]

    def head_rows(a, cols):
        return full[a, cols, :]

    def tile_rows(a, t):
        return full[a, pl.ds(pl.multiple_of(me * ROWS + t * TILE, TILE), TILE), :]

    def local_rows(t):
        return pl.ds(pl.multiple_of(t * TILE, TILE), TILE)

    def store_stat(i, t, value):
        wide = jnp.broadcast_to(value, (TILE, 128)).T
        for j in range(TILE // SHARE):
            stats[me, i, pl.ds(2 * t + j, 1), :] = wide[0:1, j * SHARE : (j + 1) * SHARE]

    def score_tile(t, _):
        query = tile_rows(1, t)
        rows = local_rows(t)
        top = None
        for cols in chunks:
            scores = lax.dot_general(query, head_rows(0, cols), NT, preferred_element_type=jnp.float32)
            scores = scores * (SCALING * LOG2E)
            scores_ref[rows, cols] = scores
            part = lane_fold(scores, jnp.maximum)
            top = part if top is None else jnp.maximum(top, part)
        top = jnp.max(top, axis=-1, keepdims=True)
        total = jnp.zeros((TILE, 128), jnp.float32)
        for cols in chunks:
            weights = jnp.exp2(scores_ref[rows, cols] - top)
            scores_ref[rows, cols] = weights
            total += lane_fold(weights, jnp.add)
        total = jnp.sum(total, axis=-1, keepdims=True)
        sums[rows, :] = jnp.broadcast_to(total, (TILE, 128))
        store_stat(0, t, top + jnp.log2(total))

        return 0

    def spread_tile(t, rows):
        tile_iota = lax.broadcasted_iota(jnp.int32, (2 * SLOTS * SEQ, TILE), 0)
        tile_codes = []
        for j in range(2):
            code = unit_codes(2 * t + j)
            tile_codes.append((code >> 3) * (2 * SLOTS) + j * SLOTS + (code & 7))
        spread = one_hot(tile_iota == jnp.concatenate(tile_codes, axis=1))
        rows = jnp.dot(spread, rows.astype(jnp.bfloat16), preferred_element_type=jnp.float32)
        return rows.astype(jnp.bfloat16).reshape(SEQ, 2 * SLOTS, HD)

    def query_tile(t, _):
        grad = tile_rows(3, t)
        rows = local_rows(t)
        weighted = jnp.zeros((TILE, 128), jnp.float32)
        for cols in chunks:
            dots = lax.dot_general(grad, head_rows(2, cols), NT, preferred_element_type=jnp.float32)
            dots_ref[:, cols] = dots
            weighted += lane_fold(scores_ref[rows, cols] * dots, jnp.add)
        share = 1.0 / sums[rows, 0:1]
        delta = jnp.sum(weighted, axis=-1, keepdims=True) * share
        result = jnp.zeros((TILE, HD), jnp.float32)
        for cols in chunks:
            dscore = (scores_ref[rows, cols] * share) * (dots_ref[:, cols] - delta)
            result += jnp.dot(dscore.astype(jnp.bfloat16), head_rows(0, cols), preferred_element_type=jnp.float32)
        grads, term = norm_grads(raw[1, rows, :], gain_q_ref[...], result * SCALING)
        terms[0:8, :] += term
        store_stat(1, t, delta)

        q_slots[:, pl.ds(pl.multiple_of(t * 2 * SLOTS, 16), 2 * SLOTS), :] = spread_tile(t, grads)

        @pl.when((t & 1) == 1)
        def _():
            send_home(lambda i: q_home(t >> 1, i), 0)

        return 0


    def stat_copy(rows, there):
        return remote(stats.at[rows], stats.at[rows], stat_send.at[there], stat_recv.at[rows], member(there))

    def stat_start():
        for step in (1, 2, 3):
            stat_copy(me, me ^ step).start()

    def stat_finish():
        for step in (1, 2, 3):
            stat_copy(me ^ step, me ^ step).wait_recv()
            stat_copy(me, me ^ step).wait_send()


    def q_home(half, i):
        count = CHUNK // 2
        return (
            q_slots.at[i, pl.ds(pl.multiple_of(half * count, count), count), :],
            home_ref.at[0, pl.ds(pl.multiple_of(seat * CHUNK + half * count, count), count), :],
        )

    def kv_home(half, i):
        count = CHUNK // 2
        return (
            kv_slots.at[:, i, pl.ds(pl.multiple_of(half * count, count), count), :],
            home_ref.at[1:3, pl.ds(pl.multiple_of(seat * CHUNK + half * count, count), count), :],
        )

    def send_home(copies, sem):
        def start(n, _):
            i = (n + s) & (SEQ - 1)
            src, dst = copies(i)

            @pl.when(jnp.logical_not(to_self(i)))
            def _():
                remote(src, dst, home_send.at[sem], home_recv.at[sem], source(i)).start()

            return 0

        lax.fori_loop(0, SEQ, start, 0)

        @pl.when(same)
        def _():
            src, dst = copies(s)
            pltpu.make_async_copy(src, dst, home_recv.at[sem]).start()


    def stat_row(i, cols):
        units = range(cols.start // SHARE, cols.stop // SHARE)
        return jnp.concatenate([stats[u // UNITS, i, u % UNITS : u % UNITS + 1, :] for u in units], axis=1)

    def key_tile(t, _):
        key, value = tile_rows(0, t), tile_rows(2, t)
        key_grad = jnp.zeros((TILE, HD), jnp.float32)
        value_grad = jnp.zeros((TILE, HD), jnp.float32)
        for cols in chunks:
            query, grad = head_rows(1, cols), head_rows(3, cols)
            scores = lax.dot_general(key, query, NT, preferred_element_type=jnp.float32)
            weights = jnp.exp2(scores * (SCALING * LOG2E) - stat_row(0, cols))
            dots = lax.dot_general(value, grad, NT, preferred_element_type=jnp.float32)
            dscore = weights * (dots - stat_row(1, cols))
            key_grad += jnp.dot(dscore.astype(jnp.bfloat16), query, preferred_element_type=jnp.float32)
            value_grad += jnp.dot(weights.astype(jnp.bfloat16), grad, preferred_element_type=jnp.float32)
        grads, term = norm_grads(raw[0, local_rows(t), :], gain_k_ref[...], key_grad * SCALING)
        terms[8:16, :] += term
        for i, result in enumerate((grads, value_grad)):
            kv_slots[i, :, pl.ds(pl.multiple_of(t * 2 * SLOTS, 16), 2 * SLOTS), :] = spread_tile(t, result)

        @pl.when((t & 1) == 1)
        def _():
            send_home(lambda i: kv_home(t >> 1, i), 1)

        return 0


    def part_start(i, _):
        @pl.when(jnp.logical_not(to_self(i)))
        def _():
            remote(terms, parts.at[seat], part_sem.at[0], part_sem.at[1], source(i)).start()

        return 0

    @pl.when(active)
    def _():
        build_pick()
        to_dense(0)

    route(2, 0, TARGETS, beside=0)

    @pl.when(active)
    def _():
        to_dense(1)

    route(3, 0, TARGETS // 2, beside=1)

    @pl.when(active)
    def _():
        terms[...] = jnp.zeros_like(terms)
        gather_pass(0)
        gather_finish(0)
        lax.fori_loop(0, TILES // 2, score_tile, 0)
        to_dense(2)

    route(3, TARGETS // 2, TARGETS, beside=2)

    @pl.when(active)
    def _():
        gather_pass(1)
        lax.fori_loop(TILES // 2, TILES, score_tile, 0)
        gather_pass(2)
        to_dense(3)
        gather_rest()
        gather_finish(2)
        lax.fori_loop(0, TILES, query_tile, 0)
        stat_start()
        gather_pass(3)
        gather_finish(1)
        gather_finish(3)
        stat_finish()
        lax.fori_loop(0, TILES, key_tile, 0)
        lax.fori_loop(0, SEQ, part_start, 0)

        @pl.when(same)
        def _():
            pltpu.make_async_copy(terms, parts.at[seat], part_sem.at[1]).start()

    remote(parts, parts, part_sem.at[0], part_sem.at[1], sibling).wait_recv()
    partial[...] = jnp.sum(parts[...], axis=0)

    def cross_copy(i, dst):
        return remote(partial, cross.at[dst], cross_send.at[i], cross_recv.at[dst], (i >> 2, s, i & 3))

    def cross_start(i, _):
        @pl.when(i != corner)
        def _():
            cross_copy(i, corner).start()

        return 0

    def cross_finish(i, _):
        @pl.when(i != corner)
        def _():
            cross_copy(i, i).wait_recv()
            cross_copy(i, corner).wait_send()

        return 0

    cross[pl.ds(corner, 1)] = partial[...][None]
    lax.fori_loop(0, 8, cross_start, 0)
    lax.fori_loop(0, 8, cross_finish, 0)
    total_ref[...] = jnp.sum(cross[...], axis=0)


    def sent(targets, sources):
        for a in range(4):
            rows = slots.at[a, 0 : targets * CHUNK, :]
            remote(rows, rows, route_send.at[a], route_recv.at[a], sibling).wait_send()
        if sources:
            for a in range(4):
                gather_sent(a)
            rows = q_slots.at[0:sources]
            remote(rows, rows, home_send.at[0], home_recv.at[0], sibling).wait_send()
            rows = kv_slots.at[:, 0:sources]
            remote(rows, rows, home_send.at[1], home_recv.at[1], sibling).wait_send()
            rows = part_bytes.at[0:sources]
            remote(rows, rows, part_sem.at[0], part_sem.at[1], sibling).wait_send()

    @pl.when(same)
    def _():
        sent(TARGETS - 1, SEQ - 1)

    @pl.when(active & jnp.logical_not(same))
    def _():
        sent(TARGETS, SEQ)

    @pl.when(jnp.logical_not(active))
    def _():
        sent(TARGETS, 0)

    remote(home_ref.at[0], home_ref.at[0], home_send.at[0], home_recv.at[0], sibling).wait_recv()
    remote(home_ref.at[1:3], home_ref.at[1:3], home_send.at[1], home_recv.at[1], sibling).wait_recv()


def core(listing, k, q, v, g, gain_q, gain_k):
    bf16, f32 = jnp.bfloat16, jnp.float32
    dma = pltpu.SemaphoreType.DMA
    in_vmem = pl.BlockSpec(memory_space=pltpu.VMEM)
    return pl.pallas_call(
        core_kernel,
        name="core",
        in_specs=[in_vmem] * 7,
        out_specs=[pl.BlockSpec(memory_space=pl.ANY), in_vmem, in_vmem],
        out_shape=(
            jax.ShapeDtypeStruct((3, OUT, HD), bf16),
            jax.ShapeDtypeStruct((SPAN, SPAN), bf16),
            jax.ShapeDtypeStruct((16, HD), f32),
        ),
        scratch_shapes=[
            pltpu.VMEM((4, OUT, HD), bf16),
            pltpu.VMEM((4, FLAT, HD), bf16),
            pltpu.VMEM((SEQ, SHARE), jnp.int32),
            pltpu.VMEM((SEQ, SHARE), jnp.int32),
            pltpu.VMEM((SEQ, SHARE), jnp.int32),
            pltpu.VMEM((ROWS, FLAT), bf16),
            pltpu.VMEM((4, KEPT, HD), bf16),
            pltpu.VMEM((2, ROWS, HD), bf16),
            pltpu.VMEM((ROWS, KEPT), f32),
            pltpu.VMEM((TILE, KEPT), f32),
            pltpu.VMEM((ROWS, 128), f32),
            pltpu.VMEM((SEQ, CHUNK, HD), bf16),
            pltpu.VMEM((2, SEQ, CHUNK, HD), bf16),
            pltpu.VMEM((MEMBERS, 2, 8, SHARE), f32),
            pltpu.VMEM((16, HD), f32),
            pltpu.VMEM((SEQ, 16, HD), f32),
            pltpu.VMEM((TARGETS, 16, HD), f32),
            pltpu.VMEM((16, HD), f32),
            pltpu.VMEM((8, 16, HD), f32),
            dma((2,)),
            dma((4,)),
            dma((4,)),
            dma((4, 3)),
            dma((4, 3)),
            dma((MEMBERS,)),
            dma((MEMBERS,)),
            dma((2,)),
            dma((2,)),
            dma((2,)),
            dma((8,)),
            dma((8,)),
        ],
        compiler_params=pltpu.CompilerParams(
            collective_id=0, has_side_effects=True, vmem_limit_bytes=VMEM_LIMIT
        ),
    )(listing, k, q, v, g, gain_q, gain_k)


def rows_kernel(back_ref, slots_ref, total_ref, q_ref, k_ref, v_ref, gain_q_ref, gain_k_ref):
    for i, ref in enumerate((q_ref, k_ref, v_ref)):
        for h in range(slots_ref.shape[1] // SPAN):
            rows = slots_ref[i, h * SPAN : (h + 1) * SPAN, :]
            rows = jnp.dot(back_ref[...], rows, preferred_element_type=jnp.float32)
            ref[0, :, h * HD : (h + 1) * HD] = rows.astype(jnp.bfloat16)
    gain_q_ref[...] = jnp.sum(total_ref[0:8, :], axis=0, keepdims=True)
    gain_k_ref[...] = jnp.sum(total_ref[8:16, :], axis=0, keepdims=True)


def to_rows(back, slots, total):
    width = HEAD_PART * HD
    parts = 2
    big = jax.ShapeDtypeStruct((1, SPAN, width), jnp.bfloat16)
    small = jax.ShapeDtypeStruct((1, HD), jnp.float32)
    return pl.pallas_call(
        rows_kernel,
        name="to_rows",
        grid=(parts,),
        in_specs=[
            pl.BlockSpec((SPAN, SPAN), lambda h: (0, 0)),
            pl.BlockSpec((3, OUT // parts, HD), lambda h: (0, h, 0)),
            pl.BlockSpec((16, HD), lambda h: (0, 0)),
        ],
        out_specs=[pl.BlockSpec((1, SPAN, width // parts), lambda h: (0, 0, h))] * 3
        + [pl.BlockSpec((1, HD), lambda h: (0, 0))] * 2,
        out_shape=(big, big, big, small, small),
        compiler_params=pltpu.CompilerParams(vmem_limit_bytes=VMEM_LIMIT),
        cost_estimate=pl.CostEstimate(flops=3 * 10**8, bytes_accessed=3 * 10**6, transcendentals=0),
    )(back, slots, total)


def on_device(q_raw, k_raw, v_raw, out_grad, gain_q, gain_k, keep_list):
    home, back, total = core(
        keep_list.reshape(SEQ, SHARE),
        k_raw[0],
        q_raw[0],
        v_raw[0],
        out_grad[0],
        gain_q.reshape(1, HD),
        gain_k.reshape(1, HD),
    )
    q_out, k_out, v_out, gain_q_grad, gain_k_grad = to_rows(back, home, total)
    return q_out, k_out, v_out, gain_q_grad.reshape(HD), gain_k_grad.reshape(HD)


def solution(mesh):
    big = P("dp", "seq", "tensor")
    return jax.shard_map(
        on_device,
        mesh=mesh,
        in_specs=(big, big, big, big, P(), P(), P("dp", None)),
        out_specs=(big, big, big, P(), P()),
        check_vma=False,
    )
```

```python
import math

import jax
import jax.numpy as jnp
from jax import lax
from jax.experimental import pallas as pl
from jax.experimental.pallas import tpu as pltpu
from jax.sharding import PartitionSpec as P

MESH = pl.DeviceIdType.MESH
HD = 128
EPSILON = 1e-06
SEQ = 32
SPAN = 256
SHARE = 128
SLOTS = 8
HEAD_PART = 6
UNITS = 8
ROWS = UNITS * SHARE
CHUNK = UNITS * SLOTS
MEMBERS = 4
TARGETS = HEAD_PART * MEMBERS
OUT = TARGETS * CHUNK
FLAT = SEQ * CHUNK
KEPT = SEQ * SHARE
TILE = 512
PART = TILE // SHARE * SLOTS
TILES = ROWS // TILE
PIECE = 128
SCALING = 1.0 / math.sqrt(HD)
LOG2E = 1.4426950408889634
VMEM_LIMIT = 56 * 1024 * 1024

NT = (((1,), (1,)), ((), ()))

def place(clip, i):
    head, quarter = i >> 2, i & 3
    third = (head * 11) >> 5
    pair = head - 3 * third
    odd = pair >> 1
    y = 2 * ((pair & 1) + odd * third) + (quarter >> 1)
    z = 4 * clip + 2 * third + odd
    return quarter & 1, y * 8 + z


def my_place(dp, s):
    y, z = s >> 3, s & 7
    third, odd, high = (z >> 1) & 1, z & 1, y >> 1
    pair = high + odd * (2 - high)
    active = (odd == 0) | (high == third)
    return z >> 2, (3 * third + pair) * 4 + 2 * (y & 1) + dp, active


def one_hot(hit):
    return jnp.where(hit, 1.0, 0.0).astype(jnp.bfloat16)


def inverse_norm(x):
    return lax.rsqrt(jnp.mean(x * x, axis=-1, keepdims=True) + EPSILON)


def norm_grads(raw, gain, upstream):
    raw = raw.astype(jnp.float32)
    inverse = inverse_norm(raw)
    scaled = upstream * gain
    inner = jnp.mean(scaled * raw, axis=-1, keepdims=True)
    grads = inverse * scaled - raw * (inverse * inverse * inverse * inner)
    terms = upstream * raw * inverse
    return grads, jnp.sum(terms.reshape(-1, 8, HD), axis=0)


def lane_fold(x, fold):
    parts = [x[:, i * 128 : (i + 1) * 128] for i in range(x.shape[1] // 128)]
    total = parts[0]
    for part in parts[1:]:
        total = fold(total, part)
    return total


def core_kernel(
    list_ref,
    k_ref,
    q_ref,
    v_ref,
    g_ref,
    gain_q_ref,
    gain_k_ref,
    home_ref,
    back_ref,
    total_ref,
    slots,
    arrived,
    enc_ref,
    other,
    codes,
    pick,
    full,
    raw,
    scores_ref,
    dots_ref,
    sums,
    q_slots,
    kv_slots,
    stats,
    terms,
    part_bytes,
    parts,
    partial,
    cross,
    enc_sem,
    route_send,
    route_recv,
    near_send,
    near_recv,
    stat_send,
    stat_recv,
    home_send,
    home_recv,
    part_sem,
    cross_send,
    cross_recv,
):
    dp, s, x = lax.axis_index("dp"), lax.axis_index("seq"), lax.axis_index("tensor")
    clip, seat, active = my_place(dp, s)
    me = seat & 3
    sibling = (1 - dp, s, x)
    corner = dp * 4 + x
    same = active & (clip == dp)
    own_source = jnp.where(same, s, -1)
    own_target = jnp.where(same, seat, -1)

    def to_self(i):
        return i == own_source

    def target(i):
        return place(dp, i) + (x,), i == own_target

    def source(i):
        return (clip, i, x)

    def member(i):
        return (i & 1, (s & 23) + 8 * (i >> 1), x)

    def remote(src, dst, send_sem, recv_sem, device):
        return pltpu.make_async_remote_copy(
            src_ref=src, dst_ref=dst, send_sem=send_sem, recv_sem=recv_sem, device_id=device, device_id_type=MESH
        )


    barrier = pltpu.get_barrier_semaphore()

    def greet_device(there):
        pl.semaphore_signal(barrier, inc=1, device_id=there, device_id_type=MESH)

    def greet_target(i, _):
        there, own = target(i)

        @pl.when(jnp.logical_not(own))
        def _():
            greet_device(there)

        return 0

    def greet_source(i, _):
        @pl.when(jnp.logical_not(to_self(i)))
        def _():
            greet_device(source(i))

        return 0

    def greet_corner(i, _):
        @pl.when(i != corner)
        def _():
            greet_device((i >> 2, s, i & 3))

        return 0

    @pl.when(active)
    def _():
        lax.fori_loop(0, SEQ, greet_source, 0)
        for step in (1, 2, 3):
            greet_device(member(me ^ step))

    lax.fori_loop(0, TARGETS, greet_target, 0)
    lax.fori_loop(0, 8, greet_corner, 0)


    listing = list_ref[...]
    from_block = listing >> 8
    hits = one_hot(jnp.concatenate([from_block == i for i in range(SEQ)], axis=0))
    earlier = lax.broadcasted_iota(jnp.int32, (SHARE, SHARE), 0) < lax.broadcasted_iota(jnp.int32, (SHARE, SHARE), 1)
    counts = jnp.dot(hits, one_hot(earlier), preferred_element_type=jnp.float32) * hits.astype(jnp.float32)
    rank = counts[0:SEQ]
    for i in range(1, SEQ):
        rank += counts[i * SEQ : (i + 1) * SEQ]
    rank = rank.astype(jnp.int32)
    enc_ref[...] = from_block * SLOTS + rank
    slot = lax.broadcasted_iota(jnp.int32, (SEQ, SHARE), 0) * SLOTS + rank + 1
    slot = jnp.where(from_block == s, slot, 0).astype(jnp.float32)
    token = listing - s * SPAN
    token_iota = lax.broadcasted_iota(jnp.int32, (SPAN, SHARE), 0)
    found = jnp.zeros((SPAN, SHARE), jnp.float32)
    for j in range(SEQ):
        found += jnp.where(token_iota == token[j : j + 1], slot[j : j + 1], 0.0)
    found = jnp.sum(found, axis=1, keepdims=True) - 1.0
    row = jnp.broadcast_to(found, (SPAN, 128)).T[0:1]
    back_ref[...] = one_hot(lax.broadcasted_iota(jnp.int32, (SPAN, SPAN), 1).astype(jnp.float32) == found)
    take = one_hot(lax.broadcasted_iota(jnp.int32, (SPAN, SPAN), 0).astype(jnp.float32) == row)
    step = 512

    def to_slots(i, ref):
        rows = jnp.dot(take, ref[...], preferred_element_type=jnp.float32).astype(jnp.bfloat16)
        for h in range(HEAD_PART):
            slots[i, h * SPAN : (h + 1) * SPAN, :] = rows[:, h * HD : (h + 1) * HD]

    def chunk(ref, a, i):
        return ref.at[a, pl.ds(pl.multiple_of(i * CHUNK, 16), CHUNK), :]

    turn = (3 * s) >> 2

    def route(a, first, last, beside=None):
        def start(n, _):
            if beside is not None:

                @pl.when(n < first + ROWS // PIECE)
                def _():
                    @pl.when(active)
                    def _():
                        piece(beside, n - first).start()

            i = n + turn
            i = jnp.where(i < TARGETS, i, i - TARGETS)
            there, own = target(i)

            @pl.when(jnp.logical_not(own))
            def _():
                remote(chunk(slots, a, i), chunk(arrived, a, s), route_send.at[a], route_recv.at[a], there).start()

            return 0

        lax.fori_loop(first, last, start, 0)

        if last == TARGETS:

            @pl.when(same)
            def _():
                pltpu.make_async_copy(chunk(slots, a, seat), chunk(arrived, a, s), route_recv.at[a]).start()

    def rows_of(a, i):
        return full.at[a, pl.ds(pl.multiple_of(i * ROWS, ROWS), ROWS), :]

    def piece(a, n):
        rows = full.at[a, pl.ds(pl.multiple_of(me * ROWS + n * PIECE, PIECE), PIECE), :]
        return remote(rows, rows, near_send.at[a, 0], near_recv.at[a, 0], member(me ^ 2))

    to_slots(0, k_ref)
    arrivals = jnp.where(active, SEQ + 3, 0) - jnp.where(same, 2, 0)
    pl.semaphore_wait(barrier, TARGETS + 7 + arrivals)
    exchange = remote(enc_ref, other, enc_sem.at[0], enc_sem.at[1], sibling)

    @pl.when(active)
    def _():
        exchange.start()

    route(0, 0, TARGETS)
    to_slots(1, q_ref)
    route(1, 0, TARGETS)
    to_slots(2, v_ref)
    to_slots(3, g_ref)


    def unit_codes(u):
        return codes[pl.ds(UNITS * me + u, 1), :]

    def build_pick():
        exchange.wait()
        codes[...] = jnp.where(clip == dp, enc_ref[...], other[...])
        wide_iota = lax.broadcasted_iota(jnp.int32, (SHARE, 128), 1).astype(jnp.float32)
        for u in range(UNITS):
            code = unit_codes(u)
            code = (code >> 3) * CHUNK + u * SLOTS + (code & 7)
            wide = jnp.broadcast_to(code.astype(jnp.float32), (SHARE, 128)).T
            for c in range(FLAT // 128):
                pick[u * SHARE : (u + 1) * SHARE, c * 128 : (c + 1) * 128] = one_hot(wide == wide_iota + c * 128.0)


    def near(a, way, rows, there):
        return remote(rows_of(a, rows), rows_of(a, rows), near_send.at[a, way], near_recv.at[a, way], member(there))

    def gather_rest():
        def start(n, _):
            piece(3, n).start()
            return 0

        lax.fori_loop(0, ROWS // PIECE, start, 0)

    def gather_pass(a):
        near(a, 0, me ^ 2, me).wait_recv()
        near(a, 2, me ^ 2, me ^ 1).start()

    def gather_finish(a):
        near(a, 1, me ^ 1, me).wait_recv()
        near(a, 2, me ^ 3, me).wait_recv()

    def gather_sent(a):
        near(a, 0, me, me ^ 2).wait_send()
        near(a, 1, me, me ^ 1).wait_send()
        near(a, 2, me ^ 2, me ^ 1).wait_send()

    own_rows = pl.ds(pl.multiple_of(me * ROWS, 256), ROWS)

    def to_dense(a):
        remote(arrived.at[a], arrived.at[a], route_send.at[a], route_recv.at[a], sibling).wait_recv()
        rows = jnp.dot(pick[...], arrived[a], preferred_element_type=jnp.float32)
        if a < 2:
            raw[a] = rows.astype(jnp.bfloat16)
            gain = (gain_k_ref, gain_q_ref)[a][...]
            rows = rows * inverse_norm(rows) * gain
        full[a, own_rows, :] = rows.astype(jnp.bfloat16)
        near(a, 1, me, me ^ 1).start()


    chunks = [slice(i * step, (i + 1) * step) for i in range(KEPT // step)]

    def head_rows(a, cols):
        return full[a, cols, :]

    def tile_rows(a, t):
        return full[a, pl.ds(pl.multiple_of(me * ROWS + t * TILE, TILE), TILE), :]

    def local_rows(t):
        return pl.ds(pl.multiple_of(t * TILE, TILE), TILE)

    def store_stat(i, t, value):
        wide = jnp.broadcast_to(value, (TILE, 128)).T
        for j in range(TILE // SHARE):
            stats[me, i, pl.ds(TILE // SHARE * t + j, 1), :] = wide[0:1, j * SHARE : (j + 1) * SHARE]

    def score_tile(t, _):
        query = tile_rows(1, t)
        rows = local_rows(t)
        top = None
        for cols in chunks:
            scores = lax.dot_general(query, head_rows(0, cols), NT, preferred_element_type=jnp.float32)
            scores = scores * (SCALING * LOG2E)
            scores_ref[rows, cols] = scores
            part = lane_fold(scores, jnp.maximum)
            top = part if top is None else jnp.maximum(top, part)
        top = jnp.max(top, axis=-1, keepdims=True)
        total = jnp.zeros((TILE, 128), jnp.float32)
        for cols in chunks:
            weights = jnp.exp2(scores_ref[rows, cols] - top)
            scores_ref[rows, cols] = weights
            total += lane_fold(weights, jnp.add)
        total = jnp.sum(total, axis=-1, keepdims=True)
        sums[rows, :] = jnp.broadcast_to(total, (TILE, 128))
        store_stat(0, t, top + jnp.log2(total))

        return 0

    def spread_tile(t, rows):
        tile_iota = lax.broadcasted_iota(jnp.int32, (SEQ * PART, TILE), 0)
        tile_codes = []
        for j in range(TILE // SHARE):
            code = unit_codes(TILE // SHARE * t + j)
            tile_codes.append((code >> 3) * PART + j * SLOTS + (code & 7))
        spread = one_hot(tile_iota == jnp.concatenate(tile_codes, axis=1))
        rows = jnp.dot(spread, rows.astype(jnp.bfloat16), preferred_element_type=jnp.float32)
        return rows.astype(jnp.bfloat16).reshape(SEQ, PART, HD)

    def part_of(t):
        return pl.ds(pl.multiple_of(t * PART, PART), PART)

    def query_tile(t, _):
        grad = tile_rows(3, t)
        rows = local_rows(t)
        weighted = jnp.zeros((TILE, 128), jnp.float32)
        for cols in chunks:
            dots = lax.dot_general(grad, head_rows(2, cols), NT, preferred_element_type=jnp.float32)
            dots_ref[:, cols] = dots
            weighted += lane_fold(scores_ref[rows, cols] * dots, jnp.add)
        share = 1.0 / sums[rows, 0:1]
        delta = jnp.sum(weighted, axis=-1, keepdims=True) * share
        result = jnp.zeros((TILE, HD), jnp.float32)
        for cols in chunks:
            dscore = (scores_ref[rows, cols] * share) * (dots_ref[:, cols] - delta)
            result += jnp.dot(dscore.astype(jnp.bfloat16), head_rows(0, cols), preferred_element_type=jnp.float32)
        grads, term = norm_grads(raw[1, rows, :], gain_q_ref[...], result * SCALING)
        terms[0:8, :] += term
        store_stat(1, t, delta)

        q_slots[:, part_of(t), :] = spread_tile(t, grads)
        send_home(lambda i: q_home(t, i), 0)
        return 0


    def stat_copy(rows, there):
        return remote(stats.at[rows], stats.at[rows], stat_send.at[there], stat_recv.at[rows], member(there))

    def stat_start():
        for step in (1, 2, 3):
            stat_copy(me, me ^ step).start()

    def stat_finish():
        for step in (1, 2, 3):
            stat_copy(me ^ step, me ^ step).wait_recv()
            stat_copy(me, me ^ step).wait_send()


    def home_rows(t):
        return pl.ds(pl.multiple_of(seat * CHUNK + t * PART, PART), PART)

    def q_home(t, i):
        return q_slots.at[i, part_of(t), :], home_ref.at[0, home_rows(t), :]

    def kv_home(t, i):
        return kv_slots.at[:, i, part_of(t), :], home_ref.at[1:3, home_rows(t), :]

    def send_home(copies, sem):
        def start(n, _):
            i = (n + s) & (SEQ - 1)
            src, dst = copies(i)

            @pl.when(jnp.logical_not(to_self(i)))
            def _():
                remote(src, dst, home_send.at[sem], home_recv.at[sem], source(i)).start()

            return 0

        lax.fori_loop(0, SEQ, start, 0)

        @pl.when(same)
        def _():
            src, dst = copies(s)
            pltpu.make_async_copy(src, dst, home_recv.at[sem]).start()


    def stat_row(i, cols):
        units = range(cols.start // SHARE, cols.stop // SHARE)
        return jnp.concatenate([stats[u // UNITS, i, u % UNITS : u % UNITS + 1, :] for u in units], axis=1)

    def key_tile(t, _):
        key, value = tile_rows(0, t), tile_rows(2, t)
        key_grad = jnp.zeros((TILE, HD), jnp.float32)
        value_grad = jnp.zeros((TILE, HD), jnp.float32)
        for cols in chunks:
            query, grad = head_rows(1, cols), head_rows(3, cols)
            scores = lax.dot_general(key, query, NT, preferred_element_type=jnp.float32)
            weights = jnp.exp2(scores * (SCALING * LOG2E) - stat_row(0, cols))
            dots = lax.dot_general(value, grad, NT, preferred_element_type=jnp.float32)
            dscore = weights * (dots - stat_row(1, cols))
            key_grad += jnp.dot(dscore.astype(jnp.bfloat16), query, preferred_element_type=jnp.float32)
            value_grad += jnp.dot(weights.astype(jnp.bfloat16), grad, preferred_element_type=jnp.float32)
        grads, term = norm_grads(raw[0, local_rows(t), :], gain_k_ref[...], key_grad * SCALING)
        terms[8:16, :] += term
        for i, result in enumerate((grads, value_grad)):
            kv_slots[i, :, part_of(t), :] = spread_tile(t, result)
        send_home(lambda i: kv_home(t, i), 1)
        return 0


    def part_start(i, _):
        @pl.when(jnp.logical_not(to_self(i)))
        def _():
            remote(terms, parts.at[seat], part_sem.at[0], part_sem.at[1], source(i)).start()

        return 0

    @pl.when(active)
    def _():
        build_pick()
        to_dense(0)

    route(2, 0, TARGETS, beside=0)

    @pl.when(active)
    def _():
        to_dense(1)

    route(3, 0, TARGETS // 2, beside=1)

    @pl.when(active)
    def _():
        terms[...] = jnp.zeros_like(terms)
        gather_pass(0)
        gather_finish(0)
        lax.fori_loop(0, TILES // 2, score_tile, 0)
        to_dense(2)

    route(3, TARGETS // 2, TARGETS, beside=2)

    @pl.when(active)
    def _():
        gather_pass(1)
        lax.fori_loop(TILES // 2, TILES, score_tile, 0)
        gather_pass(2)
        to_dense(3)
        gather_rest()
        gather_finish(2)
        lax.fori_loop(0, TILES, query_tile, 0)
        stat_start()
        gather_pass(3)
        gather_finish(1)
        gather_finish(3)
        stat_finish()
        lax.fori_loop(0, TILES, key_tile, 0)
        lax.fori_loop(0, SEQ, part_start, 0)

        @pl.when(same)
        def _():
            pltpu.make_async_copy(terms, parts.at[seat], part_sem.at[1]).start()

    remote(parts, parts, part_sem.at[0], part_sem.at[1], sibling).wait_recv()
    partial[...] = jnp.sum(parts[...], axis=0)

    def cross_copy(i, dst):
        return remote(partial, cross.at[dst], cross_send.at[i], cross_recv.at[dst], (i >> 2, s, i & 3))

    def cross_start(i, _):
        @pl.when(i != corner)
        def _():
            cross_copy(i, corner).start()

        return 0

    def cross_finish(i, _):
        @pl.when(i != corner)
        def _():
            cross_copy(i, i).wait_recv()
            cross_copy(i, corner).wait_send()

        return 0

    cross[pl.ds(corner, 1)] = partial[...][None]
    lax.fori_loop(0, 8, cross_start, 0)
    lax.fori_loop(0, 8, cross_finish, 0)
    total_ref[...] = jnp.sum(cross[...], axis=0)


    def sent(targets, sources):
        for a in range(4):
            rows = slots.at[a, 0 : targets * CHUNK, :]
            remote(rows, rows, route_send.at[a], route_recv.at[a], sibling).wait_send()
        if sources:
            for a in range(4):
                gather_sent(a)
            rows = q_slots.at[0:sources]
            remote(rows, rows, home_send.at[0], home_recv.at[0], sibling).wait_send()
            rows = kv_slots.at[:, 0:sources]
            remote(rows, rows, home_send.at[1], home_recv.at[1], sibling).wait_send()
            rows = part_bytes.at[0:sources]
            remote(rows, rows, part_sem.at[0], part_sem.at[1], sibling).wait_send()

    @pl.when(same)
    def _():
        sent(TARGETS - 1, SEQ - 1)

    @pl.when(active & jnp.logical_not(same))
    def _():
        sent(TARGETS, SEQ)

    @pl.when(jnp.logical_not(active))
    def _():
        sent(TARGETS, 0)

    remote(home_ref.at[0], home_ref.at[0], home_send.at[0], home_recv.at[0], sibling).wait_recv()
    remote(home_ref.at[1:3], home_ref.at[1:3], home_send.at[1], home_recv.at[1], sibling).wait_recv()


def core(listing, k, q, v, g, gain_q, gain_k):
    bf16, f32 = jnp.bfloat16, jnp.float32
    dma = pltpu.SemaphoreType.DMA
    in_vmem = pl.BlockSpec(memory_space=pltpu.VMEM)
    return pl.pallas_call(
        core_kernel,
        name="core",
        in_specs=[in_vmem] * 7,
        out_specs=[pl.BlockSpec(memory_space=pl.ANY), in_vmem, in_vmem],
        out_shape=(
            jax.ShapeDtypeStruct((3, OUT, HD), bf16),
            jax.ShapeDtypeStruct((SPAN, SPAN), bf16),
            jax.ShapeDtypeStruct((16, HD), f32),
        ),
        scratch_shapes=[
            pltpu.VMEM((4, OUT, HD), bf16),
            pltpu.VMEM((4, FLAT, HD), bf16),
            pltpu.VMEM((SEQ, SHARE), jnp.int32),
            pltpu.VMEM((SEQ, SHARE), jnp.int32),
            pltpu.VMEM((SEQ, SHARE), jnp.int32),
            pltpu.VMEM((ROWS, FLAT), bf16),
            pltpu.VMEM((4, KEPT, HD), bf16),
            pltpu.VMEM((2, ROWS, HD), bf16),
            pltpu.VMEM((ROWS, KEPT), f32),
            pltpu.VMEM((TILE, KEPT), f32),
            pltpu.VMEM((ROWS, 128), f32),
            pltpu.VMEM((SEQ, CHUNK, HD), bf16),
            pltpu.VMEM((2, SEQ, CHUNK, HD), bf16),
            pltpu.VMEM((MEMBERS, 2, 8, SHARE), f32),
            pltpu.VMEM((16, HD), f32),
            pltpu.VMEM((SEQ, 16, HD), f32),
            pltpu.VMEM((TARGETS, 16, HD), f32),
            pltpu.VMEM((16, HD), f32),
            pltpu.VMEM((8, 16, HD), f32),
            dma((2,)),
            dma((4,)),
            dma((4,)),
            dma((4, 3)),
            dma((4, 3)),
            dma((MEMBERS,)),
            dma((MEMBERS,)),
            dma((2,)),
            dma((2,)),
            dma((2,)),
            dma((8,)),
            dma((8,)),
        ],
        compiler_params=pltpu.CompilerParams(
            collective_id=0, has_side_effects=True, vmem_limit_bytes=VMEM_LIMIT
        ),
    )(listing, k, q, v, g, gain_q, gain_k)


def rows_kernel(back_ref, slots_ref, total_ref, q_ref, k_ref, v_ref, gain_q_ref, gain_k_ref):
    for i, ref in enumerate((q_ref, k_ref, v_ref)):
        for h in range(slots_ref.shape[1] // SPAN):
            rows = slots_ref[i, h * SPAN : (h + 1) * SPAN, :]
            rows = jnp.dot(back_ref[...], rows, preferred_element_type=jnp.float32)
            ref[0, :, h * HD : (h + 1) * HD] = rows.astype(jnp.bfloat16)
    gain_q_ref[...] = jnp.sum(total_ref[0:8, :], axis=0, keepdims=True)
    gain_k_ref[...] = jnp.sum(total_ref[8:16, :], axis=0, keepdims=True)


def to_rows(back, slots, total):
    width = HEAD_PART * HD
    parts = 2
    big = jax.ShapeDtypeStruct((1, SPAN, width), jnp.bfloat16)
    small = jax.ShapeDtypeStruct((1, HD), jnp.float32)
    return pl.pallas_call(
        rows_kernel,
        name="to_rows",
        grid=(parts,),
        in_specs=[
            pl.BlockSpec((SPAN, SPAN), lambda h: (0, 0)),
            pl.BlockSpec((3, OUT // parts, HD), lambda h: (0, h, 0)),
            pl.BlockSpec((16, HD), lambda h: (0, 0)),
        ],
        out_specs=[pl.BlockSpec((1, SPAN, width // parts), lambda h: (0, 0, h))] * 3
        + [pl.BlockSpec((1, HD), lambda h: (0, 0))] * 2,
        out_shape=(big, big, big, small, small),
        compiler_params=pltpu.CompilerParams(vmem_limit_bytes=VMEM_LIMIT),
        cost_estimate=pl.CostEstimate(flops=3 * 10**8, bytes_accessed=3 * 10**6, transcendentals=0),
    )(back, slots, total)


def on_device(q_raw, k_raw, v_raw, out_grad, gain_q, gain_k, keep_list):
    home, back, total = core(
        keep_list.reshape(SEQ, SHARE),
        k_raw[0],
        q_raw[0],
        v_raw[0],
        out_grad[0],
        gain_q.reshape(1, HD),
        gain_k.reshape(1, HD),
    )
    q_out, k_out, v_out, gain_q_grad, gain_k_grad = to_rows(back, home, total)
    return q_out, k_out, v_out, gain_q_grad.reshape(HD), gain_k_grad.reshape(HD)


def solution(mesh):
    big = P("dp", "seq", "tensor")
    return jax.shard_map(
        on_device,
        mesh=mesh,
        in_specs=(big, big, big, big, P(), P(), P("dp", None)),
        out_specs=(big, big, big, P(), P()),
        check_vma=False,
    )
```

```python
import math

import jax
import jax.numpy as jnp
from jax import lax
from jax.experimental import pallas as pl
from jax.experimental.pallas import tpu as pltpu
from jax.sharding import PartitionSpec as P

MESH = pl.DeviceIdType.MESH
HD = 128
EPSILON = 1e-06
SEQ = 32
SPAN = 256
SHARE = 128
SLOTS = 8
HEAD_PART = 6
UNITS = 8
ROWS = UNITS * SHARE
CHUNK = UNITS * SLOTS
MEMBERS = 4
TARGETS = HEAD_PART * MEMBERS
OUT = TARGETS * CHUNK
FLAT = SEQ * CHUNK
KEPT = SEQ * SHARE
TILE = 512
PART = TILE // SHARE * SLOTS
TILES = ROWS // TILE
PIECE = 128
SCALING = 1.0 / math.sqrt(HD)
LOG2E = 1.4426950408889634
VMEM_LIMIT = 56 * 1024 * 1024

NT = (((1,), (1,)), ((), ()))

def place(clip, i):
    head, quarter = i >> 2, i & 3
    third = (head * 11) >> 5
    pair = head - 3 * third
    odd = pair >> 1
    y = 2 * ((pair & 1) + odd * third) + (quarter >> 1)
    z = 4 * clip + 2 * third + odd
    return quarter & 1, y * 8 + z


def my_place(dp, s):
    y, z = s >> 3, s & 7
    third, odd, high = (z >> 1) & 1, z & 1, y >> 1
    pair = high + odd * (2 - high)
    active = (odd == 0) | (high == third)
    return z >> 2, (3 * third + pair) * 4 + 2 * (y & 1) + dp, active


def one_hot(hit):
    return jnp.where(hit, 1.0, 0.0).astype(jnp.bfloat16)


def inverse_norm(x):
    return lax.rsqrt(jnp.mean(x * x, axis=-1, keepdims=True) + EPSILON)


def norm_grads(raw, gain, upstream):
    raw = raw.astype(jnp.float32)
    inverse = inverse_norm(raw)
    scaled = upstream * gain
    inner = jnp.mean(scaled * raw, axis=-1, keepdims=True)
    grads = inverse * scaled - raw * (inverse * inverse * inverse * inner)
    terms = upstream * raw * inverse
    return grads, jnp.sum(terms.reshape(-1, 8, HD), axis=0)


def lane_fold(x, fold):
    parts = [x[:, i * 128 : (i + 1) * 128] for i in range(x.shape[1] // 128)]
    total = parts[0]
    for part in parts[1:]:
        total = fold(total, part)
    return total


def core_kernel(
    list_ref,
    k_ref,
    q_ref,
    v_ref,
    g_ref,
    gain_q_ref,
    gain_k_ref,
    home_ref,
    back_ref,
    total_ref,
    slots,
    arrived,
    enc_ref,
    other,
    codes,
    pick,
    full,
    raw,
    scores_ref,
    dots_ref,
    sums,
    q_slots,
    kv_slots,
    stats,
    terms,
    part_bytes,
    parts,
    partial,
    cross,
    enc_sem,
    route_send,
    route_recv,
    near_send,
    near_recv,
    stat_send,
    stat_recv,
    home_send,
    home_recv,
    part_sem,
    cross_send,
    cross_recv,
):
    dp, s, x = lax.axis_index("dp"), lax.axis_index("seq"), lax.axis_index("tensor")
    clip, seat, active = my_place(dp, s)
    me = seat & 3
    sibling = (1 - dp, s, x)
    corner = dp * 4 + x
    same = active & (clip == dp)
    own_source = jnp.where(same, s, -1)
    own_target = jnp.where(same, seat, -1)

    def to_self(i):
        return i == own_source

    def target(i):
        return place(dp, i) + (x,), i == own_target

    def source(i):
        return (clip, i, x)

    def member(i):
        return (i & 1, (s & 23) + 8 * (i >> 1), x)

    def remote(src, dst, send_sem, recv_sem, device):
        return pltpu.make_async_remote_copy(
            src_ref=src, dst_ref=dst, send_sem=send_sem, recv_sem=recv_sem, device_id=device, device_id_type=MESH
        )


    barrier = pltpu.get_barrier_semaphore()

    def greet_device(there):
        pl.semaphore_signal(barrier, inc=1, device_id=there, device_id_type=MESH)

    def greet_target(i, _):
        there, own = target(i)

        @pl.when(jnp.logical_not(own))
        def _():
            greet_device(there)

        return 0

    def greet_source(i, _):
        @pl.when(jnp.logical_not(to_self(i)))
        def _():
            greet_device(source(i))

        return 0

    def greet_corner(i, _):
        @pl.when(i != corner)
        def _():
            greet_device((i >> 2, s, i & 3))

        return 0

    @pl.when(active)
    def _():
        lax.fori_loop(0, SEQ, greet_source, 0)
        for step in (1, 2, 3):
            greet_device(member(me ^ step))

    lax.fori_loop(0, TARGETS, greet_target, 0)
    lax.fori_loop(0, 8, greet_corner, 0)


    listing = list_ref[...]
    from_block = listing >> 8
    hits = one_hot(jnp.concatenate([from_block == i for i in range(SEQ)], axis=0))
    earlier = lax.broadcasted_iota(jnp.int32, (SHARE, SHARE), 0) < lax.broadcasted_iota(jnp.int32, (SHARE, SHARE), 1)
    counts = jnp.dot(hits, one_hot(earlier), preferred_element_type=jnp.float32) * hits.astype(jnp.float32)
    rank = counts[0:SEQ]
    for i in range(1, SEQ):
        rank += counts[i * SEQ : (i + 1) * SEQ]
    rank = rank.astype(jnp.int32)
    enc_ref[...] = from_block * SLOTS + rank
    slot = lax.broadcasted_iota(jnp.int32, (SEQ, SHARE), 0) * SLOTS + rank + 1
    slot = jnp.where(from_block == s, slot, 0).astype(jnp.float32)
    token = listing - s * SPAN
    token_iota = lax.broadcasted_iota(jnp.int32, (SPAN, SHARE), 0)
    found = jnp.zeros((SPAN, SHARE), jnp.float32)
    for j in range(SEQ):
        found += jnp.where(token_iota == token[j : j + 1], slot[j : j + 1], 0.0)
    found = jnp.sum(found, axis=1, keepdims=True) - 1.0
    row = jnp.broadcast_to(found, (SPAN, 128)).T[0:1]
    back_ref[...] = one_hot(lax.broadcasted_iota(jnp.int32, (SPAN, SPAN), 1).astype(jnp.float32) == found)
    take = one_hot(lax.broadcasted_iota(jnp.int32, (SPAN, SPAN), 0).astype(jnp.float32) == row)
    step = 512

    def to_slots(i, ref):
        rows = jnp.dot(take, ref[...], preferred_element_type=jnp.float32).astype(jnp.bfloat16)
        for h in range(HEAD_PART):
            slots[i, h * SPAN : (h + 1) * SPAN, :] = rows[:, h * HD : (h + 1) * HD]

    def chunk(ref, a, i):
        return ref.at[a, pl.ds(pl.multiple_of(i * CHUNK, 16), CHUNK), :]

    def nth_target(n):
        v = 3 * (s & 7) + 6 * (s >> 3) + 7 * n
        return v - 24 * ((v * 171) >> 12)

    def nth_source(n):
        turn = n & 7
        away = ((turn + 1) >> 1) * (2 * (turn & 1) - 1)
        return (((s >> 3) + (n >> 3)) & 3) * 8 + (((s & 7) + away) & 7)


    def route(a, first, last, beside=None):
        def start(n, _):
            if beside is not None:

                @pl.when(n < first + ROWS // PIECE)
                def _():
                    @pl.when(active)
                    def _():
                        piece(beside, n - first).start()

            i = nth_target(n)
            there, own = target(i)

            @pl.when(jnp.logical_not(own))
            def _():
                remote(chunk(slots, a, i), chunk(arrived, a, s), route_send.at[a], route_recv.at[a], there).start()

            return 0

        lax.fori_loop(first, last, start, 0)

        if last == TARGETS:

            @pl.when(same)
            def _():
                pltpu.make_async_copy(chunk(slots, a, seat), chunk(arrived, a, s), route_recv.at[a]).start()

    def rows_of(a, i):
        return full.at[a, pl.ds(pl.multiple_of(i * ROWS, ROWS), ROWS), :]

    def piece(a, n):
        rows = full.at[a, pl.ds(pl.multiple_of(me * ROWS + n * PIECE, PIECE), PIECE), :]
        return remote(rows, rows, near_send.at[a, 0], near_recv.at[a, 0], member(me ^ 2))

    to_slots(0, k_ref)
    arrivals = jnp.where(active, SEQ + 3, 0) - jnp.where(same, 2, 0)
    pl.semaphore_wait(barrier, TARGETS + 7 + arrivals)
    exchange = remote(enc_ref, other, enc_sem.at[0], enc_sem.at[1], sibling)

    @pl.when(active)
    def _():
        exchange.start()

    route(0, 0, TARGETS)
    to_slots(1, q_ref)
    route(1, 0, TARGETS)
    to_slots(2, v_ref)
    to_slots(3, g_ref)


    def unit_codes(u):
        return codes[pl.ds(UNITS * me + u, 1), :]

    def build_pick():
        exchange.wait()
        codes[...] = jnp.where(clip == dp, enc_ref[...], other[...])
        wide_iota = lax.broadcasted_iota(jnp.int32, (SHARE, 128), 1).astype(jnp.float32)
        for u in range(UNITS):
            code = unit_codes(u)
            code = (code >> 3) * CHUNK + u * SLOTS + (code & 7)
            wide = jnp.broadcast_to(code.astype(jnp.float32), (SHARE, 128)).T
            for c in range(FLAT // 128):
                pick[u * SHARE : (u + 1) * SHARE, c * 128 : (c + 1) * 128] = one_hot(wide == wide_iota + c * 128.0)


    def near(a, way, rows, there):
        return remote(rows_of(a, rows), rows_of(a, rows), near_send.at[a, way], near_recv.at[a, way], member(there))

    def gather_rest():
        def start(n, _):
            piece(3, n).start()
            return 0

        lax.fori_loop(0, ROWS // PIECE, start, 0)

    def gather_pass(a):
        near(a, 0, me ^ 2, me).wait_recv()
        near(a, 2, me ^ 2, me ^ 1).start()

    def gather_finish(a):
        near(a, 1, me ^ 1, me).wait_recv()
        near(a, 2, me ^ 3, me).wait_recv()

    def gather_sent(a):
        near(a, 0, me, me ^ 2).wait_send()
        near(a, 1, me, me ^ 1).wait_send()
        near(a, 2, me ^ 2, me ^ 1).wait_send()

    own_rows = pl.ds(pl.multiple_of(me * ROWS, 256), ROWS)

    def to_dense(a):
        remote(arrived.at[a], arrived.at[a], route_send.at[a], route_recv.at[a], sibling).wait_recv()
        rows = jnp.dot(pick[...], arrived[a], preferred_element_type=jnp.float32)
        if a < 2:
            raw[a] = rows.astype(jnp.bfloat16)
            gain = (gain_k_ref, gain_q_ref)[a][...]
            rows = rows * inverse_norm(rows) * gain
        full[a, own_rows, :] = rows.astype(jnp.bfloat16)
        near(a, 1, me, me ^ 1).start()


    chunks = [slice(i * step, (i + 1) * step) for i in range(KEPT // step)]

    def head_rows(a, cols):
        return full[a, cols, :]

    def tile_rows(a, t):
        return full[a, pl.ds(pl.multiple_of(me * ROWS + t * TILE, TILE), TILE), :]

    def local_rows(t):
        return pl.ds(pl.multiple_of(t * TILE, TILE), TILE)

    def store_stat(i, t, value):
        wide = jnp.broadcast_to(value, (TILE, 128)).T
        for j in range(TILE // SHARE):
            stats[me, i, pl.ds(TILE // SHARE * t + j, 1), :] = wide[0:1, j * SHARE : (j + 1) * SHARE]

    def score_tile(t, _):
        query = tile_rows(1, t)
        rows = local_rows(t)
        top = None
        for cols in chunks:
            scores = lax.dot_general(query, head_rows(0, cols), NT, preferred_element_type=jnp.float32)
            scores = scores * (SCALING * LOG2E)
            scores_ref[rows, cols] = scores
            part = lane_fold(scores, jnp.maximum)
            top = part if top is None else jnp.maximum(top, part)
        top = jnp.max(top, axis=-1, keepdims=True)
        total = jnp.zeros((TILE, 128), jnp.float32)
        for cols in chunks:
            weights = jnp.exp2(scores_ref[rows, cols] - top)
            scores_ref[rows, cols] = weights
            total += lane_fold(weights, jnp.add)
        total = jnp.sum(total, axis=-1, keepdims=True)
        sums[rows, :] = jnp.broadcast_to(total, (TILE, 128))
        store_stat(0, t, top + jnp.log2(total))

        return 0

    def spread_tile(t, rows):
        tile_iota = lax.broadcasted_iota(jnp.int32, (SEQ * PART, TILE), 0)
        tile_codes = []
        for j in range(TILE // SHARE):
            code = unit_codes(TILE // SHARE * t + j)
            tile_codes.append((code >> 3) * PART + j * SLOTS + (code & 7))
        spread = one_hot(tile_iota == jnp.concatenate(tile_codes, axis=1))
        rows = jnp.dot(spread, rows.astype(jnp.bfloat16), preferred_element_type=jnp.float32)
        return rows.astype(jnp.bfloat16).reshape(SEQ, PART, HD)

    def part_of(t):
        return pl.ds(pl.multiple_of(t * PART, PART), PART)

    def query_tile(t, _):
        grad = tile_rows(3, t)
        rows = local_rows(t)
        weighted = jnp.zeros((TILE, 128), jnp.float32)
        for cols in chunks:
            dots = lax.dot_general(grad, head_rows(2, cols), NT, preferred_element_type=jnp.float32)
            dots_ref[:, cols] = dots
            weighted += lane_fold(scores_ref[rows, cols] * dots, jnp.add)
        share = 1.0 / sums[rows, 0:1]
        delta = jnp.sum(weighted, axis=-1, keepdims=True) * share
        result = jnp.zeros((TILE, HD), jnp.float32)
        for cols in chunks:
            dscore = (scores_ref[rows, cols] * share) * (dots_ref[:, cols] - delta)
            result += jnp.dot(dscore.astype(jnp.bfloat16), head_rows(0, cols), preferred_element_type=jnp.float32)
        grads, term = norm_grads(raw[1, rows, :], gain_q_ref[...], result * SCALING)
        terms[0:8, :] += term
        store_stat(1, t, delta)

        q_slots[:, part_of(t), :] = spread_tile(t, grads)
        send_home(lambda i: q_home(t, i), 0)
        return 0


    def stat_copy(rows, there):
        return remote(stats.at[rows], stats.at[rows], stat_send.at[there], stat_recv.at[rows], member(there))

    def stat_start():
        for step in (1, 2, 3):
            stat_copy(me, me ^ step).start()

    def stat_finish():
        for step in (1, 2, 3):
            stat_copy(me ^ step, me ^ step).wait_recv()
            stat_copy(me, me ^ step).wait_send()


    def home_rows(t):
        return pl.ds(pl.multiple_of(seat * CHUNK + t * PART, PART), PART)

    def q_home(t, i):
        return q_slots.at[i, part_of(t), :], home_ref.at[0, home_rows(t), :]

    def kv_home(t, i):
        return kv_slots.at[:, i, part_of(t), :], home_ref.at[1:3, home_rows(t), :]

    def send_home(copies, sem):
        def start(n, _):
            i = nth_source(n)
            src, dst = copies(i)

            @pl.when(jnp.logical_not(to_self(i)))
            def _():
                remote(src, dst, home_send.at[sem], home_recv.at[sem], source(i)).start()

            return 0

        lax.fori_loop(0, SEQ, start, 0)

        @pl.when(same)
        def _():
            src, dst = copies(s)
            pltpu.make_async_copy(src, dst, home_recv.at[sem]).start()


    def stat_row(i, cols):
        units = range(cols.start // SHARE, cols.stop // SHARE)
        return jnp.concatenate([stats[u // UNITS, i, u % UNITS : u % UNITS + 1, :] for u in units], axis=1)

    def key_tile(t, _):
        key, value = tile_rows(0, t), tile_rows(2, t)
        key_grad = jnp.zeros((TILE, HD), jnp.float32)
        value_grad = jnp.zeros((TILE, HD), jnp.float32)
        for cols in chunks:
            query, grad = head_rows(1, cols), head_rows(3, cols)
            scores = lax.dot_general(key, query, NT, preferred_element_type=jnp.float32)
            weights = jnp.exp2(scores * (SCALING * LOG2E) - stat_row(0, cols))
            dots = lax.dot_general(value, grad, NT, preferred_element_type=jnp.float32)
            dscore = weights * (dots - stat_row(1, cols))
            key_grad += jnp.dot(dscore.astype(jnp.bfloat16), query, preferred_element_type=jnp.float32)
            value_grad += jnp.dot(weights.astype(jnp.bfloat16), grad, preferred_element_type=jnp.float32)
        grads, term = norm_grads(raw[0, local_rows(t), :], gain_k_ref[...], key_grad * SCALING)
        terms[8:16, :] += term
        for i, result in enumerate((grads, value_grad)):
            kv_slots[i, :, part_of(t), :] = spread_tile(t, result)
        send_home(lambda i: kv_home(t, i), 1)
        return 0


    def part_start(i, _):
        @pl.when(jnp.logical_not(to_self(i)))
        def _():
            remote(terms, parts.at[seat], part_sem.at[0], part_sem.at[1], source(i)).start()

        return 0

    @pl.when(active)
    def _():
        build_pick()
        to_dense(0)

    route(2, 0, TARGETS, beside=0)

    @pl.when(active)
    def _():
        to_dense(1)

    route(3, 0, TARGETS // 2, beside=1)

    @pl.when(active)
    def _():
        terms[...] = jnp.zeros_like(terms)
        gather_pass(0)
        gather_finish(0)
        lax.fori_loop(0, TILES // 2, score_tile, 0)
        to_dense(2)

    route(3, TARGETS // 2, TARGETS, beside=2)

    @pl.when(active)
    def _():
        gather_pass(1)
        lax.fori_loop(TILES // 2, TILES, score_tile, 0)
        gather_pass(2)
        to_dense(3)
        gather_rest()
        gather_finish(2)
        lax.fori_loop(0, TILES, query_tile, 0)
        stat_start()
        gather_pass(3)
        gather_finish(1)
        gather_finish(3)
        stat_finish()
        lax.fori_loop(0, TILES, key_tile, 0)
        lax.fori_loop(0, SEQ, part_start, 0)

        @pl.when(same)
        def _():
            pltpu.make_async_copy(terms, parts.at[seat], part_sem.at[1]).start()

    remote(parts, parts, part_sem.at[0], part_sem.at[1], sibling).wait_recv()
    partial[...] = jnp.sum(parts[...], axis=0)

    def cross_copy(i, dst):
        return remote(partial, cross.at[dst], cross_send.at[i], cross_recv.at[dst], (i >> 2, s, i & 3))

    def cross_start(i, _):
        @pl.when(i != corner)
        def _():
            cross_copy(i, corner).start()

        return 0

    def cross_finish(i, _):
        @pl.when(i != corner)
        def _():
            cross_copy(i, i).wait_recv()
            cross_copy(i, corner).wait_send()

        return 0

    cross[pl.ds(corner, 1)] = partial[...][None]
    lax.fori_loop(0, 8, cross_start, 0)
    lax.fori_loop(0, 8, cross_finish, 0)
    total_ref[...] = jnp.sum(cross[...], axis=0)


    def sent(targets, sources):
        for a in range(4):
            rows = slots.at[a, 0 : targets * CHUNK, :]
            remote(rows, rows, route_send.at[a], route_recv.at[a], sibling).wait_send()
        if sources:
            for a in range(4):
                gather_sent(a)
            rows = q_slots.at[0:sources]
            remote(rows, rows, home_send.at[0], home_recv.at[0], sibling).wait_send()
            rows = kv_slots.at[:, 0:sources]
            remote(rows, rows, home_send.at[1], home_recv.at[1], sibling).wait_send()
            rows = part_bytes.at[0:sources]
            remote(rows, rows, part_sem.at[0], part_sem.at[1], sibling).wait_send()

    @pl.when(same)
    def _():
        sent(TARGETS - 1, SEQ - 1)

    @pl.when(active & jnp.logical_not(same))
    def _():
        sent(TARGETS, SEQ)

    @pl.when(jnp.logical_not(active))
    def _():
        sent(TARGETS, 0)

    remote(home_ref.at[0], home_ref.at[0], home_send.at[0], home_recv.at[0], sibling).wait_recv()
    remote(home_ref.at[1:3], home_ref.at[1:3], home_send.at[1], home_recv.at[1], sibling).wait_recv()


def core(listing, k, q, v, g, gain_q, gain_k):
    bf16, f32 = jnp.bfloat16, jnp.float32
    dma = pltpu.SemaphoreType.DMA
    in_vmem = pl.BlockSpec(memory_space=pltpu.VMEM)
    return pl.pallas_call(
        core_kernel,
        name="core",
        in_specs=[in_vmem] * 7,
        out_specs=[pl.BlockSpec(memory_space=pl.ANY), in_vmem, in_vmem],
        out_shape=(
            jax.ShapeDtypeStruct((3, OUT, HD), bf16),
            jax.ShapeDtypeStruct((SPAN, SPAN), bf16),
            jax.ShapeDtypeStruct((16, HD), f32),
        ),
        scratch_shapes=[
            pltpu.VMEM((4, OUT, HD), bf16),
            pltpu.VMEM((4, FLAT, HD), bf16),
            pltpu.VMEM((SEQ, SHARE), jnp.int32),
            pltpu.VMEM((SEQ, SHARE), jnp.int32),
            pltpu.VMEM((SEQ, SHARE), jnp.int32),
            pltpu.VMEM((ROWS, FLAT), bf16),
            pltpu.VMEM((4, KEPT, HD), bf16),
            pltpu.VMEM((2, ROWS, HD), bf16),
            pltpu.VMEM((ROWS, KEPT), f32),
            pltpu.VMEM((TILE, KEPT), f32),
            pltpu.VMEM((ROWS, 128), f32),
            pltpu.VMEM((SEQ, CHUNK, HD), bf16),
            pltpu.VMEM((2, SEQ, CHUNK, HD), bf16),
            pltpu.VMEM((MEMBERS, 2, 8, SHARE), f32),
            pltpu.VMEM((16, HD), f32),
            pltpu.VMEM((SEQ, 16, HD), f32),
            pltpu.VMEM((TARGETS, 16, HD), f32),
            pltpu.VMEM((16, HD), f32),
            pltpu.VMEM((8, 16, HD), f32),
            dma((2,)),
            dma((4,)),
            dma((4,)),
            dma((4, 3)),
            dma((4, 3)),
            dma((MEMBERS,)),
            dma((MEMBERS,)),
            dma((2,)),
            dma((2,)),
            dma((2,)),
            dma((8,)),
            dma((8,)),
        ],
        compiler_params=pltpu.CompilerParams(
            collective_id=0, has_side_effects=True, vmem_limit_bytes=VMEM_LIMIT
        ),
    )(listing, k, q, v, g, gain_q, gain_k)


def rows_kernel(back_ref, slots_ref, total_ref, q_ref, k_ref, v_ref, gain_q_ref, gain_k_ref):
    for i, ref in enumerate((q_ref, k_ref, v_ref)):
        for h in range(slots_ref.shape[1] // SPAN):
            rows = slots_ref[i, h * SPAN : (h + 1) * SPAN, :]
            rows = jnp.dot(back_ref[...], rows, preferred_element_type=jnp.float32)
            ref[0, :, h * HD : (h + 1) * HD] = rows.astype(jnp.bfloat16)
    gain_q_ref[...] = jnp.sum(total_ref[0:8, :], axis=0, keepdims=True)
    gain_k_ref[...] = jnp.sum(total_ref[8:16, :], axis=0, keepdims=True)


def to_rows(back, slots, total):
    width = HEAD_PART * HD
    parts = 2
    big = jax.ShapeDtypeStruct((1, SPAN, width), jnp.bfloat16)
    small = jax.ShapeDtypeStruct((1, HD), jnp.float32)
    return pl.pallas_call(
        rows_kernel,
        name="to_rows",
        grid=(parts,),
        in_specs=[
            pl.BlockSpec((SPAN, SPAN), lambda h: (0, 0)),
            pl.BlockSpec((3, OUT // parts, HD), lambda h: (0, h, 0)),
            pl.BlockSpec((16, HD), lambda h: (0, 0)),
        ],
        out_specs=[pl.BlockSpec((1, SPAN, width // parts), lambda h: (0, 0, h))] * 3
        + [pl.BlockSpec((1, HD), lambda h: (0, 0))] * 2,
        out_shape=(big, big, big, small, small),
        compiler_params=pltpu.CompilerParams(vmem_limit_bytes=VMEM_LIMIT),
        cost_estimate=pl.CostEstimate(flops=3 * 10**8, bytes_accessed=3 * 10**6, transcendentals=0),
    )(back, slots, total)


def on_device(q_raw, k_raw, v_raw, out_grad, gain_q, gain_k, keep_list):
    home, back, total = core(
        keep_list.reshape(SEQ, SHARE),
        k_raw[0],
        q_raw[0],
        v_raw[0],
        out_grad[0],
        gain_q.reshape(1, HD),
        gain_k.reshape(1, HD),
    )
    q_out, k_out, v_out, gain_q_grad, gain_k_grad = to_rows(back, home, total)
    return q_out, k_out, v_out, gain_q_grad.reshape(HD), gain_k_grad.reshape(HD)


def solution(mesh):
    big = P("dp", "seq", "tensor")
    return jax.shard_map(
        on_device,
        mesh=mesh,
        in_specs=(big, big, big, big, P(), P(), P("dp", None)),
        out_specs=(big, big, big, P(), P()),
        check_vma=False,
    )
```

```python
import math

import jax
import jax.numpy as jnp
from jax import lax
from jax.experimental import pallas as pl
from jax.experimental.pallas import tpu as pltpu
from jax.sharding import PartitionSpec as P

MESH = pl.DeviceIdType.MESH
HD = 128
EPSILON = 1e-06
SEQ = 32
SPAN = 256
SHARE = 128
SLOTS = 8
HEAD_PART = 6
UNITS = 8
ROWS = UNITS * SHARE
CHUNK = UNITS * SLOTS
MEMBERS = 4
TARGETS = HEAD_PART * MEMBERS
OUT = TARGETS * CHUNK
FLAT = SEQ * CHUNK
KEPT = SEQ * SHARE
TILE = 512
PART = TILE // SHARE * SLOTS
TILES = ROWS // TILE
SCALING = 1.0 / math.sqrt(HD)
LOG2E = 1.4426950408889634
VMEM_LIMIT = 56 * 1024 * 1024

NT = (((1,), (1,)), ((), ()))

def place(clip, i):
    head, quarter = i >> 2, i & 3
    third = (head * 11) >> 5
    pair = head - 3 * third
    odd = pair >> 1
    y = 2 * ((pair & 1) + odd * third) + (quarter >> 1)
    z = 4 * clip + 2 * third + odd
    return quarter & 1, y * 8 + z


def my_place(dp, s):
    y, z = s >> 3, s & 7
    third, odd, high = (z >> 1) & 1, z & 1, y >> 1
    pair = high + odd * (2 - high)
    active = (odd == 0) | (high == third)
    return z >> 2, (3 * third + pair) * 4 + 2 * (y & 1) + dp, active


def one_hot(hit):
    return jnp.where(hit, 1.0, 0.0).astype(jnp.bfloat16)


def inverse_norm(x):
    return lax.rsqrt(jnp.mean(x * x, axis=-1, keepdims=True) + EPSILON)


def norm_grads(raw, gain, upstream):
    raw = raw.astype(jnp.float32)
    inverse = inverse_norm(raw)
    scaled = upstream * gain
    inner = jnp.mean(scaled * raw, axis=-1, keepdims=True)
    grads = inverse * scaled - raw * (inverse * inverse * inverse * inner)
    terms = upstream * raw * inverse
    return grads, jnp.sum(terms.reshape(-1, 8, HD), axis=0)


def lane_fold(x, fold):
    parts = [x[:, i * 128 : (i + 1) * 128] for i in range(x.shape[1] // 128)]
    total = parts[0]
    for part in parts[1:]:
        total = fold(total, part)
    return total


def core_kernel(
    list_ref,
    k_ref,
    q_ref,
    v_ref,
    g_ref,
    gain_q_ref,
    gain_k_ref,
    home_ref,
    back_ref,
    total_ref,
    slots,
    arrived,
    enc_ref,
    other,
    codes,
    pick,
    full,
    raw,
    scores_ref,
    dots_ref,
    sums,
    q_slots,
    kv_slots,
    stats,
    terms,
    part_bytes,
    parts,
    partial,
    cross,
    enc_sem,
    route_send,
    route_recv,
    near_send,
    near_recv,
    stat_send,
    stat_recv,
    home_send,
    home_recv,
    part_sem,
    cross_send,
    cross_recv,
):
    dp, s, x = lax.axis_index("dp"), lax.axis_index("seq"), lax.axis_index("tensor")
    clip, seat, active = my_place(dp, s)
    me = seat & 3
    sibling = (1 - dp, s, x)
    corner = dp * 4 + x
    same = active & (clip == dp)

    first_target = jnp.where(same, seat, 3 * (s & 7) + 6 * (s >> 3))

    def nth_target(n):
        v = first_target + 7 * n
        return v - TARGETS * ((v * 171) >> 12)

    def nth_source(n):
        turn = n & 7
        away = ((turn + 1) >> 1) * (2 * (turn & 1) - 1)
        return (((s >> 3) + (n >> 3)) & 3) * 8 + (((s & 7) + away) & 7)

    def target(i):
        return place(dp, i) + (x,)

    def source(i):
        return (clip, i, x)

    def each(count, act, act_self=None):
        @pl.when(jnp.logical_not(same))
        def _():
            act(0)

        if act_self is not None:
            pl.when(same)(act_self)

        def step(n, _):
            act(n)
            return 0

        lax.fori_loop(1, count, step, 0, unroll=count - 1)

    def member(i):
        return (i & 1, (s & 23) + 8 * (i >> 1), x)

    def remote(src, dst, send_sem, recv_sem, device):
        return pltpu.make_async_remote_copy(
            src_ref=src, dst_ref=dst, send_sem=send_sem, recv_sem=recv_sem, device_id=device, device_id_type=MESH
        )


    barrier = pltpu.get_barrier_semaphore()

    def greet_device(there):
        pl.semaphore_signal(barrier, inc=1, device_id=there, device_id_type=MESH)

    @pl.when(active)
    def _():
        each(SEQ, lambda n: greet_device(source(nth_source(n))))
        for step in (1, 2, 3):
            greet_device(member(me ^ step))

    each(TARGETS, lambda n: greet_device(target(nth_target(n))))

    def at_corner(i):
        return (i >> 2, s, i & 3)

    for step in range(1, 8):
        greet_device(at_corner(corner ^ step))


    listing = list_ref[...]
    from_block = listing >> 8
    hits = one_hot(jnp.concatenate([from_block == i for i in range(SEQ)], axis=0))
    earlier = lax.broadcasted_iota(jnp.int32, (SHARE, SHARE), 0) < lax.broadcasted_iota(jnp.int32, (SHARE, SHARE), 1)
    counts = jnp.dot(hits, one_hot(earlier), preferred_element_type=jnp.float32) * hits.astype(jnp.float32)
    rank = counts[0:SEQ]
    for i in range(1, SEQ):
        rank += counts[i * SEQ : (i + 1) * SEQ]
    rank = rank.astype(jnp.int32)
    enc_ref[...] = from_block * SLOTS + rank
    slot = lax.broadcasted_iota(jnp.int32, (SEQ, SHARE), 0) * SLOTS + rank + 1
    slot = jnp.where(from_block == s, slot, 0).astype(jnp.float32)
    token = listing - s * SPAN
    token_iota = lax.broadcasted_iota(jnp.int32, (SPAN, SHARE), 0)
    found = jnp.zeros((SPAN, SHARE), jnp.float32)
    for j in range(SEQ):
        found += jnp.where(token_iota == token[j : j + 1], slot[j : j + 1], 0.0)
    found = jnp.sum(found, axis=1, keepdims=True) - 1.0
    row = jnp.broadcast_to(found, (SPAN, 128)).T[0:1]
    back_ref[...] = one_hot(lax.broadcasted_iota(jnp.int32, (SPAN, SPAN), 1).astype(jnp.float32) == found)
    take = one_hot(lax.broadcasted_iota(jnp.int32, (SPAN, SPAN), 0).astype(jnp.float32) == row)
    step = 512

    def to_slots(i, ref):
        rows = jnp.dot(take, ref[...], preferred_element_type=jnp.float32).astype(jnp.bfloat16)
        for h in range(HEAD_PART):
            slots[i, h * SPAN : (h + 1) * SPAN, :] = rows[:, h * HD : (h + 1) * HD]

    def chunk(ref, a, i):
        return ref.at[a, pl.ds(pl.multiple_of(i * CHUNK, 16), CHUNK), :]

    def route(a):
        def start(n):
            i = nth_target(n)
            there = target(i)
            remote(chunk(slots, a, i), chunk(arrived, a, s), route_send.at[a], route_recv.at[a], there).start()

        def start_self():
            pltpu.make_async_copy(chunk(slots, a, seat), chunk(arrived, a, s), route_recv.at[a]).start()

        each(TARGETS, start, start_self)

    def rows_of(a, i):
        return full.at[a, pl.ds(pl.multiple_of(i * ROWS, ROWS), ROWS), :]

    to_slots(0, k_ref)
    arrivals = jnp.where(active, SEQ + 3, 0) - jnp.where(same, 2, 0)
    pl.semaphore_wait(barrier, TARGETS + 7 + arrivals)
    exchange = remote(enc_ref, other, enc_sem.at[0], enc_sem.at[1], sibling)

    @pl.when(active)
    def _():
        exchange.start()

    route(0)
    to_slots(1, q_ref)
    route(1)
    to_slots(2, v_ref)
    to_slots(3, g_ref)


    def unit_codes(u):
        return codes[pl.ds(UNITS * me + u, 1), :]

    def build_pick():
        exchange.wait()
        codes[...] = jnp.where(clip == dp, enc_ref[...], other[...])
        wide_iota = lax.broadcasted_iota(jnp.int32, (SHARE, 128), 1).astype(jnp.float32)
        for u in range(UNITS):
            code = unit_codes(u)
            code = (code >> 3) * CHUNK + u * SLOTS + (code & 7)
            wide = jnp.broadcast_to(code.astype(jnp.float32), (SHARE, 128)).T
            for c in range(FLAT // 128):
                pick[u * SHARE : (u + 1) * SHARE, c * 128 : (c + 1) * 128] = one_hot(wide == wide_iota + c * 128.0)


    def near(a, way, rows, there):
        return remote(rows_of(a, rows), rows_of(a, rows), near_send.at[a, way], near_recv.at[a, way], member(there))

    def gather_pass(a):
        near(a, 0, me ^ 2, me).wait_recv()
        near(a, 2, me ^ 2, me ^ 1).start()

    def gather_finish(a):
        near(a, 1, me ^ 1, me).wait_recv()
        near(a, 2, me ^ 3, me).wait_recv()

    def gather_sent(a):
        near(a, 0, me, me ^ 2).wait_send()
        near(a, 1, me, me ^ 1).wait_send()
        near(a, 2, me ^ 2, me ^ 1).wait_send()

    own_rows = pl.ds(pl.multiple_of(me * ROWS, 256), ROWS)

    def to_dense(a):
        remote(arrived.at[a], arrived.at[a], route_send.at[a], route_recv.at[a], sibling).wait_recv()
        rows = jnp.dot(pick[...], arrived[a], preferred_element_type=jnp.float32)
        if a < 2:
            raw[a] = rows.astype(jnp.bfloat16)
            gain = (gain_k_ref, gain_q_ref)[a][...]
            rows = rows * inverse_norm(rows) * gain
        full[a, own_rows, :] = rows.astype(jnp.bfloat16)
        near(a, 0, me, me ^ 2).start()
        near(a, 1, me, me ^ 1).start()


    chunks = [slice(i * step, (i + 1) * step) for i in range(KEPT // step)]

    def head_rows(a, cols):
        return full[a, cols, :]

    def tile_rows(a, t):
        return full[a, pl.ds(pl.multiple_of(me * ROWS + t * TILE, TILE), TILE), :]

    def local_rows(t):
        return pl.ds(pl.multiple_of(t * TILE, TILE), TILE)

    def store_stat(i, t, value):
        wide = jnp.broadcast_to(value, (TILE, 128)).T
        for j in range(TILE // SHARE):
            stats[me, i, pl.ds(TILE // SHARE * t + j, 1), :] = wide[0:1, j * SHARE : (j + 1) * SHARE]

    def score_tile(t, _):
        query = tile_rows(1, t)
        rows = local_rows(t)
        top = None
        for cols in chunks:
            scores = lax.dot_general(query, head_rows(0, cols), NT, preferred_element_type=jnp.float32)
            scores = scores * (SCALING * LOG2E)
            scores_ref[rows, cols] = scores
            part = lane_fold(scores, jnp.maximum)
            top = part if top is None else jnp.maximum(top, part)
        top = jnp.max(top, axis=-1, keepdims=True)
        total = jnp.zeros((TILE, 128), jnp.float32)
        for cols in chunks:
            weights = jnp.exp2(scores_ref[rows, cols] - top)
            scores_ref[rows, cols] = weights
            total += lane_fold(weights, jnp.add)
        total = jnp.sum(total, axis=-1, keepdims=True)
        sums[rows, :] = jnp.broadcast_to(total, (TILE, 128))
        store_stat(0, t, top + jnp.log2(total))

        return 0

    def spread_tile(t, rows):
        tile_iota = lax.broadcasted_iota(jnp.int32, (SEQ * PART, TILE), 0)
        tile_codes = []
        for j in range(TILE // SHARE):
            code = unit_codes(TILE // SHARE * t + j)
            tile_codes.append((code >> 3) * PART + j * SLOTS + (code & 7))
        spread = one_hot(tile_iota == jnp.concatenate(tile_codes, axis=1))
        rows = jnp.dot(spread, rows.astype(jnp.bfloat16), preferred_element_type=jnp.float32)
        return rows.astype(jnp.bfloat16).reshape(SEQ, PART, HD)

    def part_of(t):
        return pl.ds(pl.multiple_of(t * PART, PART), PART)

    def query_tile(t, _):
        grad = tile_rows(3, t)
        rows = local_rows(t)
        weighted = jnp.zeros((TILE, 128), jnp.float32)
        for cols in chunks:
            dots = lax.dot_general(grad, head_rows(2, cols), NT, preferred_element_type=jnp.float32)
            dots_ref[:, cols] = dots
            weighted += lane_fold(scores_ref[rows, cols] * dots, jnp.add)
        share = 1.0 / sums[rows, 0:1]
        delta = jnp.sum(weighted, axis=-1, keepdims=True) * share
        result = jnp.zeros((TILE, HD), jnp.float32)
        for cols in chunks:
            dscore = (scores_ref[rows, cols] * share) * (dots_ref[:, cols] - delta)
            result += jnp.dot(dscore.astype(jnp.bfloat16), head_rows(0, cols), preferred_element_type=jnp.float32)
        grads, term = norm_grads(raw[1, rows, :], gain_q_ref[...], result * SCALING)
        terms[0:8, :] += term
        store_stat(1, t, delta)

        q_slots[:, part_of(t), :] = spread_tile(t, grads)
        return 0


    def stat_copy(rows, there):
        return remote(stats.at[rows], stats.at[rows], stat_send.at[there], stat_recv.at[rows], member(there))

    def stat_start():
        for step in (1, 2, 3):
            stat_copy(me, me ^ step).start()

    def stat_finish():
        for step in (1, 2, 3):
            stat_copy(me ^ step, me ^ step).wait_recv()
            stat_copy(me, me ^ step).wait_send()


    def home_rows(t):
        return pl.ds(pl.multiple_of(seat * CHUNK + t * PART, PART), PART)

    def q_home(i):
        return q_slots.at[i], home_ref.at[0, pl.ds(pl.multiple_of(seat * CHUNK, CHUNK), CHUNK), :]

    def kv_home(t, i):
        return kv_slots.at[:, i, part_of(t), :], home_ref.at[1:3, home_rows(t), :]

    def send_home(copies, sem):
        def start(n):
            i = nth_source(n)
            src, dst = copies(i)
            remote(src, dst, home_send.at[sem], home_recv.at[sem], source(i)).start()

        def start_self():
            src, dst = copies(s)
            pltpu.make_async_copy(src, dst, home_recv.at[sem]).start()

        each(SEQ, start, start_self)


    def stat_row(i, cols):
        units = range(cols.start // SHARE, cols.stop // SHARE)
        return jnp.concatenate([stats[u // UNITS, i, u % UNITS : u % UNITS + 1, :] for u in units], axis=1)

    def key_tile(t, _):
        key, value = tile_rows(0, t), tile_rows(2, t)
        key_grad = jnp.zeros((TILE, HD), jnp.float32)
        value_grad = jnp.zeros((TILE, HD), jnp.float32)
        for cols in chunks:
            query, grad = head_rows(1, cols), head_rows(3, cols)
            scores = lax.dot_general(key, query, NT, preferred_element_type=jnp.float32)
            weights = jnp.exp2(scores * (SCALING * LOG2E) - stat_row(0, cols))
            dots = lax.dot_general(value, grad, NT, preferred_element_type=jnp.float32)
            dscore = weights * (dots - stat_row(1, cols))
            key_grad += jnp.dot(dscore.astype(jnp.bfloat16), query, preferred_element_type=jnp.float32)
            value_grad += jnp.dot(weights.astype(jnp.bfloat16), grad, preferred_element_type=jnp.float32)
        grads, term = norm_grads(raw[0, local_rows(t), :], gain_k_ref[...], key_grad * SCALING)
        terms[8:16, :] += term
        for i, result in enumerate((grads, value_grad)):
            kv_slots[i, :, part_of(t), :] = spread_tile(t, result)
        send_home(lambda i: kv_home(t, i), 1)
        return 0


    def part_start(n):
        remote(terms, parts.at[seat], part_sem.at[0], part_sem.at[1], source(nth_source(n))).start()

    def part_self():
        pltpu.make_async_copy(terms, parts.at[seat], part_sem.at[1]).start()

    @pl.when(active)
    def _():
        build_pick()
        to_dense(0)

    route(2)

    @pl.when(active)
    def _():
        to_dense(1)

    route(3)

    @pl.when(active)
    def _():
        terms[...] = jnp.zeros_like(terms)
        gather_pass(0)
        gather_finish(0)
        lax.fori_loop(0, TILES // 2, score_tile, 0)
        to_dense(2)
        gather_pass(1)
        lax.fori_loop(TILES // 2, TILES, score_tile, 0)
        gather_pass(2)
        to_dense(3)
        gather_finish(2)
        lax.fori_loop(0, TILES, query_tile, 0)
        stat_start()
        gather_pass(3)
        send_home(q_home, 0)
        gather_finish(1)
        gather_finish(3)
        stat_finish()
        lax.fori_loop(0, TILES, key_tile, 0)
        each(SEQ, part_start, part_self)

    remote(parts, parts, part_sem.at[0], part_sem.at[1], sibling).wait_recv()
    partial[...] = jnp.sum(parts[...], axis=0)

    def cross_copy(i, dst):
        return remote(partial, cross.at[dst], cross_send.at[i], cross_recv.at[dst], at_corner(i))

    cross[pl.ds(corner, 1)] = partial[...][None]
    for step in range(1, 8):
        cross_copy(corner ^ step, corner).start()
    for step in range(1, 8):
        cross_copy(corner ^ step, corner ^ step).wait_recv()
        cross_copy(corner ^ step, corner).wait_send()
    total_ref[...] = jnp.sum(cross[...], axis=0)


    def sent(targets, sources):
        for a in range(4):
            rows = slots.at[a, 0 : targets * CHUNK, :]
            remote(rows, rows, route_send.at[a], route_recv.at[a], sibling).wait_send()
        if sources:
            for a in range(4):
                gather_sent(a)
            rows = q_slots.at[0:sources]
            remote(rows, rows, home_send.at[0], home_recv.at[0], sibling).wait_send()
            rows = kv_slots.at[:, 0:sources]
            remote(rows, rows, home_send.at[1], home_recv.at[1], sibling).wait_send()
            rows = part_bytes.at[0:sources]
            remote(rows, rows, part_sem.at[0], part_sem.at[1], sibling).wait_send()

    @pl.when(same)
    def _():
        sent(TARGETS - 1, SEQ - 1)

    @pl.when(active & jnp.logical_not(same))
    def _():
        sent(TARGETS, SEQ)

    @pl.when(jnp.logical_not(active))
    def _():
        sent(TARGETS, 0)

    remote(home_ref.at[0], home_ref.at[0], home_send.at[0], home_recv.at[0], sibling).wait_recv()
    remote(home_ref.at[1:3], home_ref.at[1:3], home_send.at[1], home_recv.at[1], sibling).wait_recv()


def core(listing, k, q, v, g, gain_q, gain_k):
    bf16, f32 = jnp.bfloat16, jnp.float32
    dma = pltpu.SemaphoreType.DMA
    in_vmem = pl.BlockSpec(memory_space=pltpu.VMEM)
    return pl.pallas_call(
        core_kernel,
        name="core",
        in_specs=[in_vmem] * 7,
        out_specs=[pl.BlockSpec(memory_space=pl.ANY), in_vmem, in_vmem],
        out_shape=(
            jax.ShapeDtypeStruct((3, OUT, HD), bf16),
            jax.ShapeDtypeStruct((SPAN, SPAN), bf16),
            jax.ShapeDtypeStruct((16, HD), f32),
        ),
        scratch_shapes=[
            pltpu.VMEM((4, OUT, HD), bf16),
            pltpu.VMEM((4, FLAT, HD), bf16),
            pltpu.VMEM((SEQ, SHARE), jnp.int32),
            pltpu.VMEM((SEQ, SHARE), jnp.int32),
            pltpu.VMEM((SEQ, SHARE), jnp.int32),
            pltpu.VMEM((ROWS, FLAT), bf16),
            pltpu.VMEM((4, KEPT, HD), bf16),
            pltpu.VMEM((2, ROWS, HD), bf16),
            pltpu.VMEM((ROWS, KEPT), f32),
            pltpu.VMEM((TILE, KEPT), f32),
            pltpu.VMEM((ROWS, 128), f32),
            pltpu.VMEM((SEQ, CHUNK, HD), bf16),
            pltpu.VMEM((2, SEQ, CHUNK, HD), bf16),
            pltpu.VMEM((MEMBERS, 2, 8, SHARE), f32),
            pltpu.VMEM((16, HD), f32),
            pltpu.VMEM((SEQ, 16, HD), f32),
            pltpu.VMEM((TARGETS, 16, HD), f32),
            pltpu.VMEM((16, HD), f32),
            pltpu.VMEM((8, 16, HD), f32),
            dma((2,)),
            dma((4,)),
            dma((4,)),
            dma((4, 3)),
            dma((4, 3)),
            dma((MEMBERS,)),
            dma((MEMBERS,)),
            dma((2,)),
            dma((2,)),
            dma((2,)),
            dma((8,)),
            dma((8,)),
        ],
        compiler_params=pltpu.CompilerParams(
            collective_id=0, has_side_effects=True, vmem_limit_bytes=VMEM_LIMIT
        ),
    )(listing, k, q, v, g, gain_q, gain_k)


def rows_kernel(back_ref, slots_ref, total_ref, q_ref, k_ref, v_ref, gain_q_ref, gain_k_ref):
    for i, ref in enumerate((q_ref, k_ref, v_ref)):
        for h in range(slots_ref.shape[1] // SPAN):
            rows = slots_ref[i, h * SPAN : (h + 1) * SPAN, :]
            rows = jnp.dot(back_ref[...], rows, preferred_element_type=jnp.float32)
            ref[0, :, h * HD : (h + 1) * HD] = rows.astype(jnp.bfloat16)
    gain_q_ref[...] = jnp.sum(total_ref[0:8, :], axis=0, keepdims=True)
    gain_k_ref[...] = jnp.sum(total_ref[8:16, :], axis=0, keepdims=True)


def to_rows(back, slots, total):
    width = HEAD_PART * HD
    parts = 2
    big = jax.ShapeDtypeStruct((1, SPAN, width), jnp.bfloat16)
    small = jax.ShapeDtypeStruct((1, HD), jnp.float32)
    return pl.pallas_call(
        rows_kernel,
        name="to_rows",
        grid=(parts,),
        in_specs=[
            pl.BlockSpec((SPAN, SPAN), lambda h: (0, 0)),
            pl.BlockSpec((3, OUT // parts, HD), lambda h: (0, h, 0)),
            pl.BlockSpec((16, HD), lambda h: (0, 0)),
        ],
        out_specs=[pl.BlockSpec((1, SPAN, width // parts), lambda h: (0, 0, h))] * 3
        + [pl.BlockSpec((1, HD), lambda h: (0, 0))] * 2,
        out_shape=(big, big, big, small, small),
        compiler_params=pltpu.CompilerParams(vmem_limit_bytes=VMEM_LIMIT),
        cost_estimate=pl.CostEstimate(flops=3 * 10**8, bytes_accessed=3 * 10**6, transcendentals=0),
    )(back, slots, total)


def on_device(q_raw, k_raw, v_raw, out_grad, gain_q, gain_k, keep_list):
    home, back, total = core(
        keep_list.reshape(SEQ, SHARE),
        k_raw[0],
        q_raw[0],
        v_raw[0],
        out_grad[0],
        gain_q.reshape(1, HD),
        gain_k.reshape(1, HD),
    )
    q_out, k_out, v_out, gain_q_grad, gain_k_grad = to_rows(back, home, total)
    return q_out, k_out, v_out, gain_q_grad.reshape(HD), gain_k_grad.reshape(HD)


def solution(mesh):
    big = P("dp", "seq", "tensor")
    return jax.shard_map(
        on_device,
        mesh=mesh,
        in_specs=(big, big, big, big, P(), P(), P("dp", None)),
        out_specs=(big, big, big, P(), P()),
        check_vma=False,
    )
```

```python
import math

import jax
import jax.numpy as jnp
from jax import lax
from jax.experimental import pallas as pl
from jax.experimental.pallas import tpu as pltpu
from jax.sharding import PartitionSpec as P

MESH = pl.DeviceIdType.MESH
HD = 128
EPSILON = 1e-06
SEQ = 32
SPAN = 256
SHARE = 128
SLOTS = 8
HEAD_PART = 6
UNITS = 8
ROWS = UNITS * SHARE
CHUNK = UNITS * SLOTS
MEMBERS = 4
TARGETS = HEAD_PART * MEMBERS
FLAT = SEQ * CHUNK
KEPT = SEQ * SHARE
TILE = 512
PART = TILE // SHARE * SLOTS
TILES = ROWS // TILE
SCALING = 1.0 / math.sqrt(HD)
LOG2E = 1.4426950408889634
VMEM_LIMIT = 56 * 1024 * 1024

NT = (((1,), (1,)), ((), ()))

def place(clip, i):
    head, quarter = i >> 2, i & 3
    third = (head * 11) >> 5
    pair = head - 3 * third
    odd = pair >> 1
    y = 2 * ((pair & 1) + odd * third) + (quarter >> 1)
    z = 4 * clip + 2 * third + odd
    return quarter & 1, y * 8 + z


def my_place(dp, s):
    y, z = s >> 3, s & 7
    third, odd, high = (z >> 1) & 1, z & 1, y >> 1
    pair = high + odd * (2 - high)
    active = (odd == 0) | (high == third)
    return z >> 2, (3 * third + pair) * 4 + 2 * (y & 1) + dp, active


def one_hot(hit):
    return jnp.where(hit, 1.0, 0.0).astype(jnp.bfloat16)


def inverse_norm(x):
    return lax.rsqrt(jnp.mean(x * x, axis=-1, keepdims=True) + EPSILON)


def norm_grads(raw, gain, upstream):
    raw = raw.astype(jnp.float32)
    inverse = inverse_norm(raw)
    scaled = upstream * gain
    inner = jnp.mean(scaled * raw, axis=-1, keepdims=True)
    grads = inverse * scaled - raw * (inverse * inverse * inverse * inner)
    terms = upstream * raw * inverse
    return grads, jnp.sum(terms.reshape(-1, 8, HD), axis=0)


def lane_fold(x, fold):
    parts = [x[:, i * 128 : (i + 1) * 128] for i in range(x.shape[1] // 128)]
    total = parts[0]
    for part in parts[1:]:
        total = fold(total, part)
    return total


def core_kernel(
    list_ref,
    k_ref,
    q_ref,
    v_ref,
    g_ref,
    gain_q_ref,
    gain_k_ref,
    home_q_ref,
    home_kv_ref,
    back_ref,
    total_ref,
    slots_kq,
    slots_v,
    slots_g,
    arrived_kq,
    arrived_v,
    arrived_g,
    enc_ref,
    other,
    codes,
    pick,
    full,
    raw,
    scores_ref,
    dots_ref,
    sums,
    q_slots,
    kv_slots,
    stats,
    terms,
    part_bytes,
    parts,
    partial,
    cross,
    enc_sem,
    route_send,
    route_recv,
    near_send,
    near_recv,
    stat_send,
    stat_recv,
    home_send,
    home_recv,
    part_sem,
    cross_send,
    cross_recv,
):
    dp, s, x = lax.axis_index("dp"), lax.axis_index("seq"), lax.axis_index("tensor")
    clip, seat, active = my_place(dp, s)
    me = seat & 3
    sibling = (1 - dp, s, x)
    corner = dp * 4 + x
    same = active & (clip == dp)

    first_target = jnp.where(same, seat, 3 * (s & 7) + 6 * (s >> 3))

    def nth_target(n):
        v = first_target + 7 * n
        return v - TARGETS * ((v * 171) >> 12)

    def nth_source(n):
        turn = n & 7
        away = ((turn + 1) >> 1) * (2 * (turn & 1) - 1)
        return (((s >> 3) + (n >> 3)) & 3) * 8 + (((s & 7) + away) & 7)

    def target(i):
        return place(dp, i) + (x,)

    def source(i):
        return (clip, i, x)

    def each(count, act, act_self=None):
        @pl.when(jnp.logical_not(same))
        def _():
            act(0)

        if act_self is not None:
            pl.when(same)(act_self)

        def step(n, _):
            act(n)
            return 0

        lax.fori_loop(1, count, step, 0)

    def member(i):
        return (i & 1, (s & 23) + 8 * (i >> 1), x)

    def remote(src, dst, send_sem, recv_sem, device):
        return pltpu.make_async_remote_copy(
            src_ref=src, dst_ref=dst, send_sem=send_sem, recv_sem=recv_sem, device_id=device, device_id_type=MESH
        )


    barrier = pltpu.get_barrier_semaphore()

    def greet_device(there):
        pl.semaphore_signal(barrier, inc=1, device_id=there, device_id_type=MESH)

    @pl.when(active)
    def _():
        each(SEQ, lambda n: greet_device(source(nth_source(n))))
        for step in (1, 2, 3):
            greet_device(member(me ^ step))

    each(TARGETS, lambda n: greet_device(target(nth_target(n))))

    def at_corner(i):
        return (i >> 2, s, i & 3)

    for step in range(1, 8):
        greet_device(at_corner(corner ^ step))


    listing = list_ref[...]
    from_block = listing >> 8
    hits = one_hot(jnp.concatenate([from_block == i for i in range(SEQ)], axis=0))
    earlier = lax.broadcasted_iota(jnp.int32, (SHARE, SHARE), 0) < lax.broadcasted_iota(jnp.int32, (SHARE, SHARE), 1)
    counts = jnp.dot(hits, one_hot(earlier), preferred_element_type=jnp.float32) * hits.astype(jnp.float32)
    rank = counts[0:SEQ]
    for i in range(1, SEQ):
        rank += counts[i * SEQ : (i + 1) * SEQ]
    rank = rank.astype(jnp.int32)
    enc_ref[...] = from_block * SLOTS + rank
    slot = lax.broadcasted_iota(jnp.int32, (SEQ, SHARE), 0) * SLOTS + rank + 1
    slot = jnp.where(from_block == s, slot, 0).astype(jnp.float32)
    token = listing - s * SPAN
    token_iota = lax.broadcasted_iota(jnp.int32, (SPAN, SHARE), 0)
    found = jnp.zeros((SPAN, SHARE), jnp.float32)
    for j in range(SEQ):
        found += jnp.where(token_iota == token[j : j + 1], slot[j : j + 1], 0.0)
    found = jnp.sum(found, axis=1, keepdims=True) - 1.0
    row = jnp.broadcast_to(found, (SPAN, 128)).T[0:1]
    back_ref[...] = one_hot(lax.broadcasted_iota(jnp.int32, (SPAN, SPAN), 1).astype(jnp.float32) == found)
    take = one_hot(lax.broadcasted_iota(jnp.int32, (SPAN, SPAN), 0).astype(jnp.float32) == row)
    step = 512

    slots = (slots_kq, slots_v, slots_g)
    arrived = (arrived_kq, arrived_v, arrived_g)

    def to_slots(part, i, ref):
        rows = jnp.dot(take, ref[...], preferred_element_type=jnp.float32).astype(jnp.bfloat16)
        for h in range(HEAD_PART):
            quarters = rows[:, h * HD : (h + 1) * HD].reshape(MEMBERS, CHUNK, HD)
            slots[part][h * MEMBERS : (h + 1) * MEMBERS, i] = quarters

    def route(part):
        def start(n):
            i = nth_target(n)
            src, dst = slots[part].at[i], arrived[part].at[s]
            remote(src, dst, route_send.at[part], route_recv.at[part], target(i)).start()

        def start_self():
            pltpu.make_async_copy(slots[part].at[seat], arrived[part].at[s], route_recv.at[part]).start()

        each(TARGETS, start, start_self)

    def arrive(part):
        remote(arrived[part], arrived[part], route_send.at[part], route_recv.at[part], sibling).wait_recv()

    def rows_of(a, i):
        return full.at[a, pl.ds(pl.multiple_of(i * ROWS, ROWS), ROWS), :]

    to_slots(0, 0, k_ref)
    to_slots(0, 1, q_ref)
    arrivals = jnp.where(active, SEQ + 3, 0) - jnp.where(same, 2, 0)
    pl.semaphore_wait(barrier, TARGETS + 7 + arrivals)
    exchange = remote(enc_ref, other, enc_sem.at[0], enc_sem.at[1], sibling)

    @pl.when(active)
    def _():
        exchange.start()

    route(0)
    to_slots(1, 0, v_ref)
    route(1)
    to_slots(2, 0, g_ref)


    def unit_codes(u):
        return codes[pl.ds(UNITS * me + u, 1), :]

    def build_pick():
        exchange.wait()
        codes[...] = jnp.where(clip == dp, enc_ref[...], other[...])
        wide_iota = lax.broadcasted_iota(jnp.int32, (SHARE, 128), 1).astype(jnp.float32)
        for u in range(UNITS):
            code = unit_codes(u)
            code = (code >> 3) * CHUNK + u * SLOTS + (code & 7)
            wide = jnp.broadcast_to(code.astype(jnp.float32), (SHARE, 128)).T
            for c in range(FLAT // 128):
                pick[u * SHARE : (u + 1) * SHARE, c * 128 : (c + 1) * 128] = one_hot(wide == wide_iota + c * 128.0)


    def near(a, way, rows, there):
        return remote(rows_of(a, rows), rows_of(a, rows), near_send.at[a, way], near_recv.at[a, way], member(there))

    def gather_pass(a):
        near(a, 0, me ^ 2, me).wait_recv()
        near(a, 2, me ^ 2, me ^ 1).start()

    def gather_finish(a):
        near(a, 1, me ^ 1, me).wait_recv()
        near(a, 2, me ^ 3, me).wait_recv()

    def gather_sent(a):
        near(a, 0, me, me ^ 2).wait_send()
        near(a, 1, me, me ^ 1).wait_send()
        near(a, 2, me ^ 2, me ^ 1).wait_send()

    own_rows = pl.ds(pl.multiple_of(me * ROWS, 256), ROWS)

    def to_dense(a):
        part, i = ((0, 0), (0, 1), (1, 0), (2, 0))[a]
        rows = arrived[part][:, i].reshape(FLAT, HD)
        rows = jnp.dot(pick[...], rows, preferred_element_type=jnp.float32)
        if a < 2:
            raw[a] = rows.astype(jnp.bfloat16)
            gain = (gain_k_ref, gain_q_ref)[a][...]
            rows = rows * inverse_norm(rows) * gain
        full[a, own_rows, :] = rows.astype(jnp.bfloat16)
        near(a, 0, me, me ^ 2).start()
        near(a, 1, me, me ^ 1).start()


    chunks = [slice(i * step, (i + 1) * step) for i in range(KEPT // step)]

    def head_rows(a, cols):
        return full[a, cols, :]

    def tile_rows(a, t):
        return full[a, pl.ds(pl.multiple_of(me * ROWS + t * TILE, TILE), TILE), :]

    def local_rows(t):
        return pl.ds(pl.multiple_of(t * TILE, TILE), TILE)

    def store_stat(i, t, value):
        wide = jnp.broadcast_to(value, (TILE, 128)).T
        for j in range(TILE // SHARE):
            stats[me, i, pl.ds(TILE // SHARE * t + j, 1), :] = wide[0:1, j * SHARE : (j + 1) * SHARE]

    def score_tile(t, _):
        query = tile_rows(1, t)
        rows = local_rows(t)
        top = None
        for cols in chunks:
            scores = lax.dot_general(query, head_rows(0, cols), NT, preferred_element_type=jnp.float32)
            scores = scores * (SCALING * LOG2E)
            scores_ref[rows, cols] = scores
            part = lane_fold(scores, jnp.maximum)
            top = part if top is None else jnp.maximum(top, part)
        top = jnp.max(top, axis=-1, keepdims=True)
        total = jnp.zeros((TILE, 128), jnp.float32)
        for cols in chunks:
            weights = jnp.exp2(scores_ref[rows, cols] - top)
            scores_ref[rows, cols] = weights
            total += lane_fold(weights, jnp.add)
        total = jnp.sum(total, axis=-1, keepdims=True)
        sums[rows, :] = jnp.broadcast_to(total, (TILE, 128))
        store_stat(0, t, top + jnp.log2(total))

        return 0

    def spread_tile(t, rows):
        tile_iota = lax.broadcasted_iota(jnp.int32, (SEQ * PART, TILE), 0)
        tile_codes = []
        for j in range(TILE // SHARE):
            code = unit_codes(TILE // SHARE * t + j)
            tile_codes.append((code >> 3) * PART + j * SLOTS + (code & 7))
        spread = one_hot(tile_iota == jnp.concatenate(tile_codes, axis=1))
        rows = jnp.dot(spread, rows.astype(jnp.bfloat16), preferred_element_type=jnp.float32)
        return rows.astype(jnp.bfloat16).reshape(SEQ, PART, HD)

    def part_of(t):
        return pl.ds(pl.multiple_of(t * PART, PART), PART)

    def query_tile(t, _):
        grad = tile_rows(3, t)
        rows = local_rows(t)
        weighted = jnp.zeros((TILE, 128), jnp.float32)
        for cols in chunks:
            dots = lax.dot_general(grad, head_rows(2, cols), NT, preferred_element_type=jnp.float32)
            dots_ref[:, cols] = dots
            weighted += lane_fold(scores_ref[rows, cols] * dots, jnp.add)
        share = 1.0 / sums[rows, 0:1]
        delta = jnp.sum(weighted, axis=-1, keepdims=True) * share
        result = jnp.zeros((TILE, HD), jnp.float32)
        for cols in chunks:
            dscore = (scores_ref[rows, cols] * share) * (dots_ref[:, cols] - delta)
            result += jnp.dot(dscore.astype(jnp.bfloat16), head_rows(0, cols), preferred_element_type=jnp.float32)
        grads, term = norm_grads(raw[1, rows, :], gain_q_ref[...], result * SCALING)
        terms[0:8, :] += term
        store_stat(1, t, delta)

        q_slots[:, part_of(t), :] = spread_tile(t, grads)
        return 0


    def stat_copy(rows, there):
        return remote(stats.at[rows], stats.at[rows], stat_send.at[there], stat_recv.at[rows], member(there))

    def stat_start():
        for step in (1, 2, 3):
            stat_copy(me, me ^ step).start()

    def stat_finish():
        for step in (1, 2, 3):
            stat_copy(me ^ step, me ^ step).wait_recv()
            stat_copy(me, me ^ step).wait_send()


    def q_home(i):
        return q_slots.at[i], home_q_ref.at[seat]

    def kv_home(t, i):
        return kv_slots.at[t, i], home_kv_ref.at[seat, t]

    def send_home(copies, sem):
        def start(n):
            i = nth_source(n)
            src, dst = copies(i)
            remote(src, dst, home_send.at[sem], home_recv.at[sem], source(i)).start()

        def start_self():
            src, dst = copies(s)
            pltpu.make_async_copy(src, dst, home_recv.at[sem]).start()

        each(SEQ, start, start_self)


    def stat_row(i, cols):
        units = range(cols.start // SHARE, cols.stop // SHARE)
        return jnp.concatenate([stats[u // UNITS, i, u % UNITS : u % UNITS + 1, :] for u in units], axis=1)

    def key_tile(t, _):
        key, value = tile_rows(0, t), tile_rows(2, t)
        key_grad = jnp.zeros((TILE, HD), jnp.float32)
        value_grad = jnp.zeros((TILE, HD), jnp.float32)
        for cols in chunks:
            query, grad = head_rows(1, cols), head_rows(3, cols)
            scores = lax.dot_general(key, query, NT, preferred_element_type=jnp.float32)
            weights = jnp.exp2(scores * (SCALING * LOG2E) - stat_row(0, cols))
            dots = lax.dot_general(value, grad, NT, preferred_element_type=jnp.float32)
            dscore = weights * (dots - stat_row(1, cols))
            key_grad += jnp.dot(dscore.astype(jnp.bfloat16), query, preferred_element_type=jnp.float32)
            value_grad += jnp.dot(weights.astype(jnp.bfloat16), grad, preferred_element_type=jnp.float32)
        grads, term = norm_grads(raw[0, local_rows(t), :], gain_k_ref[...], key_grad * SCALING)
        terms[8:16, :] += term
        for i, result in enumerate((grads, value_grad)):
            kv_slots[t, :, i] = spread_tile(t, result)
        send_home(lambda i: kv_home(t, i), 1)
        return 0


    def part_start(n):
        remote(terms, parts.at[seat], part_sem.at[0], part_sem.at[1], source(nth_source(n))).start()

    def part_self():
        pltpu.make_async_copy(terms, parts.at[seat], part_sem.at[1]).start()

    @pl.when(active)
    def _():
        build_pick()
        arrive(0)
        to_dense(0)

    route(2)

    @pl.when(active)
    def _():
        terms[...] = jnp.zeros_like(terms)
        to_dense(1)
        gather_pass(0)
        gather_finish(0)
        lax.fori_loop(0, TILES // 2, score_tile, 0)
        arrive(1)
        to_dense(2)
        gather_pass(1)
        lax.fori_loop(TILES // 2, TILES, score_tile, 0)
        gather_pass(2)
        arrive(2)
        to_dense(3)
        gather_finish(2)
        lax.fori_loop(0, TILES, query_tile, 0)
        stat_start()
        gather_pass(3)
        send_home(q_home, 0)
        gather_finish(1)
        gather_finish(3)
        stat_finish()
        lax.fori_loop(0, TILES, key_tile, 0)
        each(SEQ, part_start, part_self)

    remote(parts, parts, part_sem.at[0], part_sem.at[1], sibling).wait_recv()
    partial[...] = jnp.sum(parts[...], axis=0)

    def cross_copy(i, dst):
        return remote(partial, cross.at[dst], cross_send.at[i], cross_recv.at[dst], at_corner(i))

    cross[pl.ds(corner, 1)] = partial[...][None]
    for step in range(1, 8):
        cross_copy(corner ^ step, corner).start()
    for step in range(1, 8):
        cross_copy(corner ^ step, corner ^ step).wait_recv()
        cross_copy(corner ^ step, corner).wait_send()
    total_ref[...] = jnp.sum(cross[...], axis=0)


    def sent(targets, sources):
        for part in range(3):
            rows = slots[part].at[0:targets]
            remote(rows, rows, route_send.at[part], route_recv.at[part], sibling).wait_send()
        if sources:
            for a in range(4):
                gather_sent(a)
            rows = q_slots.at[0:sources]
            remote(rows, rows, home_send.at[0], home_recv.at[0], sibling).wait_send()
            rows = kv_slots.at[:, 0:sources]
            remote(rows, rows, home_send.at[1], home_recv.at[1], sibling).wait_send()
            rows = part_bytes.at[0:sources]
            remote(rows, rows, part_sem.at[0], part_sem.at[1], sibling).wait_send()

    @pl.when(same)
    def _():
        sent(TARGETS - 1, SEQ - 1)

    @pl.when(active & jnp.logical_not(same))
    def _():
        sent(TARGETS, SEQ)

    @pl.when(jnp.logical_not(active))
    def _():
        sent(TARGETS, 0)

    remote(home_q_ref, home_q_ref, home_send.at[0], home_recv.at[0], sibling).wait_recv()
    remote(home_kv_ref, home_kv_ref, home_send.at[1], home_recv.at[1], sibling).wait_recv()


def core(listing, k, q, v, g, gain_q, gain_k):
    bf16, f32 = jnp.bfloat16, jnp.float32
    dma = pltpu.SemaphoreType.DMA
    in_vmem = pl.BlockSpec(memory_space=pltpu.VMEM)
    return pl.pallas_call(
        core_kernel,
        name="core",
        in_specs=[in_vmem] * 7,
        out_specs=[pl.BlockSpec(memory_space=pl.ANY)] * 2 + [in_vmem] * 2,
        out_shape=(
            jax.ShapeDtypeStruct((TARGETS, CHUNK, HD), bf16),
            jax.ShapeDtypeStruct((TARGETS, TILES, 2, PART, HD), bf16),
            jax.ShapeDtypeStruct((SPAN, SPAN), bf16),
            jax.ShapeDtypeStruct((16, HD), f32),
        ),
        scratch_shapes=[
            pltpu.VMEM((TARGETS, 2, CHUNK, HD), bf16),
            pltpu.VMEM((TARGETS, 1, CHUNK, HD), bf16),
            pltpu.VMEM((TARGETS, 1, CHUNK, HD), bf16),
            pltpu.VMEM((SEQ, 2, CHUNK, HD), bf16),
            pltpu.VMEM((SEQ, 1, CHUNK, HD), bf16),
            pltpu.VMEM((SEQ, 1, CHUNK, HD), bf16),
            pltpu.VMEM((SEQ, SHARE), jnp.int32),
            pltpu.VMEM((SEQ, SHARE), jnp.int32),
            pltpu.VMEM((SEQ, SHARE), jnp.int32),
            pltpu.VMEM((ROWS, FLAT), bf16),
            pltpu.VMEM((4, KEPT, HD), bf16),
            pltpu.VMEM((2, ROWS, HD), bf16),
            pltpu.VMEM((ROWS, KEPT), f32),
            pltpu.VMEM((TILE, KEPT), f32),
            pltpu.VMEM((ROWS, 128), f32),
            pltpu.VMEM((SEQ, CHUNK, HD), bf16),
            pltpu.VMEM((TILES, SEQ, 2, PART, HD), bf16),
            pltpu.VMEM((MEMBERS, 2, 8, SHARE), f32),
            pltpu.VMEM((16, HD), f32),
            pltpu.VMEM((SEQ, 16, HD), f32),
            pltpu.VMEM((TARGETS, 16, HD), f32),
            pltpu.VMEM((16, HD), f32),
            pltpu.VMEM((8, 16, HD), f32),
            dma((2,)),
            dma((3,)),
            dma((3,)),
            dma((4, 3)),
            dma((4, 3)),
            dma((MEMBERS,)),
            dma((MEMBERS,)),
            dma((2,)),
            dma((2,)),
            dma((2,)),
            dma((8,)),
            dma((8,)),
        ],
        compiler_params=pltpu.CompilerParams(
            collective_id=0, has_side_effects=True, vmem_limit_bytes=VMEM_LIMIT
        ),
    )(listing, k, q, v, g, gain_q, gain_k)


def rows_kernel(back_ref, home_q_ref, home_kv_ref, total_ref, q_ref, k_ref, v_ref, gain_q_ref, gain_k_ref):
    for h in range(home_q_ref.shape[0] // MEMBERS):
        seats = slice(h * MEMBERS, (h + 1) * MEMBERS)
        for ref, rows in (
            (q_ref, home_q_ref[seats]),
            (k_ref, home_kv_ref[seats, :, 0]),
            (v_ref, home_kv_ref[seats, :, 1]),
        ):
            rows = jnp.dot(back_ref[...], rows.reshape(SPAN, HD), preferred_element_type=jnp.float32)
            ref[0, :, h * HD : (h + 1) * HD] = rows.astype(jnp.bfloat16)
    gain_q_ref[...] = jnp.sum(total_ref[0:8, :], axis=0, keepdims=True)
    gain_k_ref[...] = jnp.sum(total_ref[8:16, :], axis=0, keepdims=True)


def to_rows(back, home_q, home_kv, total):
    width = HEAD_PART * HD
    parts = 2
    big = jax.ShapeDtypeStruct((1, SPAN, width), jnp.bfloat16)
    small = jax.ShapeDtypeStruct((1, HD), jnp.float32)
    return pl.pallas_call(
        rows_kernel,
        name="to_rows",
        grid=(parts,),
        in_specs=[
            pl.BlockSpec((SPAN, SPAN), lambda h: (0, 0)),
            pl.BlockSpec((TARGETS // parts, CHUNK, HD), lambda h: (h, 0, 0)),
            pl.BlockSpec((TARGETS // parts, TILES, 2, PART, HD), lambda h: (h, 0, 0, 0, 0)),
            pl.BlockSpec((16, HD), lambda h: (0, 0)),
        ],
        out_specs=[pl.BlockSpec((1, SPAN, width // parts), lambda h: (0, 0, h))] * 3
        + [pl.BlockSpec((1, HD), lambda h: (0, 0))] * 2,
        out_shape=(big, big, big, small, small),
        compiler_params=pltpu.CompilerParams(vmem_limit_bytes=VMEM_LIMIT),
        cost_estimate=pl.CostEstimate(flops=3 * 10**8, bytes_accessed=3 * 10**6, transcendentals=0),
    )(back, home_q, home_kv, total)


def on_device(q_raw, k_raw, v_raw, out_grad, gain_q, gain_k, keep_list):
    home_q, home_kv, back, total = core(
        keep_list.reshape(SEQ, SHARE),
        k_raw[0],
        q_raw[0],
        v_raw[0],
        out_grad[0],
        gain_q.reshape(1, HD),
        gain_k.reshape(1, HD),
    )
    q_out, k_out, v_out, gain_q_grad, gain_k_grad = to_rows(back, home_q, home_kv, total)
    return q_out, k_out, v_out, gain_q_grad.reshape(HD), gain_k_grad.reshape(HD)


def solution(mesh):
    big = P("dp", "seq", "tensor")
    return jax.shard_map(
        on_device,
        mesh=mesh,
        in_specs=(big, big, big, big, P(), P(), P("dp", None)),
        out_specs=(big, big, big, P(), P()),
        check_vma=False,
    )
```

```python
import math

import jax
import jax.numpy as jnp
from jax import lax
from jax.experimental import pallas as pl
from jax.experimental.pallas import tpu as pltpu
from jax.sharding import PartitionSpec as P

MESH = pl.DeviceIdType.MESH
HD = 128
EPSILON = 1e-06
SEQ = 32
SPAN = 256
SHARE = 128
SLOTS = 8
HEAD_PART = 6
UNITS = 8
ROWS = UNITS * SHARE
CHUNK = UNITS * SLOTS
MEMBERS = 4
TARGETS = HEAD_PART * MEMBERS
OUT = TARGETS * CHUNK
FLAT = SEQ * CHUNK
KEPT = SEQ * SHARE
TILE = 256
PART = TILE // SHARE * SLOTS
TILES = ROWS // TILE
PIECE = 128
SCALING = 1.0 / math.sqrt(HD)
LOG2E = 1.4426950408889634
VMEM_LIMIT = 56 * 1024 * 1024

NT = (((1,), (1,)), ((), ()))

def place(clip, i):
    head, quarter = i >> 2, i & 3
    third = (head * 11) >> 5
    pair = head - 3 * third
    odd = pair >> 1
    y = 2 * ((pair & 1) + odd * third) + (quarter >> 1)
    z = 4 * clip + 2 * third + odd
    return quarter & 1, y * 8 + z


def my_place(dp, s):
    y, z = s >> 3, s & 7
    third, odd, high = (z >> 1) & 1, z & 1, y >> 1
    pair = high + odd * (2 - high)
    active = (odd == 0) | (high == third)
    return z >> 2, (3 * third + pair) * 4 + 2 * (y & 1) + dp, active


def one_hot(hit):
    return jnp.where(hit, 1.0, 0.0).astype(jnp.bfloat16)


def inverse_norm(x):
    return lax.rsqrt(jnp.mean(x * x, axis=-1, keepdims=True) + EPSILON)


def norm_grads(raw, gain, upstream):
    raw = raw.astype(jnp.float32)
    inverse = inverse_norm(raw)
    scaled = upstream * gain
    inner = jnp.mean(scaled * raw, axis=-1, keepdims=True)
    grads = inverse * scaled - raw * (inverse * inverse * inverse * inner)
    terms = upstream * raw * inverse
    return grads, jnp.sum(terms.reshape(-1, 8, HD), axis=0)


def lane_fold(x, fold):
    parts = [x[:, i * 128 : (i + 1) * 128] for i in range(x.shape[1] // 128)]
    total = parts[0]
    for part in parts[1:]:
        total = fold(total, part)
    return total


def core_kernel(
    list_ref,
    k_ref,
    q_ref,
    v_ref,
    g_ref,
    gain_q_ref,
    gain_k_ref,
    home_ref,
    back_ref,
    total_ref,
    slots,
    arrived,
    enc_ref,
    other,
    codes,
    pick,
    full,
    raw,
    scores_ref,
    dots_ref,
    sums,
    q_slots,
    kv_slots,
    stats,
    terms,
    part_bytes,
    parts,
    partial,
    cross,
    enc_sem,
    route_send,
    route_recv,
    near_send,
    near_recv,
    stat_send,
    stat_recv,
    home_send,
    home_recv,
    part_sem,
    cross_send,
    cross_recv,
):
    dp, s, x = lax.axis_index("dp"), lax.axis_index("seq"), lax.axis_index("tensor")
    clip, seat, active = my_place(dp, s)
    me = seat & 3
    sibling = (1 - dp, s, x)
    corner = dp * 4 + x
    same = active & (clip == dp)
    own_source = jnp.where(same, s, -1)
    own_target = jnp.where(same, seat, -1)

    def to_self(i):
        return i == own_source

    def target(i):
        return place(dp, i) + (x,), i == own_target

    def source(i):
        return (clip, i, x)

    def member(i):
        return (i & 1, (s & 23) + 8 * (i >> 1), x)

    def remote(src, dst, send_sem, recv_sem, device):
        return pltpu.make_async_remote_copy(
            src_ref=src, dst_ref=dst, send_sem=send_sem, recv_sem=recv_sem, device_id=device, device_id_type=MESH
        )


    barrier = pltpu.get_barrier_semaphore()

    def greet_device(there):
        pl.semaphore_signal(barrier, inc=1, device_id=there, device_id_type=MESH)

    def greet_target(i, _):
        there, own = target(i)

        @pl.when(jnp.logical_not(own))
        def _():
            greet_device(there)

        return 0

    def greet_source(i, _):
        @pl.when(jnp.logical_not(to_self(i)))
        def _():
            greet_device(source(i))

        return 0

    def greet_corner(i, _):
        @pl.when(i != corner)
        def _():
            greet_device((i >> 2, s, i & 3))

        return 0

    @pl.when(active)
    def _():
        lax.fori_loop(0, SEQ, greet_source, 0)
        for step in (1, 2, 3):
            greet_device(member(me ^ step))

    lax.fori_loop(0, TARGETS, greet_target, 0)
    lax.fori_loop(0, 8, greet_corner, 0)


    listing = list_ref[...]
    from_block = listing >> 8
    hits = one_hot(jnp.concatenate([from_block == i for i in range(SEQ)], axis=0))
    earlier = lax.broadcasted_iota(jnp.int32, (SHARE, SHARE), 0) < lax.broadcasted_iota(jnp.int32, (SHARE, SHARE), 1)
    counts = jnp.dot(hits, one_hot(earlier), preferred_element_type=jnp.float32) * hits.astype(jnp.float32)
    rank = counts[0:SEQ]
    for i in range(1, SEQ):
        rank += counts[i * SEQ : (i + 1) * SEQ]
    rank = rank.astype(jnp.int32)
    enc_ref[...] = from_block * SLOTS + rank
    slot = lax.broadcasted_iota(jnp.int32, (SEQ, SHARE), 0) * SLOTS + rank + 1
    slot = jnp.where(from_block == s, slot, 0).astype(jnp.float32)
    token = listing - s * SPAN
    token_iota = lax.broadcasted_iota(jnp.int32, (SPAN, SHARE), 0)
    found = jnp.zeros((SPAN, SHARE), jnp.float32)
    for j in range(SEQ):
        found += jnp.where(token_iota == token[j : j + 1], slot[j : j + 1], 0.0)
    found = jnp.sum(found, axis=1, keepdims=True) - 1.0
    row = jnp.broadcast_to(found, (SPAN, 128)).T[0:1]
    back_ref[...] = one_hot(lax.broadcasted_iota(jnp.int32, (SPAN, SPAN), 1).astype(jnp.float32) == found)
    take = one_hot(lax.broadcasted_iota(jnp.int32, (SPAN, SPAN), 0).astype(jnp.float32) == row)
    step = 512

    def to_slots(i, ref):
        rows = jnp.dot(take, ref[...], preferred_element_type=jnp.float32).astype(jnp.bfloat16)
        for h in range(HEAD_PART):
            slots[i, h * SPAN : (h + 1) * SPAN, :] = rows[:, h * HD : (h + 1) * HD]

    def chunk(ref, a, i):
        return ref.at[a, pl.ds(pl.multiple_of(i * CHUNK, 16), CHUNK), :]

    def nth_target(n):
        v = 3 * (s & 7) + 6 * (s >> 3) + 7 * n
        return v - 24 * ((v * 171) >> 12)

    def nth_source(n):
        turn = n & 7
        away = ((turn + 1) >> 1) * (2 * (turn & 1) - 1)
        return (((s >> 3) + (n >> 3)) & 3) * 8 + (((s & 7) + away) & 7)


    def route(a, first, last, beside=None):
        def start(n, _):
            if beside is not None:

                @pl.when(n < first + ROWS // PIECE)
                def _():
                    @pl.when(active)
                    def _():
                        piece(beside, n - first).start()

            i = nth_target(n)
            there, own = target(i)

            @pl.when(jnp.logical_not(own))
            def _():
                remote(chunk(slots, a, i), chunk(arrived, a, s), route_send.at[a], route_recv.at[a], there).start()

            return 0

        lax.fori_loop(first, last, start, 0)

        if last == TARGETS:

            @pl.when(same)
            def _():
                pltpu.make_async_copy(chunk(slots, a, seat), chunk(arrived, a, s), route_recv.at[a]).start()

    def rows_of(a, i):
        return full.at[a, pl.ds(pl.multiple_of(i * ROWS, ROWS), ROWS), :]

    def piece(a, n):
        rows = full.at[a, pl.ds(pl.multiple_of(me * ROWS + n * PIECE, PIECE), PIECE), :]
        return remote(rows, rows, near_send.at[a, 0], near_recv.at[a, 0], member(me ^ 2))

    to_slots(0, k_ref)
    arrivals = jnp.where(active, SEQ + 3, 0) - jnp.where(same, 2, 0)
    pl.semaphore_wait(barrier, TARGETS + 7 + arrivals)
    exchange = remote(enc_ref, other, enc_sem.at[0], enc_sem.at[1], sibling)

    @pl.when(active)
    def _():
        exchange.start()

    route(0, 0, TARGETS)
    to_slots(1, q_ref)
    route(1, 0, TARGETS // 2)
    to_slots(2, v_ref)
    to_slots(3, g_ref)


    def unit_codes(u):
        return codes[pl.ds(UNITS * me + u, 1), :]

    def build_pick():
        exchange.wait()
        codes[...] = jnp.where(clip == dp, enc_ref[...], other[...])
        wide_iota = lax.broadcasted_iota(jnp.int32, (SHARE, 128), 1).astype(jnp.float32)
        for u in range(UNITS):
            code = unit_codes(u)
            code = (code >> 3) * CHUNK + u * SLOTS + (code & 7)
            wide = jnp.broadcast_to(code.astype(jnp.float32), (SHARE, 128)).T
            for c in range(FLAT // 128):
                pick[u * SHARE : (u + 1) * SHARE, c * 128 : (c + 1) * 128] = one_hot(wide == wide_iota + c * 128.0)


    def near(a, way, rows, there):
        return remote(rows_of(a, rows), rows_of(a, rows), near_send.at[a, way], near_recv.at[a, way], member(there))

    def gather_rest():
        def start(n, _):
            piece(3, n).start()
            return 0

        lax.fori_loop(0, ROWS // PIECE, start, 0)

    def gather_pass(a):
        near(a, 0, me ^ 2, me).wait_recv()
        near(a, 2, me ^ 2, me ^ 1).start()

    def gather_finish(a):
        near(a, 1, me ^ 1, me).wait_recv()
        near(a, 2, me ^ 3, me).wait_recv()

    def gather_sent(a):
        near(a, 0, me, me ^ 2).wait_send()
        near(a, 1, me, me ^ 1).wait_send()
        near(a, 2, me ^ 2, me ^ 1).wait_send()

    own_rows = pl.ds(pl.multiple_of(me * ROWS, 256), ROWS)

    def to_dense(a):
        remote(arrived.at[a], arrived.at[a], route_send.at[a], route_recv.at[a], sibling).wait_recv()
        rows = jnp.dot(pick[...], arrived[a], preferred_element_type=jnp.float32)
        if a < 2:
            raw[a] = rows.astype(jnp.bfloat16)
            gain = (gain_k_ref, gain_q_ref)[a][...]
            rows = rows * inverse_norm(rows) * gain
        full[a, own_rows, :] = rows.astype(jnp.bfloat16)
        near(a, 1, me, me ^ 1).start()


    chunks = [slice(i * step, (i + 1) * step) for i in range(KEPT // step)]

    def head_rows(a, cols):
        return full[a, cols, :]

    def tile_rows(a, t):
        return full[a, pl.ds(pl.multiple_of(me * ROWS + t * TILE, TILE), TILE), :]

    def local_rows(t):
        return pl.ds(pl.multiple_of(t * TILE, TILE), TILE)

    def store_stat(i, t, value):
        wide = jnp.broadcast_to(value, (TILE, 128)).T
        for j in range(TILE // SHARE):
            stats[me, i, pl.ds(TILE // SHARE * t + j, 1), :] = wide[0:1, j * SHARE : (j + 1) * SHARE]

    def score_tile(t, _):
        query = tile_rows(1, t)
        rows = local_rows(t)
        top = None
        for cols in chunks:
            scores = lax.dot_general(query, head_rows(0, cols), NT, preferred_element_type=jnp.float32)
            scores = scores * (SCALING * LOG2E)
            scores_ref[rows, cols] = scores
            part = lane_fold(scores, jnp.maximum)
            top = part if top is None else jnp.maximum(top, part)
        top = jnp.max(top, axis=-1, keepdims=True)
        total = jnp.zeros((TILE, 128), jnp.float32)
        for cols in chunks:
            weights = jnp.exp2(scores_ref[rows, cols] - top)
            scores_ref[rows, cols] = weights
            total += lane_fold(weights, jnp.add)
        total = jnp.sum(total, axis=-1, keepdims=True)
        sums[rows, :] = jnp.broadcast_to(total, (TILE, 128))
        store_stat(0, t, top + jnp.log2(total))

        return 0

    def spread_tile(t, rows):
        tile_iota = lax.broadcasted_iota(jnp.int32, (SEQ * PART, TILE), 0)
        tile_codes = []
        for j in range(TILE // SHARE):
            code = unit_codes(TILE // SHARE * t + j)
            tile_codes.append((code >> 3) * PART + j * SLOTS + (code & 7))
        spread = one_hot(tile_iota == jnp.concatenate(tile_codes, axis=1))
        rows = jnp.dot(spread, rows.astype(jnp.bfloat16), preferred_element_type=jnp.float32)
        return rows.astype(jnp.bfloat16).reshape(SEQ, PART, HD)

    def part_of(t):
        return pl.ds(pl.multiple_of(t * PART, PART), PART)

    def query_tile(t, _):
        grad = tile_rows(3, t)
        rows = local_rows(t)
        weighted = jnp.zeros((TILE, 128), jnp.float32)
        for cols in chunks:
            dots = lax.dot_general(grad, head_rows(2, cols), NT, preferred_element_type=jnp.float32)
            dots_ref[:, cols] = dots
            weighted += lane_fold(scores_ref[rows, cols] * dots, jnp.add)
        share = 1.0 / sums[rows, 0:1]
        delta = jnp.sum(weighted, axis=-1, keepdims=True) * share
        result = jnp.zeros((TILE, HD), jnp.float32)
        for cols in chunks:
            dscore = (scores_ref[rows, cols] * share) * (dots_ref[:, cols] - delta)
            result += jnp.dot(dscore.astype(jnp.bfloat16), head_rows(0, cols), preferred_element_type=jnp.float32)
        grads, term = norm_grads(raw[1, rows, :], gain_q_ref[...], result * SCALING)
        terms[0:8, :] += term
        store_stat(1, t, delta)

        q_slots[:, part_of(t), :] = spread_tile(t, grads)

        @pl.when((t & 1) == 1)
        def _():
            send_home(lambda i: q_home(t >> 1, i), 0)

        return 0


    def stat_copy(rows, there):
        return remote(stats.at[rows], stats.at[rows], stat_send.at[there], stat_recv.at[rows], member(there))

    def stat_start():
        for step in (1, 2, 3):
            stat_copy(me, me ^ step).start()

    def stat_finish():
        for step in (1, 2, 3):
            stat_copy(me ^ step, me ^ step).wait_recv()
            stat_copy(me, me ^ step).wait_send()


    half = CHUNK // 2

    def half_of(h):
        return pl.ds(pl.multiple_of(h * half, half), half)

    def home_half(h):
        return pl.ds(pl.multiple_of(seat * CHUNK + h * half, half), half)

    def q_home(h, i):
        return q_slots.at[i, half_of(h), :], home_ref.at[0, home_half(h), :]

    def kv_home(h, i):
        return kv_slots.at[:, i, half_of(h), :], home_ref.at[1:3, home_half(h), :]

    def send_home(copies, sem):
        def start(n, _):
            i = nth_source(n)
            src, dst = copies(i)

            @pl.when(jnp.logical_not(to_self(i)))
            def _():
                remote(src, dst, home_send.at[sem], home_recv.at[sem], source(i)).start()

            return 0

        lax.fori_loop(0, SEQ, start, 0)

        @pl.when(same)
        def _():
            src, dst = copies(s)
            pltpu.make_async_copy(src, dst, home_recv.at[sem]).start()


    def stat_row(i, cols):
        units = range(cols.start // SHARE, cols.stop // SHARE)
        return jnp.concatenate([stats[u // UNITS, i, u % UNITS : u % UNITS + 1, :] for u in units], axis=1)

    def key_tile(t, _):
        key, value = tile_rows(0, t), tile_rows(2, t)
        key_grad = jnp.zeros((TILE, HD), jnp.float32)
        value_grad = jnp.zeros((TILE, HD), jnp.float32)
        for cols in chunks:
            query, grad = head_rows(1, cols), head_rows(3, cols)
            scores = lax.dot_general(key, query, NT, preferred_element_type=jnp.float32)
            weights = jnp.exp2(scores * (SCALING * LOG2E) - stat_row(0, cols))
            dots = lax.dot_general(value, grad, NT, preferred_element_type=jnp.float32)
            dscore = weights * (dots - stat_row(1, cols))
            key_grad += jnp.dot(dscore.astype(jnp.bfloat16), query, preferred_element_type=jnp.float32)
            value_grad += jnp.dot(weights.astype(jnp.bfloat16), grad, preferred_element_type=jnp.float32)
        grads, term = norm_grads(raw[0, local_rows(t), :], gain_k_ref[...], key_grad * SCALING)
        terms[8:16, :] += term
        for i, result in enumerate((grads, value_grad)):
            kv_slots[i, :, part_of(t), :] = spread_tile(t, result)

        @pl.when((t & 1) == 1)
        def _():
            send_home(lambda i: kv_home(t >> 1, i), 1)

        return 0


    def part_start(i, _):
        @pl.when(jnp.logical_not(to_self(i)))
        def _():
            remote(terms, parts.at[seat], part_sem.at[0], part_sem.at[1], source(i)).start()

        return 0

    @pl.when(active)
    def _():
        build_pick()
        to_dense(0)

    route(1, TARGETS // 2, TARGETS, beside=0)
    route(2, 0, TARGETS)

    @pl.when(active)
    def _():
        terms[...] = jnp.zeros_like(terms)
        to_dense(1)
        gather_pass(0)
        gather_finish(0)
        lax.fori_loop(0, 1, score_tile, 0)

    route(3, 0, TARGETS // 2, beside=1)

    @pl.when(active)
    def _():
        lax.fori_loop(1, TILES // 2, score_tile, 0)
        to_dense(2)

    route(3, TARGETS // 2, TARGETS, beside=2)

    @pl.when(active)
    def _():
        lax.fori_loop(TILES // 2, TILES, score_tile, 0)
        gather_pass(1)
        gather_pass(2)
        to_dense(3)
        gather_rest()
        gather_finish(2)
        lax.fori_loop(0, TILES, query_tile, 0)
        stat_start()
        gather_pass(3)
        gather_finish(1)
        gather_finish(3)
        stat_finish()
        lax.fori_loop(0, TILES, key_tile, 0)
        lax.fori_loop(0, SEQ, part_start, 0)

        @pl.when(same)
        def _():
            pltpu.make_async_copy(terms, parts.at[seat], part_sem.at[1]).start()

    remote(parts, parts, part_sem.at[0], part_sem.at[1], sibling).wait_recv()
    partial[...] = jnp.sum(parts[...], axis=0)

    def cross_copy(i, dst):
        return remote(partial, cross.at[dst], cross_send.at[i], cross_recv.at[dst], (i >> 2, s, i & 3))

    def cross_start(i, _):
        @pl.when(i != corner)
        def _():
            cross_copy(i, corner).start()

        return 0

    def cross_finish(i, _):
        @pl.when(i != corner)
        def _():
            cross_copy(i, i).wait_recv()
            cross_copy(i, corner).wait_send()

        return 0

    cross[pl.ds(corner, 1)] = partial[...][None]
    lax.fori_loop(0, 8, cross_start, 0)
    lax.fori_loop(0, 8, cross_finish, 0)
    total_ref[...] = jnp.sum(cross[...], axis=0)


    def sent(targets, sources):
        for a in range(4):
            rows = slots.at[a, 0 : targets * CHUNK, :]
            remote(rows, rows, route_send.at[a], route_recv.at[a], sibling).wait_send()
        if sources:
            for a in range(4):
                gather_sent(a)
            rows = q_slots.at[0:sources]
            remote(rows, rows, home_send.at[0], home_recv.at[0], sibling).wait_send()
            rows = kv_slots.at[:, 0:sources]
            remote(rows, rows, home_send.at[1], home_recv.at[1], sibling).wait_send()
            rows = part_bytes.at[0:sources]
            remote(rows, rows, part_sem.at[0], part_sem.at[1], sibling).wait_send()

    @pl.when(same)
    def _():
        sent(TARGETS - 1, SEQ - 1)

    @pl.when(active & jnp.logical_not(same))
    def _():
        sent(TARGETS, SEQ)

    @pl.when(jnp.logical_not(active))
    def _():
        sent(TARGETS, 0)

    remote(home_ref.at[0], home_ref.at[0], home_send.at[0], home_recv.at[0], sibling).wait_recv()
    remote(home_ref.at[1:3], home_ref.at[1:3], home_send.at[1], home_recv.at[1], sibling).wait_recv()


def core(listing, k, q, v, g, gain_q, gain_k):
    bf16, f32 = jnp.bfloat16, jnp.float32
    dma = pltpu.SemaphoreType.DMA
    in_vmem = pl.BlockSpec(memory_space=pltpu.VMEM)
    return pl.pallas_call(
        core_kernel,
        name="core",
        in_specs=[in_vmem] * 7,
        out_specs=[pl.BlockSpec(memory_space=pl.ANY), in_vmem, in_vmem],
        out_shape=(
            jax.ShapeDtypeStruct((3, OUT, HD), bf16),
            jax.ShapeDtypeStruct((SPAN, SPAN), bf16),
            jax.ShapeDtypeStruct((16, HD), f32),
        ),
        scratch_shapes=[
            pltpu.VMEM((4, OUT, HD), bf16),
            pltpu.VMEM((4, FLAT, HD), bf16),
            pltpu.VMEM((SEQ, SHARE), jnp.int32),
            pltpu.VMEM((SEQ, SHARE), jnp.int32),
            pltpu.VMEM((SEQ, SHARE), jnp.int32),
            pltpu.VMEM((ROWS, FLAT), bf16),
            pltpu.VMEM((4, KEPT, HD), bf16),
            pltpu.VMEM((2, ROWS, HD), bf16),
            pltpu.VMEM((ROWS, KEPT), f32),
            pltpu.VMEM((TILE, KEPT), f32),
            pltpu.VMEM((ROWS, 128), f32),
            pltpu.VMEM((SEQ, CHUNK, HD), bf16),
            pltpu.VMEM((2, SEQ, CHUNK, HD), bf16),
            pltpu.VMEM((MEMBERS, 2, 8, SHARE), f32),
            pltpu.VMEM((16, HD), f32),
            pltpu.VMEM((SEQ, 16, HD), f32),
            pltpu.VMEM((TARGETS, 16, HD), f32),
            pltpu.VMEM((16, HD), f32),
            pltpu.VMEM((8, 16, HD), f32),
            dma((2,)),
            dma((4,)),
            dma((4,)),
            dma((4, 3)),
            dma((4, 3)),
            dma((MEMBERS,)),
            dma((MEMBERS,)),
            dma((2,)),
            dma((2,)),
            dma((2,)),
            dma((8,)),
            dma((8,)),
        ],
        compiler_params=pltpu.CompilerParams(
            collective_id=0, has_side_effects=True, vmem_limit_bytes=VMEM_LIMIT
        ),
    )(listing, k, q, v, g, gain_q, gain_k)


def rows_kernel(back_ref, slots_ref, total_ref, q_ref, k_ref, v_ref, gain_q_ref, gain_k_ref):
    for i, ref in enumerate((q_ref, k_ref, v_ref)):
        for h in range(slots_ref.shape[1] // SPAN):
            rows = slots_ref[i, h * SPAN : (h + 1) * SPAN, :]
            rows = jnp.dot(back_ref[...], rows, preferred_element_type=jnp.float32)
            ref[0, :, h * HD : (h + 1) * HD] = rows.astype(jnp.bfloat16)
    gain_q_ref[...] = jnp.sum(total_ref[0:8, :], axis=0, keepdims=True)
    gain_k_ref[...] = jnp.sum(total_ref[8:16, :], axis=0, keepdims=True)


def to_rows(back, slots, total):
    width = HEAD_PART * HD
    parts = 2
    big = jax.ShapeDtypeStruct((1, SPAN, width), jnp.bfloat16)
    small = jax.ShapeDtypeStruct((1, HD), jnp.float32)
    return pl.pallas_call(
        rows_kernel,
        name="to_rows",
        grid=(parts,),
        in_specs=[
            pl.BlockSpec((SPAN, SPAN), lambda h: (0, 0)),
            pl.BlockSpec((3, OUT // parts, HD), lambda h: (0, h, 0)),
            pl.BlockSpec((16, HD), lambda h: (0, 0)),
        ],
        out_specs=[pl.BlockSpec((1, SPAN, width // parts), lambda h: (0, 0, h))] * 3
        + [pl.BlockSpec((1, HD), lambda h: (0, 0))] * 2,
        out_shape=(big, big, big, small, small),
        compiler_params=pltpu.CompilerParams(vmem_limit_bytes=VMEM_LIMIT),
        cost_estimate=pl.CostEstimate(flops=3 * 10**8, bytes_accessed=3 * 10**6, transcendentals=0),
    )(back, slots, total)


def on_device(q_raw, k_raw, v_raw, out_grad, gain_q, gain_k, keep_list):
    home, back, total = core(
        keep_list.reshape(SEQ, SHARE),
        k_raw[0],
        q_raw[0],
        v_raw[0],
        out_grad[0],
        gain_q.reshape(1, HD),
        gain_k.reshape(1, HD),
    )
    q_out, k_out, v_out, gain_q_grad, gain_k_grad = to_rows(back, home, total)
    return q_out, k_out, v_out, gain_q_grad.reshape(HD), gain_k_grad.reshape(HD)


def solution(mesh):
    big = P("dp", "seq", "tensor")
    return jax.shard_map(
        on_device,
        mesh=mesh,
        in_specs=(big, big, big, big, P(), P(), P("dp", None)),
        out_specs=(big, big, big, P(), P()),
        check_vma=False,
    )
```

```python
import math

import jax
import jax.numpy as jnp
from jax import lax
from jax.experimental import pallas as pl
from jax.experimental.pallas import tpu as pltpu
from jax.sharding import PartitionSpec as P

MESH = pl.DeviceIdType.MESH
HD = 128
EPSILON = 1e-06
SEQ = 32
SPAN = 256
SHARE = 128
SLOTS = 8
HEAD_PART = 6
UNITS = 8
ROWS = UNITS * SHARE
CHUNK = UNITS * SLOTS
MEMBERS = 4
TARGETS = HEAD_PART * MEMBERS
OUT = TARGETS * CHUNK
FLAT = SEQ * CHUNK
KEPT = SEQ * SHARE
TILE = 256
PART = TILE // SHARE * SLOTS
TILES = ROWS // TILE
PIECE = 128
SCALING = 1.0 / math.sqrt(HD)
LOG2E = 1.4426950408889634
VMEM_LIMIT = 56 * 1024 * 1024

NT = (((1,), (1,)), ((), ()))

def place(clip, i):
    head, quarter = i >> 2, i & 3
    third = (head * 11) >> 5
    pair = head - 3 * third
    odd = pair >> 1
    y = 2 * ((pair & 1) + odd * third) + (quarter >> 1)
    z = 4 * clip + 2 * third + odd
    return quarter & 1, y * 8 + z


def my_place(dp, s):
    y, z = s >> 3, s & 7
    third, odd, high = (z >> 1) & 1, z & 1, y >> 1
    pair = high + odd * (2 - high)
    active = (odd == 0) | (high == third)
    return z >> 2, (3 * third + pair) * 4 + 2 * (y & 1) + dp, active


def one_hot(hit):
    return jnp.where(hit, 1.0, 0.0).astype(jnp.bfloat16)


def inverse_norm(x):
    return lax.rsqrt(jnp.mean(x * x, axis=-1, keepdims=True) + EPSILON)


def norm_grads(raw, gain, upstream):
    raw = raw.astype(jnp.float32)
    inverse = inverse_norm(raw)
    scaled = upstream * gain
    inner = jnp.mean(scaled * raw, axis=-1, keepdims=True)
    grads = inverse * scaled - raw * (inverse * inverse * inverse * inner)
    terms = upstream * raw * inverse
    return grads, jnp.sum(terms.reshape(-1, 8, HD), axis=0)


def lane_fold(x, fold):
    parts = [x[:, i * 128 : (i + 1) * 128] for i in range(x.shape[1] // 128)]
    total = parts[0]
    for part in parts[1:]:
        total = fold(total, part)
    return total


def core_kernel(
    list_ref,
    k_ref,
    q_ref,
    v_ref,
    g_ref,
    gain_q_ref,
    gain_k_ref,
    home_ref,
    back_ref,
    total_ref,
    slots,
    arrived,
    enc_ref,
    other,
    codes,
    pick,
    full,
    raw,
    scores_ref,
    dots_ref,
    sums,
    q_slots,
    kv_slots,
    stats,
    terms,
    part_bytes,
    parts,
    partial,
    cross,
    enc_sem,
    route_send,
    route_recv,
    near_send,
    near_recv,
    stat_send,
    stat_recv,
    home_send,
    home_recv,
    part_sem,
    cross_send,
    cross_recv,
):
    dp, s, x = lax.axis_index("dp"), lax.axis_index("seq"), lax.axis_index("tensor")
    clip, seat, active = my_place(dp, s)
    me = seat & 3
    sibling = (1 - dp, s, x)
    corner = dp * 4 + x
    same = active & (clip == dp)
    own_source = jnp.where(same, s, -1)
    own_target = jnp.where(same, seat, -1)

    def to_self(i):
        return i == own_source

    def target(i):
        return place(dp, i) + (x,), i == own_target

    def source(i):
        return (clip, i, x)

    def member(i):
        return (i & 1, (s & 23) + 8 * (i >> 1), x)

    def remote(src, dst, send_sem, recv_sem, device):
        return pltpu.make_async_remote_copy(
            src_ref=src, dst_ref=dst, send_sem=send_sem, recv_sem=recv_sem, device_id=device, device_id_type=MESH
        )


    barrier = pltpu.get_barrier_semaphore()

    def greet_device(there):
        pl.semaphore_signal(barrier, inc=1, device_id=there, device_id_type=MESH)

    def greet_target(i, _):
        there, own = target(i)

        @pl.when(jnp.logical_not(own))
        def _():
            greet_device(there)

        return 0

    def greet_source(i, _):
        @pl.when(jnp.logical_not(to_self(i)))
        def _():
            greet_device(source(i))

        return 0

    def greet_corner(i, _):
        @pl.when(i != corner)
        def _():
            greet_device((i >> 2, s, i & 3))

        return 0

    @pl.when(active)
    def _():
        lax.fori_loop(0, SEQ, greet_source, 0)
        for step in (1, 2, 3):
            greet_device(member(me ^ step))

    lax.fori_loop(0, TARGETS, greet_target, 0)
    lax.fori_loop(0, 8, greet_corner, 0)


    listing = list_ref[...]
    from_block = listing >> 8
    hits = one_hot(jnp.concatenate([from_block == i for i in range(SEQ)], axis=0))
    earlier = lax.broadcasted_iota(jnp.int32, (SHARE, SHARE), 0) < lax.broadcasted_iota(jnp.int32, (SHARE, SHARE), 1)
    counts = jnp.dot(hits, one_hot(earlier), preferred_element_type=jnp.float32) * hits.astype(jnp.float32)
    rank = counts[0:SEQ]
    for i in range(1, SEQ):
        rank += counts[i * SEQ : (i + 1) * SEQ]
    rank = rank.astype(jnp.int32)
    enc_ref[...] = from_block * SLOTS + rank
    slot = lax.broadcasted_iota(jnp.int32, (SEQ, SHARE), 0) * SLOTS + rank + 1
    slot = jnp.where(from_block == s, slot, 0).astype(jnp.float32)
    token = listing - s * SPAN
    token_iota = lax.broadcasted_iota(jnp.int32, (SPAN, SHARE), 0)
    found = jnp.zeros((SPAN, SHARE), jnp.float32)
    for j in range(SEQ):
        found += jnp.where(token_iota == token[j : j + 1], slot[j : j + 1], 0.0)
    found = jnp.sum(found, axis=1, keepdims=True) - 1.0
    row = jnp.broadcast_to(found, (SPAN, 128)).T[0:1]
    back_ref[...] = one_hot(lax.broadcasted_iota(jnp.int32, (SPAN, SPAN), 1).astype(jnp.float32) == found)
    take = one_hot(lax.broadcasted_iota(jnp.int32, (SPAN, SPAN), 0).astype(jnp.float32) == row)
    step = 512

    def to_slots(i, ref):
        rows = jnp.dot(take, ref[...], preferred_element_type=jnp.float32).astype(jnp.bfloat16)
        for h in range(HEAD_PART):
            slots[i, h * SPAN : (h + 1) * SPAN, :] = rows[:, h * HD : (h + 1) * HD]

    def chunk(ref, a, i):
        return ref.at[a, pl.ds(pl.multiple_of(i * CHUNK, 16), CHUNK), :]

    def nth_target(n):
        v = 3 * (s & 7) + 6 * (s >> 3) + 7 * n
        return v - 24 * ((v * 171) >> 12)

    def nth_source(n):
        turn = n & 7
        away = ((turn + 1) >> 1) * (2 * (turn & 1) - 1)
        return (((s >> 3) + (n >> 3)) & 3) * 8 + (((s & 7) + away) & 7)


    def route(a, first, last, beside=None):
        def start(n, _):
            if beside is not None:

                @pl.when(n < first + ROWS // PIECE)
                def _():
                    @pl.when(active)
                    def _():
                        piece(beside, n - first).start()

            i = nth_target(n)
            there, own = target(i)

            @pl.when(jnp.logical_not(own))
            def _():
                remote(chunk(slots, a, i), chunk(arrived, a, s), route_send.at[a], route_recv.at[a], there).start()

            return 0

        lax.fori_loop(first, last, start, 0)

        if last == TARGETS:

            @pl.when(same)
            def _():
                pltpu.make_async_copy(chunk(slots, a, seat), chunk(arrived, a, s), route_recv.at[a]).start()

    def rows_of(a, i):
        return full.at[a, pl.ds(pl.multiple_of(i * ROWS, ROWS), ROWS), :]

    def piece(a, n):
        rows = full.at[a, pl.ds(pl.multiple_of(me * ROWS + n * PIECE, PIECE), PIECE), :]
        return remote(rows, rows, near_send.at[a, 0], near_recv.at[a, 0], member(me ^ 2))

    to_slots(0, k_ref)
    arrivals = jnp.where(active, SEQ + 3, 0) - jnp.where(same, 2, 0)
    pl.semaphore_wait(barrier, TARGETS + 7 + arrivals)
    exchange = remote(enc_ref, other, enc_sem.at[0], enc_sem.at[1], sibling)

    @pl.when(active)
    def _():
        exchange.start()

    route(0, 0, TARGETS)
    to_slots(1, q_ref)
    route(1, 0, TARGETS)
    to_slots(2, v_ref)
    to_slots(3, g_ref)


    def unit_codes(u):
        return codes[pl.ds(UNITS * me + u, 1), :]

    def build_pick():
        exchange.wait()
        codes[...] = jnp.where(clip == dp, enc_ref[...], other[...])
        wide_iota = lax.broadcasted_iota(jnp.int32, (SHARE, 128), 1).astype(jnp.float32)
        for u in range(UNITS):
            code = unit_codes(u)
            code = (code >> 3) * CHUNK + u * SLOTS + (code & 7)
            wide = jnp.broadcast_to(code.astype(jnp.float32), (SHARE, 128)).T
            for c in range(FLAT // 128):
                pick[u * SHARE : (u + 1) * SHARE, c * 128 : (c + 1) * 128] = one_hot(wide == wide_iota + c * 128.0)


    def near(a, way, rows, there):
        return remote(rows_of(a, rows), rows_of(a, rows), near_send.at[a, way], near_recv.at[a, way], member(there))

    def gather_rest():
        def start(n, _):
            piece(3, n).start()
            return 0

        lax.fori_loop(0, ROWS // PIECE, start, 0)

    def gather_pass(a):
        near(a, 0, me ^ 2, me).wait_recv()
        near(a, 2, me ^ 2, me ^ 1).start()

    def gather_finish(a):
        near(a, 1, me ^ 1, me).wait_recv()
        near(a, 2, me ^ 3, me).wait_recv()

    def gather_sent(a):
        near(a, 0, me, me ^ 2).wait_send()
        near(a, 1, me, me ^ 1).wait_send()
        near(a, 2, me ^ 2, me ^ 1).wait_send()

    own_rows = pl.ds(pl.multiple_of(me * ROWS, 256), ROWS)

    def to_dense(a):
        remote(arrived.at[a], arrived.at[a], route_send.at[a], route_recv.at[a], sibling).wait_recv()
        rows = jnp.dot(pick[...], arrived[a], preferred_element_type=jnp.float32)
        if a < 2:
            raw[a] = rows.astype(jnp.bfloat16)
            gain = (gain_k_ref, gain_q_ref)[a][...]
            rows = rows * inverse_norm(rows) * gain
        full[a, own_rows, :] = rows.astype(jnp.bfloat16)
        near(a, 1, me, me ^ 1).start()


    chunks = [slice(i * step, (i + 1) * step) for i in range(KEPT // step)]

    def head_rows(a, cols):
        return full[a, cols, :]

    def tile_rows(a, t):
        return full[a, pl.ds(pl.multiple_of(me * ROWS + t * TILE, TILE), TILE), :]

    def local_rows(t):
        return pl.ds(pl.multiple_of(t * TILE, TILE), TILE)

    def store_stat(i, t, value):
        wide = jnp.broadcast_to(value, (TILE, 128)).T
        for j in range(TILE // SHARE):
            stats[me, i, pl.ds(TILE // SHARE * t + j, 1), :] = wide[0:1, j * SHARE : (j + 1) * SHARE]

    def score_tile(t, _):
        query = tile_rows(1, t)
        rows = local_rows(t)
        top = None
        for cols in chunks:
            scores = lax.dot_general(query, head_rows(0, cols), NT, preferred_element_type=jnp.float32)
            scores = scores * (SCALING * LOG2E)
            scores_ref[rows, cols] = scores
            part = lane_fold(scores, jnp.maximum)
            top = part if top is None else jnp.maximum(top, part)
        top = jnp.max(top, axis=-1, keepdims=True)
        total = jnp.zeros((TILE, 128), jnp.float32)
        for cols in chunks:
            weights = jnp.exp2(scores_ref[rows, cols] - top)
            scores_ref[rows, cols] = weights
            total += lane_fold(weights, jnp.add)
        total = jnp.sum(total, axis=-1, keepdims=True)
        sums[rows, :] = jnp.broadcast_to(total, (TILE, 128))
        store_stat(0, t, top + jnp.log2(total))

        return 0

    def spread_tile(t, rows):
        tile_iota = lax.broadcasted_iota(jnp.int32, (SEQ * PART, TILE), 0)
        tile_codes = []
        for j in range(TILE // SHARE):
            code = unit_codes(TILE // SHARE * t + j)
            tile_codes.append((code >> 3) * PART + j * SLOTS + (code & 7))
        spread = one_hot(tile_iota == jnp.concatenate(tile_codes, axis=1))
        rows = jnp.dot(spread, rows.astype(jnp.bfloat16), preferred_element_type=jnp.float32)
        return rows.astype(jnp.bfloat16).reshape(SEQ, PART, HD)

    def part_of(t):
        return pl.ds(pl.multiple_of(t * PART, PART), PART)

    def query_tile(t, _):
        grad = tile_rows(3, t)
        rows = local_rows(t)
        weighted = jnp.zeros((TILE, 128), jnp.float32)
        for cols in chunks:
            dots = lax.dot_general(grad, head_rows(2, cols), NT, preferred_element_type=jnp.float32)
            dots_ref[:, cols] = dots
            weighted += lane_fold(scores_ref[rows, cols] * dots, jnp.add)
        share = 1.0 / sums[rows, 0:1]
        delta = jnp.sum(weighted, axis=-1, keepdims=True) * share
        result = jnp.zeros((TILE, HD), jnp.float32)
        for cols in chunks:
            dscore = (scores_ref[rows, cols] * share) * (dots_ref[:, cols] - delta)
            result += jnp.dot(dscore.astype(jnp.bfloat16), head_rows(0, cols), preferred_element_type=jnp.float32)
        grads, term = norm_grads(raw[1, rows, :], gain_q_ref[...], result * SCALING)
        terms[0:8, :] += term
        store_stat(1, t, delta)

        q_slots[:, part_of(t), :] = spread_tile(t, grads)

        @pl.when((t & 1) == 1)
        def _():
            send_home(lambda i: q_home(t >> 1, i), 0)

        return 0


    def stat_copy(rows, there):
        return remote(stats.at[rows], stats.at[rows], stat_send.at[there], stat_recv.at[rows], member(there))

    def stat_start():
        for step in (1, 2, 3):
            stat_copy(me, me ^ step).start()

    def stat_finish():
        for step in (1, 2, 3):
            stat_copy(me ^ step, me ^ step).wait_recv()
            stat_copy(me, me ^ step).wait_send()


    half = CHUNK // 2

    def half_of(h):
        return pl.ds(pl.multiple_of(h * half, half), half)

    def home_half(h):
        return pl.ds(pl.multiple_of(seat * CHUNK + h * half, half), half)

    def q_home(h, i):
        return q_slots.at[i, half_of(h), :], home_ref.at[0, home_half(h), :]

    def kv_home(h, i):
        return kv_slots.at[:, i, half_of(h), :], home_ref.at[1:3, home_half(h), :]

    def send_home(copies, sem):
        def start(n, _):
            i = nth_source(n)
            src, dst = copies(i)

            @pl.when(jnp.logical_not(to_self(i)))
            def _():
                remote(src, dst, home_send.at[sem], home_recv.at[sem], source(i)).start()

            return 0

        lax.fori_loop(0, SEQ, start, 0)

        @pl.when(same)
        def _():
            src, dst = copies(s)
            pltpu.make_async_copy(src, dst, home_recv.at[sem]).start()


    def stat_row(i, cols):
        units = range(cols.start // SHARE, cols.stop // SHARE)
        return jnp.concatenate([stats[u // UNITS, i, u % UNITS : u % UNITS + 1, :] for u in units], axis=1)

    def key_tile(t, _):
        key, value = tile_rows(0, t), tile_rows(2, t)
        key_grad = jnp.zeros((TILE, HD), jnp.float32)
        value_grad = jnp.zeros((TILE, HD), jnp.float32)
        for cols in chunks:
            query, grad = head_rows(1, cols), head_rows(3, cols)
            scores = lax.dot_general(key, query, NT, preferred_element_type=jnp.float32)
            weights = jnp.exp2(scores * (SCALING * LOG2E) - stat_row(0, cols))
            dots = lax.dot_general(value, grad, NT, preferred_element_type=jnp.float32)
            dscore = weights * (dots - stat_row(1, cols))
            key_grad += jnp.dot(dscore.astype(jnp.bfloat16), query, preferred_element_type=jnp.float32)
            value_grad += jnp.dot(weights.astype(jnp.bfloat16), grad, preferred_element_type=jnp.float32)
        grads, term = norm_grads(raw[0, local_rows(t), :], gain_k_ref[...], key_grad * SCALING)
        terms[8:16, :] += term
        for i, result in enumerate((grads, value_grad)):
            kv_slots[i, :, part_of(t), :] = spread_tile(t, result)

        @pl.when((t & 1) == 1)
        def _():
            send_home(lambda i: kv_home(t >> 1, i), 1)

        return 0


    def part_start(i, _):
        @pl.when(jnp.logical_not(to_self(i)))
        def _():
            remote(terms, parts.at[seat], part_sem.at[0], part_sem.at[1], source(i)).start()

        return 0

    @pl.when(active)
    def _():
        build_pick()
        to_dense(0)

    route(2, 0, TARGETS, beside=0)

    @pl.when(active)
    def _():
        to_dense(1)

    route(3, 0, TARGETS // 2, beside=1)

    @pl.when(active)
    def _():
        terms[...] = jnp.zeros_like(terms)
        gather_pass(0)
        gather_finish(0)
        lax.fori_loop(0, TILES // 2, score_tile, 0)
        to_dense(2)

    route(3, TARGETS // 2, TARGETS, beside=2)

    @pl.when(active)
    def _():
        gather_pass(1)
        lax.fori_loop(TILES // 2, TILES, score_tile, 0)
        gather_pass(2)
        to_dense(3)
        gather_rest()
        gather_finish(2)
        lax.fori_loop(0, TILES, query_tile, 0)
        stat_start()
        gather_pass(3)
        gather_finish(1)
        gather_finish(3)
        stat_finish()
        lax.fori_loop(0, TILES, key_tile, 0)
        lax.fori_loop(0, SEQ, part_start, 0)

        @pl.when(same)
        def _():
            pltpu.make_async_copy(terms, parts.at[seat], part_sem.at[1]).start()

    remote(parts, parts, part_sem.at[0], part_sem.at[1], sibling).wait_recv()
    partial[...] = jnp.sum(parts[...], axis=0)

    def cross_copy(i, dst):
        return remote(partial, cross.at[dst], cross_send.at[i], cross_recv.at[dst], (i >> 2, s, i & 3))

    def cross_start(i, _):
        @pl.when(i != corner)
        def _():
            cross_copy(i, corner).start()

        return 0

    def cross_finish(i, _):
        @pl.when(i != corner)
        def _():
            cross_copy(i, i).wait_recv()
            cross_copy(i, corner).wait_send()

        return 0

    cross[pl.ds(corner, 1)] = partial[...][None]
    lax.fori_loop(0, 8, cross_start, 0)
    lax.fori_loop(0, 8, cross_finish, 0)
    total_ref[...] = jnp.sum(cross[...], axis=0)


    def sent(targets, sources):
        for a in range(4):
            rows = slots.at[a, 0 : targets * CHUNK, :]
            remote(rows, rows, route_send.at[a], route_recv.at[a], sibling).wait_send()
        if sources:
            for a in range(4):
                gather_sent(a)
            rows = q_slots.at[0:sources]
            remote(rows, rows, home_send.at[0], home_recv.at[0], sibling).wait_send()
            rows = kv_slots.at[:, 0:sources]
            remote(rows, rows, home_send.at[1], home_recv.at[1], sibling).wait_send()
            rows = part_bytes.at[0:sources]
            remote(rows, rows, part_sem.at[0], part_sem.at[1], sibling).wait_send()

    @pl.when(same)
    def _():
        sent(TARGETS - 1, SEQ - 1)

    @pl.when(active & jnp.logical_not(same))
    def _():
        sent(TARGETS, SEQ)

    @pl.when(jnp.logical_not(active))
    def _():
        sent(TARGETS, 0)

    remote(home_ref.at[0], home_ref.at[0], home_send.at[0], home_recv.at[0], sibling).wait_recv()
    remote(home_ref.at[1:3], home_ref.at[1:3], home_send.at[1], home_recv.at[1], sibling).wait_recv()


def core(listing, k, q, v, g, gain_q, gain_k):
    bf16, f32 = jnp.bfloat16, jnp.float32
    dma = pltpu.SemaphoreType.DMA
    in_vmem = pl.BlockSpec(memory_space=pltpu.VMEM)
    return pl.pallas_call(
        core_kernel,
        name="core",
        in_specs=[in_vmem] * 7,
        out_specs=[pl.BlockSpec(memory_space=pl.ANY), in_vmem, in_vmem],
        out_shape=(
            jax.ShapeDtypeStruct((3, OUT, HD), bf16),
            jax.ShapeDtypeStruct((SPAN, SPAN), bf16),
            jax.ShapeDtypeStruct((16, HD), f32),
        ),
        scratch_shapes=[
            pltpu.VMEM((4, OUT, HD), bf16),
            pltpu.VMEM((4, FLAT, HD), bf16),
            pltpu.VMEM((SEQ, SHARE), jnp.int32),
            pltpu.VMEM((SEQ, SHARE), jnp.int32),
            pltpu.VMEM((SEQ, SHARE), jnp.int32),
            pltpu.VMEM((ROWS, FLAT), bf16),
            pltpu.VMEM((4, KEPT, HD), bf16),
            pltpu.VMEM((2, ROWS, HD), bf16),
            pltpu.VMEM((ROWS, KEPT), f32),
            pltpu.VMEM((TILE, KEPT), f32),
            pltpu.VMEM((ROWS, 128), f32),
            pltpu.VMEM((SEQ, CHUNK, HD), bf16),
            pltpu.VMEM((2, SEQ, CHUNK, HD), bf16),
            pltpu.VMEM((MEMBERS, 2, 8, SHARE), f32),
            pltpu.VMEM((16, HD), f32),
            pltpu.VMEM((SEQ, 16, HD), f32),
            pltpu.VMEM((TARGETS, 16, HD), f32),
            pltpu.VMEM((16, HD), f32),
            pltpu.VMEM((8, 16, HD), f32),
            dma((2,)),
            dma((4,)),
            dma((4,)),
            dma((4, 3)),
            dma((4, 3)),
            dma((MEMBERS,)),
            dma((MEMBERS,)),
            dma((2,)),
            dma((2,)),
            dma((2,)),
            dma((8,)),
            dma((8,)),
        ],
        compiler_params=pltpu.CompilerParams(
            collective_id=0, has_side_effects=True, vmem_limit_bytes=VMEM_LIMIT
        ),
    )(listing, k, q, v, g, gain_q, gain_k)


def rows_kernel(back_ref, slots_ref, total_ref, q_ref, k_ref, v_ref, gain_q_ref, gain_k_ref):
    for i, ref in enumerate((q_ref, k_ref, v_ref)):
        for h in range(slots_ref.shape[1] // SPAN):
            rows = slots_ref[i, h * SPAN : (h + 1) * SPAN, :]
            rows = jnp.dot(back_ref[...], rows, preferred_element_type=jnp.float32)
            ref[0, :, h * HD : (h + 1) * HD] = rows.astype(jnp.bfloat16)
    gain_q_ref[...] = jnp.sum(total_ref[0:8, :], axis=0, keepdims=True)
    gain_k_ref[...] = jnp.sum(total_ref[8:16, :], axis=0, keepdims=True)


def to_rows(back, slots, total):
    width = HEAD_PART * HD
    parts = 2
    big = jax.ShapeDtypeStruct((1, SPAN, width), jnp.bfloat16)
    small = jax.ShapeDtypeStruct((1, HD), jnp.float32)
    return pl.pallas_call(
        rows_kernel,
        name="to_rows",
        grid=(parts,),
        in_specs=[
            pl.BlockSpec((SPAN, SPAN), lambda h: (0, 0)),
            pl.BlockSpec((3, OUT // parts, HD), lambda h: (0, h, 0)),
            pl.BlockSpec((16, HD), lambda h: (0, 0)),
        ],
        out_specs=[pl.BlockSpec((1, SPAN, width // parts), lambda h: (0, 0, h))] * 3
        + [pl.BlockSpec((1, HD), lambda h: (0, 0))] * 2,
        out_shape=(big, big, big, small, small),
        compiler_params=pltpu.CompilerParams(vmem_limit_bytes=VMEM_LIMIT),
        cost_estimate=pl.CostEstimate(flops=3 * 10**8, bytes_accessed=3 * 10**6, transcendentals=0),
    )(back, slots, total)


def on_device(q_raw, k_raw, v_raw, out_grad, gain_q, gain_k, keep_list):
    home, back, total = core(
        keep_list.reshape(SEQ, SHARE),
        k_raw[0],
        q_raw[0],
        v_raw[0],
        out_grad[0],
        gain_q.reshape(1, HD),
        gain_k.reshape(1, HD),
    )
    q_out, k_out, v_out, gain_q_grad, gain_k_grad = to_rows(back, home, total)
    return q_out, k_out, v_out, gain_q_grad.reshape(HD), gain_k_grad.reshape(HD)


def solution(mesh):
    big = P("dp", "seq", "tensor")
    return jax.shard_map(
        on_device,
        mesh=mesh,
        in_specs=(big, big, big, big, P(), P(), P("dp", None)),
        out_specs=(big, big, big, P(), P()),
        check_vma=False,
    )
```

```python
import math

import jax
import jax.numpy as jnp
from jax import lax
from jax.experimental import pallas as pl
from jax.experimental.pallas import tpu as pltpu
from jax.sharding import PartitionSpec as P

MESH = pl.DeviceIdType.MESH
HD = 128
EPSILON = 1e-06
SEQ = 32
SPAN = 256
SHARE = 128
SLOTS = 8
HEAD_PART = 6
UNITS = 8
ROWS = UNITS * SHARE
CHUNK = UNITS * SLOTS
MEMBERS = 4
TARGETS = HEAD_PART * MEMBERS
OUT = TARGETS * CHUNK
FLAT = SEQ * CHUNK
KEPT = SEQ * SHARE
TILE = 256
PART = TILE // SHARE * SLOTS
TILES = ROWS // TILE
PIECE = 128
SCALING = 1.0 / math.sqrt(HD)
LOG2E = 1.4426950408889634
VMEM_LIMIT = 56 * 1024 * 1024

NT = (((1,), (1,)), ((), ()))

def place(clip, i):
    head, quarter = i >> 2, i & 3
    third = (head * 11) >> 5
    pair = head - 3 * third
    odd = pair >> 1
    y = 2 * ((pair & 1) + odd * third) + (quarter >> 1)
    z = 4 * clip + 2 * third + odd
    return quarter & 1, y * 8 + z


def my_place(dp, s):
    y, z = s >> 3, s & 7
    third, odd, high = (z >> 1) & 1, z & 1, y >> 1
    pair = high + odd * (2 - high)
    active = (odd == 0) | (high == third)
    return z >> 2, (3 * third + pair) * 4 + 2 * (y & 1) + dp, active


def one_hot(hit):
    return jnp.where(hit, 1.0, 0.0).astype(jnp.bfloat16)


def inverse_norm(x):
    return lax.rsqrt(jnp.mean(x * x, axis=-1, keepdims=True) + EPSILON)


def norm_grads(raw, gain, upstream):
    raw = raw.astype(jnp.float32)
    inverse = inverse_norm(raw)
    scaled = upstream * gain
    inner = jnp.mean(scaled * raw, axis=-1, keepdims=True)
    grads = inverse * scaled - raw * (inverse * inverse * inverse * inner)
    terms = upstream * raw * inverse
    return grads, jnp.sum(terms.reshape(-1, 8, HD), axis=0)


def lane_fold(x, fold):
    parts = [x[:, i * 128 : (i + 1) * 128] for i in range(x.shape[1] // 128)]
    total = parts[0]
    for part in parts[1:]:
        total = fold(total, part)
    return total


def core_kernel(
    list_ref,
    k_ref,
    q_ref,
    v_ref,
    g_ref,
    gain_q_ref,
    gain_k_ref,
    home_ref,
    back_ref,
    total_ref,
    slots,
    arrived,
    enc_ref,
    other,
    codes,
    pick,
    full,
    raw,
    scores_ref,
    dots_ref,
    sums,
    q_slots,
    kv_slots,
    stats,
    terms,
    part_bytes,
    parts,
    partial,
    cross,
    enc_sem,
    route_send,
    route_recv,
    near_send,
    near_recv,
    stat_send,
    stat_recv,
    home_send,
    home_recv,
    part_sem,
    cross_send,
    cross_recv,
):
    dp, s, x = lax.axis_index("dp"), lax.axis_index("seq"), lax.axis_index("tensor")
    clip, seat, active = my_place(dp, s)
    me = seat & 3
    sibling = (1 - dp, s, x)
    corner = dp * 4 + x
    same = active & (clip == dp)
    own_source = jnp.where(same, s, -1)
    own_target = jnp.where(same, seat, -1)

    def to_self(i):
        return i == own_source

    def target(i):
        return place(dp, i) + (x,), i == own_target

    def source(i):
        return (clip, i, x)

    def member(i):
        return (i & 1, (s & 23) + 8 * (i >> 1), x)

    def remote(src, dst, send_sem, recv_sem, device):
        return pltpu.make_async_remote_copy(
            src_ref=src, dst_ref=dst, send_sem=send_sem, recv_sem=recv_sem, device_id=device, device_id_type=MESH
        )


    barrier = pltpu.get_barrier_semaphore()

    def greet_device(there):
        pl.semaphore_signal(barrier, inc=1, device_id=there, device_id_type=MESH)

    def greet_target(i, _):
        there, own = target(i)

        @pl.when(jnp.logical_not(own))
        def _():
            greet_device(there)

        return 0

    def greet_source(i, _):
        @pl.when(jnp.logical_not(to_self(i)))
        def _():
            greet_device(source(i))

        return 0

    def greet_corner(i, _):
        @pl.when(i != corner)
        def _():
            greet_device((i >> 2, s, i & 3))

        return 0

    @pl.when(active)
    def _():
        lax.fori_loop(0, SEQ, greet_source, 0)
        for step in (1, 2, 3):
            greet_device(member(me ^ step))

    lax.fori_loop(0, TARGETS, greet_target, 0)
    lax.fori_loop(0, 8, greet_corner, 0)


    listing = list_ref[...]
    from_block = listing >> 8
    hits = one_hot(jnp.concatenate([from_block == i for i in range(SEQ)], axis=0))
    earlier = lax.broadcasted_iota(jnp.int32, (SHARE, SHARE), 0) < lax.broadcasted_iota(jnp.int32, (SHARE, SHARE), 1)
    counts = jnp.dot(hits, one_hot(earlier), preferred_element_type=jnp.float32) * hits.astype(jnp.float32)
    rank = counts[0:SEQ]
    for i in range(1, SEQ):
        rank += counts[i * SEQ : (i + 1) * SEQ]
    rank = rank.astype(jnp.int32)
    enc_ref[...] = from_block * SLOTS + rank
    slot = lax.broadcasted_iota(jnp.int32, (SEQ, SHARE), 0) * SLOTS + rank + 1
    slot = jnp.where(from_block == s, slot, 0).astype(jnp.float32)
    token = listing - s * SPAN
    token_iota = lax.broadcasted_iota(jnp.int32, (SPAN, SHARE), 0)
    found = jnp.zeros((SPAN, SHARE), jnp.float32)
    for j in range(SEQ):
        found += jnp.where(token_iota == token[j : j + 1], slot[j : j + 1], 0.0)
    found = jnp.sum(found, axis=1, keepdims=True) - 1.0
    row = jnp.broadcast_to(found, (SPAN, 128)).T[0:1]
    back_ref[...] = one_hot(lax.broadcasted_iota(jnp.int32, (SPAN, SPAN), 1).astype(jnp.float32) == found)
    take = one_hot(lax.broadcasted_iota(jnp.int32, (SPAN, SPAN), 0).astype(jnp.float32) == row)
    step = 512

    def to_slots(i, ref):
        rows = jnp.dot(take, ref[...], preferred_element_type=jnp.float32).astype(jnp.bfloat16)
        for h in range(HEAD_PART):
            slots[i, h * SPAN : (h + 1) * SPAN, :] = rows[:, h * HD : (h + 1) * HD]

    def chunk(ref, a, i):
        return ref.at[a, pl.ds(pl.multiple_of(i * CHUNK, 16), CHUNK), :]

    def nth_target(n):
        v = 3 * (s & 7) + 6 * (s >> 3) + 7 * n
        return v - 24 * ((v * 171) >> 12)

    def nth_source(n):
        turn = n & 7
        away = ((turn + 1) >> 1) * (2 * (turn & 1) - 1)
        return (((s >> 3) + (n >> 3)) & 3) * 8 + (((s & 7) + away) & 7)


    def route(a, first, last, beside=None):
        def start(n, _):
            if beside is not None:

                @pl.when(n < first + ROWS // PIECE)
                def _():
                    @pl.when(active)
                    def _():
                        piece(beside, n - first).start()

            i = nth_target(n)
            there, own = target(i)

            @pl.when(jnp.logical_not(own))
            def _():
                remote(chunk(slots, a, i), chunk(arrived, a, s), route_send.at[a], route_recv.at[a], there).start()

            return 0

        lax.fori_loop(first, last, start, 0)

        if last == TARGETS:

            @pl.when(same)
            def _():
                pltpu.make_async_copy(chunk(slots, a, seat), chunk(arrived, a, s), route_recv.at[a]).start()

    def rows_of(a, i):
        return full.at[a, pl.ds(pl.multiple_of(i * ROWS, ROWS), ROWS), :]

    def piece(a, n):
        rows = full.at[a, pl.ds(pl.multiple_of(me * ROWS + n * PIECE, PIECE), PIECE), :]
        return remote(rows, rows, near_send.at[a, 0], near_recv.at[a, 0], member(me ^ 2))

    to_slots(0, k_ref)
    arrivals = jnp.where(active, SEQ + 3, 0) - jnp.where(same, 2, 0)
    pl.semaphore_wait(barrier, TARGETS + 7 + arrivals)
    exchange = remote(enc_ref, other, enc_sem.at[0], enc_sem.at[1], sibling)

    @pl.when(active)
    def _():
        exchange.start()

    route(0, 0, TARGETS)
    to_slots(1, q_ref)
    route(1, 0, TARGETS)
    to_slots(2, v_ref)
    to_slots(3, g_ref)


    def unit_codes(u):
        return codes[pl.ds(UNITS * me + u, 1), :]

    def build_pick():
        exchange.wait()
        codes[...] = jnp.where(clip == dp, enc_ref[...], other[...])
        wide_iota = lax.broadcasted_iota(jnp.int32, (SHARE, 128), 1).astype(jnp.float32)
        for u in range(UNITS):
            code = unit_codes(u)
            code = (code >> 3) * CHUNK + u * SLOTS + (code & 7)
            wide = jnp.broadcast_to(code.astype(jnp.float32), (SHARE, 128)).T
            for c in range(FLAT // 128):
                pick[u * SHARE : (u + 1) * SHARE, c * 128 : (c + 1) * 128] = one_hot(wide == wide_iota + c * 128.0)


    def near(a, way, rows, there):
        return remote(rows_of(a, rows), rows_of(a, rows), near_send.at[a, way], near_recv.at[a, way], member(there))

    def gather_rest():
        def start(n, _):
            piece(3, n).start()
            return 0

        lax.fori_loop(0, ROWS // PIECE, start, 0)

    def gather_pass(a):
        near(a, 0, me ^ 2, me).wait_recv()
        near(a, 2, me ^ 2, me ^ 1).start()

    def gather_finish(a):
        near(a, 1, me ^ 1, me).wait_recv()
        near(a, 2, me ^ 3, me).wait_recv()

    def gather_sent(a):
        near(a, 0, me, me ^ 2).wait_send()
        near(a, 1, me, me ^ 1).wait_send()
        near(a, 2, me ^ 2, me ^ 1).wait_send()

    own_rows = pl.ds(pl.multiple_of(me * ROWS, 256), ROWS)

    def to_dense(a):
        remote(arrived.at[a], arrived.at[a], route_send.at[a], route_recv.at[a], sibling).wait_recv()
        rows = jnp.dot(pick[...], arrived[a], preferred_element_type=jnp.float32)
        if a < 2:
            raw[a] = rows.astype(jnp.bfloat16)
            gain = (gain_k_ref, gain_q_ref)[a][...]
            rows = rows * inverse_norm(rows) * gain
        full[a, own_rows, :] = rows.astype(jnp.bfloat16)
        near(a, 1, me, me ^ 1).start()


    chunks = [slice(i * step, (i + 1) * step) for i in range(KEPT // step)]

    def head_rows(a, cols):
        return full[a, cols, :]

    def tile_rows(a, t):
        return full[a, pl.ds(pl.multiple_of(me * ROWS + t * TILE, TILE), TILE), :]

    def local_rows(t):
        return pl.ds(pl.multiple_of(t * TILE, TILE), TILE)

    def store_stat(i, t, value):
        wide = jnp.broadcast_to(value, (TILE, 128)).T
        for j in range(TILE // SHARE):
            stats[me, i, pl.ds(TILE // SHARE * t + j, 1), :] = wide[0:1, j * SHARE : (j + 1) * SHARE]

    def score_tile(t, _):
        query = tile_rows(1, t)
        rows = local_rows(t)
        top = None
        for cols in chunks:
            scores = lax.dot_general(query, head_rows(0, cols), NT, preferred_element_type=jnp.float32)
            scores = scores * (SCALING * LOG2E)
            scores_ref[rows, cols] = scores
            part = lane_fold(scores, jnp.maximum)
            top = part if top is None else jnp.maximum(top, part)
        top = jnp.max(top, axis=-1, keepdims=True)
        total = jnp.zeros((TILE, 128), jnp.float32)
        for cols in chunks:
            weights = jnp.exp2(scores_ref[rows, cols] - top)
            scores_ref[rows, cols] = weights
            total += lane_fold(weights, jnp.add)
        total = jnp.sum(total, axis=-1, keepdims=True)
        sums[rows, :] = jnp.broadcast_to(total, (TILE, 128))
        store_stat(0, t, top + jnp.log2(total))

        return 0

    def spread_tile(t, rows):
        tile_iota = lax.broadcasted_iota(jnp.int32, (SEQ * PART, TILE), 0)
        tile_codes = []
        for j in range(TILE // SHARE):
            code = unit_codes(TILE // SHARE * t + j)
            tile_codes.append((code >> 3) * PART + j * SLOTS + (code & 7))
        spread = one_hot(tile_iota == jnp.concatenate(tile_codes, axis=1))
        rows = jnp.dot(spread, rows.astype(jnp.bfloat16), preferred_element_type=jnp.float32)
        return rows.astype(jnp.bfloat16).reshape(SEQ, PART, HD)

    def part_of(t):
        return pl.ds(pl.multiple_of(t * PART, PART), PART)

    def query_tile(t, _):
        grad = tile_rows(3, t)
        rows = local_rows(t)
        weighted = jnp.zeros((TILE, 128), jnp.float32)
        for cols in chunks:
            dots = lax.dot_general(grad, head_rows(2, cols), NT, preferred_element_type=jnp.float32)
            dots_ref[:, cols] = dots
            weighted += lane_fold(scores_ref[rows, cols] * dots, jnp.add)
        share = 1.0 / sums[rows, 0:1]
        delta = jnp.sum(weighted, axis=-1, keepdims=True) * share
        result = jnp.zeros((TILE, HD), jnp.float32)
        for cols in chunks:
            dscore = (scores_ref[rows, cols] * share) * (dots_ref[:, cols] - delta)
            result += jnp.dot(dscore.astype(jnp.bfloat16), head_rows(0, cols), preferred_element_type=jnp.float32)
        grads, term = norm_grads(raw[1, rows, :], gain_q_ref[...], result * SCALING)
        terms[0:8, :] += term
        store_stat(1, t, delta)

        q_slots[:, part_of(t), :] = spread_tile(t, grads)

        @pl.when((t & 1) == 1)
        def _():
            send_home(lambda i: q_home(t >> 1, i), 0)

        return 0


    def stat_copy(rows, there):
        return remote(stats.at[rows], stats.at[rows], stat_send.at[there], stat_recv.at[rows], member(there))

    def stat_start():
        for step in (1, 2, 3):
            stat_copy(me, me ^ step).start()

    def stat_finish():
        for step in (1, 2, 3):
            stat_copy(me ^ step, me ^ step).wait_recv()
            stat_copy(me, me ^ step).wait_send()


    half = CHUNK // 2

    def half_of(h):
        return pl.ds(pl.multiple_of(h * half, half), half)

    def home_half(h):
        return pl.ds(pl.multiple_of(seat * CHUNK + h * half, half), half)

    def q_home(h, i):
        return q_slots.at[i, half_of(h), :], home_ref.at[0, home_half(h), :]

    def kv_home(first, count, i):
        rows = pl.ds(pl.multiple_of(first, PART), count)
        home_rows = pl.ds(pl.multiple_of(seat * CHUNK + first, PART), count)
        return kv_slots.at[:, i, rows, :], home_ref.at[1:3, home_rows, :]

    def send_home(copies, sem):
        def start(n, _):
            i = nth_source(n)
            src, dst = copies(i)

            @pl.when(jnp.logical_not(to_self(i)))
            def _():
                remote(src, dst, home_send.at[sem], home_recv.at[sem], source(i)).start()

            return 0

        lax.fori_loop(0, SEQ, start, 0)

        @pl.when(same)
        def _():
            src, dst = copies(s)
            pltpu.make_async_copy(src, dst, home_recv.at[sem]).start()


    def stat_row(i, cols):
        units = range(cols.start // SHARE, cols.stop // SHARE)
        return jnp.concatenate([stats[u // UNITS, i, u % UNITS : u % UNITS + 1, :] for u in units], axis=1)

    def key_tile(t, _):
        key, value = tile_rows(0, t), tile_rows(2, t)
        key_grad = jnp.zeros((TILE, HD), jnp.float32)
        value_grad = jnp.zeros((TILE, HD), jnp.float32)
        for cols in chunks:
            query, grad = head_rows(1, cols), head_rows(3, cols)
            scores = lax.dot_general(key, query, NT, preferred_element_type=jnp.float32)
            weights = jnp.exp2(scores * (SCALING * LOG2E) - stat_row(0, cols))
            dots = lax.dot_general(value, grad, NT, preferred_element_type=jnp.float32)
            dscore = weights * (dots - stat_row(1, cols))
            key_grad += jnp.dot(dscore.astype(jnp.bfloat16), query, preferred_element_type=jnp.float32)
            value_grad += jnp.dot(weights.astype(jnp.bfloat16), grad, preferred_element_type=jnp.float32)
        grads, term = norm_grads(raw[0, local_rows(t), :], gain_k_ref[...], key_grad * SCALING)
        terms[8:16, :] += term
        for i, result in enumerate((grads, value_grad)):
            kv_slots[i, :, part_of(t), :] = spread_tile(t, result)

        @pl.when(t == 1)
        def _():
            send_home(lambda i: kv_home(0, 2 * PART, i), 1)

        @pl.when(t > 1)
        def _():
            send_home(lambda i: kv_home(t * PART, PART, i), 1)

        return 0


    def part_start(i, _):
        @pl.when(jnp.logical_not(to_self(i)))
        def _():
            remote(terms, parts.at[seat], part_sem.at[0], part_sem.at[1], source(i)).start()

        return 0

    @pl.when(active)
    def _():
        build_pick()
        to_dense(0)

    route(2, 0, TARGETS, beside=0)

    @pl.when(active)
    def _():
        to_dense(1)

    route(3, 0, TARGETS // 2, beside=1)

    @pl.when(active)
    def _():
        terms[...] = jnp.zeros_like(terms)
        gather_pass(0)
        gather_finish(0)
        lax.fori_loop(0, TILES // 2, score_tile, 0)
        to_dense(2)

    route(3, TARGETS // 2, TARGETS, beside=2)

    @pl.when(active)
    def _():
        gather_pass(1)
        lax.fori_loop(TILES // 2, TILES, score_tile, 0)
        gather_pass(2)
        to_dense(3)
        gather_rest()
        gather_finish(2)
        lax.fori_loop(0, TILES, query_tile, 0)
        stat_start()
        gather_pass(3)
        gather_finish(1)
        gather_finish(3)
        stat_finish()
        lax.fori_loop(0, TILES, key_tile, 0)
        lax.fori_loop(0, SEQ, part_start, 0)

        @pl.when(same)
        def _():
            pltpu.make_async_copy(terms, parts.at[seat], part_sem.at[1]).start()

    remote(parts, parts, part_sem.at[0], part_sem.at[1], sibling).wait_recv()
    partial[...] = jnp.sum(parts[...], axis=0)

    def cross_copy(i, dst):
        return remote(partial, cross.at[dst], cross_send.at[i], cross_recv.at[dst], (i >> 2, s, i & 3))

    def cross_start(i, _):
        @pl.when(i != corner)
        def _():
            cross_copy(i, corner).start()

        return 0

    def cross_finish(i, _):
        @pl.when(i != corner)
        def _():
            cross_copy(i, i).wait_recv()
            cross_copy(i, corner).wait_send()

        return 0

    cross[pl.ds(corner, 1)] = partial[...][None]
    lax.fori_loop(0, 8, cross_start, 0)
    lax.fori_loop(0, 8, cross_finish, 0)
    total_ref[...] = jnp.sum(cross[...], axis=0)


    def sent(targets, sources):
        for a in range(4):
            rows = slots.at[a, 0 : targets * CHUNK, :]
            remote(rows, rows, route_send.at[a], route_recv.at[a], sibling).wait_send()
        if sources:
            for a in range(4):
                gather_sent(a)
            rows = q_slots.at[0:sources]
            remote(rows, rows, home_send.at[0], home_recv.at[0], sibling).wait_send()
            rows = kv_slots.at[:, 0:sources]
            remote(rows, rows, home_send.at[1], home_recv.at[1], sibling).wait_send()
            rows = part_bytes.at[0:sources]
            remote(rows, rows, part_sem.at[0], part_sem.at[1], sibling).wait_send()

    @pl.when(same)
    def _():
        sent(TARGETS - 1, SEQ - 1)

    @pl.when(active & jnp.logical_not(same))
    def _():
        sent(TARGETS, SEQ)

    @pl.when(jnp.logical_not(active))
    def _():
        sent(TARGETS, 0)

    remote(home_ref.at[0], home_ref.at[0], home_send.at[0], home_recv.at[0], sibling).wait_recv()
    remote(home_ref.at[1:3], home_ref.at[1:3], home_send.at[1], home_recv.at[1], sibling).wait_recv()


def core(listing, k, q, v, g, gain_q, gain_k):
    bf16, f32 = jnp.bfloat16, jnp.float32
    dma = pltpu.SemaphoreType.DMA
    in_vmem = pl.BlockSpec(memory_space=pltpu.VMEM)
    return pl.pallas_call(
        core_kernel,
        name="core",
        in_specs=[in_vmem] * 7,
        out_specs=[pl.BlockSpec(memory_space=pl.ANY), in_vmem, in_vmem],
        out_shape=(
            jax.ShapeDtypeStruct((3, OUT, HD), bf16),
            jax.ShapeDtypeStruct((SPAN, SPAN), bf16),
            jax.ShapeDtypeStruct((16, HD), f32),
        ),
        scratch_shapes=[
            pltpu.VMEM((4, OUT, HD), bf16),
            pltpu.VMEM((4, FLAT, HD), bf16),
            pltpu.VMEM((SEQ, SHARE), jnp.int32),
            pltpu.VMEM((SEQ, SHARE), jnp.int32),
            pltpu.VMEM((SEQ, SHARE), jnp.int32),
            pltpu.VMEM((ROWS, FLAT), bf16),
            pltpu.VMEM((4, KEPT, HD), bf16),
            pltpu.VMEM((2, ROWS, HD), bf16),
            pltpu.VMEM((ROWS, KEPT), f32),
            pltpu.VMEM((TILE, KEPT), f32),
            pltpu.VMEM((ROWS, 128), f32),
            pltpu.VMEM((SEQ, CHUNK, HD), bf16),
            pltpu.VMEM((2, SEQ, CHUNK, HD), bf16),
            pltpu.VMEM((MEMBERS, 2, 8, SHARE), f32),
            pltpu.VMEM((16, HD), f32),
            pltpu.VMEM((SEQ, 16, HD), f32),
            pltpu.VMEM((TARGETS, 16, HD), f32),
            pltpu.VMEM((16, HD), f32),
            pltpu.VMEM((8, 16, HD), f32),
            dma((2,)),
            dma((4,)),
            dma((4,)),
            dma((4, 3)),
            dma((4, 3)),
            dma((MEMBERS,)),
            dma((MEMBERS,)),
            dma((2,)),
            dma((2,)),
            dma((2,)),
            dma((8,)),
            dma((8,)),
        ],
        compiler_params=pltpu.CompilerParams(
            collective_id=0, has_side_effects=True, vmem_limit_bytes=VMEM_LIMIT
        ),
    )(listing, k, q, v, g, gain_q, gain_k)


def rows_kernel(back_ref, slots_ref, total_ref, q_ref, k_ref, v_ref, gain_q_ref, gain_k_ref):
    for i, ref in enumerate((q_ref, k_ref, v_ref)):
        for h in range(slots_ref.shape[1] // SPAN):
            rows = slots_ref[i, h * SPAN : (h + 1) * SPAN, :]
            rows = jnp.dot(back_ref[...], rows, preferred_element_type=jnp.float32)
            ref[0, :, h * HD : (h + 1) * HD] = rows.astype(jnp.bfloat16)
    gain_q_ref[...] = jnp.sum(total_ref[0:8, :], axis=0, keepdims=True)
    gain_k_ref[...] = jnp.sum(total_ref[8:16, :], axis=0, keepdims=True)


def to_rows(back, slots, total):
    width = HEAD_PART * HD
    parts = 2
    big = jax.ShapeDtypeStruct((1, SPAN, width), jnp.bfloat16)
    small = jax.ShapeDtypeStruct((1, HD), jnp.float32)
    return pl.pallas_call(
        rows_kernel,
        name="to_rows",
        grid=(parts,),
        in_specs=[
            pl.BlockSpec((SPAN, SPAN), lambda h: (0, 0)),
            pl.BlockSpec((3, OUT // parts, HD), lambda h: (0, h, 0)),
            pl.BlockSpec((16, HD), lambda h: (0, 0)),
        ],
        out_specs=[pl.BlockSpec((1, SPAN, width // parts), lambda h: (0, 0, h))] * 3
        + [pl.BlockSpec((1, HD), lambda h: (0, 0))] * 2,
        out_shape=(big, big, big, small, small),
        compiler_params=pltpu.CompilerParams(vmem_limit_bytes=VMEM_LIMIT),
        cost_estimate=pl.CostEstimate(flops=3 * 10**8, bytes_accessed=3 * 10**6, transcendentals=0),
    )(back, slots, total)


def on_device(q_raw, k_raw, v_raw, out_grad, gain_q, gain_k, keep_list):
    home, back, total = core(
        keep_list.reshape(SEQ, SHARE),
        k_raw[0],
        q_raw[0],
        v_raw[0],
        out_grad[0],
        gain_q.reshape(1, HD),
        gain_k.reshape(1, HD),
    )
    q_out, k_out, v_out, gain_q_grad, gain_k_grad = to_rows(back, home, total)
    return q_out, k_out, v_out, gain_q_grad.reshape(HD), gain_k_grad.reshape(HD)


def solution(mesh):
    big = P("dp", "seq", "tensor")
    return jax.shard_map(
        on_device,
        mesh=mesh,
        in_specs=(big, big, big, big, P(), P(), P("dp", None)),
        out_specs=(big, big, big, P(), P()),
        check_vma=False,
    )
```
